128 devices in a mesh: sec: 4 (over y_lo, core), dom: 32 (over y_hi, z, x).
Axes of the slice: x: 4, y: 4 (y_hi: 2, y_lo: 2; y = y_hi * 2 + y_lo), z: 4, core: 2. Of those that a mesh axis runs over, the one named last changes fastest.
Arguments:
- les_state: float32 [4, 3, 512, 8192], P('sec', None, 'dom'), may hold values from -3 to 3
- les_density: float32 [4, 512, 8192], P('sec', 'dom'), may hold values from 0.5 to 2
- far_state: float32 [4, 3, 512, 8192], P('sec', None, 'dom'), may hold values from -3 to 3
- far_density: float32 [4, 512, 8192], P('sec', 'dom'), may hold values from 0.5 to 2
- face_cell: int32 [1048576], P(('sec', 'dom')), may hold values from 0 to 131071
- face_area: float32 [1048576], P(('sec', 'dom')), may hold values from 0.25 to 4
- face_owner: int32 [1048576], P(('sec', 'dom')), may hold values from 0 to 127, as said below
- face_counts: int32 [128], P(('sec', 'dom')), may hold values from 4096 to 8192, as said below
- face_target: int32 [1048576], P(('sec', 'dom')), may hold values from 0 to 131071
Outputs:
- les_final: float32 [4, 3, 512, 8192], P('sec', None, 'dom')
- far_final: float32 [4, 3, 512, 8192], P('sec', None, 'dom')
The draws below stay inside these ranges and needn't reach their ends.
Inputs may be any that keep to these rules, and one draw needn't show every extreme that they name: `face_owner`: among one device's 8192 face slots every owner that is named is named by exactly 128 slots, and one owner is named by 128 slots of every device. `face_counts`: some device has all 8192 slots live.
All inputs are finite; a program needn't handle non-finite values.
Results may differ from the reference program's by a relative error of at most 0.0003.
Values sent between devices are 32-bit elements; how exact they have to be, the bound alone decides.
A program may use at most 192 MiB of HBM per device.

```python
import math
import jax
import jax.numpy as jnp

LX = 16
LY = 8192
FX = 16
F_DEV = 8192
SUBSTEPS = 5
SECTIONS = 4
DEVS = 128
CAP = 128
GX = 512
GF = 512
FACES = 1048576
N_DOM = 32


def draw_face_owner(key, part):
    key = jax.random.fold_in(key, 11)
    hottest = jax.random.randint(jax.random.fold_in(key, 0), (), 0, DEVS)
    groups = jnp.arange(F_DEV) // CAP

    def one_source(source):
        source_key = jax.random.fold_in(key, source + 1)
        offsets = jax.random.permutation(jax.random.fold_in(source_key, 0), DEVS - 1)
        picked = offsets[jnp.maximum(groups - 1, 0)]
        owners = jnp.where(groups == 0, hottest, (hottest + 1 + picked) % DEVS)
        shuffle = jax.random.permutation(jax.random.fold_in(source_key, 1), F_DEV)
        return owners[shuffle]
    return jax.vmap(one_source)(jnp.arange(DEVS)).reshape(-1).astype(jnp.int32)


def draw_face_counts(key, part):
    key = jax.random.fold_in(key, 12)
    counted = jax.random.randint(jax.random.fold_in(key, 0), (DEVS,), F_DEV // 2, F_DEV + 1)
    fullest = jax.random.randint(jax.random.fold_in(key, 1), (), 0, DEVS)
    return jnp.where(jnp.arange(DEVS) == fullest, F_DEV, counted).astype(jnp.int32)


def with_ends(array, stream_key, smallest, high):
    longest = array.shape.index(max(array.shape))
    spots = []
    for shift in (0, 1):
        where = [jax.random.randint(jax.random.fold_in(stream_key, axis), (), 0, length) for axis, length in enumerate(array.shape)]
        where[longest] = (where[longest] + shift) % array.shape[longest]
        spots.append(tuple(where))
    return array.at[spots[0]].set(smallest).at[spots[1]].set(high)


def steps_of(rng, shape, pieces, smallest, top_value):
    loudness = 1.0
    for position, shards_of in pieces:
        heights = jax.random.uniform(jax.random.fold_in(jax.random.fold_in(rng, 6), position), (shards_of,), jnp.float32, smallest / len(pieces), top_value / len(pieces))
        loudness = loudness * jnp.repeat(jnp.exp(heights), shape[position] // shards_of).reshape((-1,) + (1,) * (len(shape) - 1 - position))
    return loudness


def scatter_about(key, shape, scale, bound, cuts=(), held_as=jnp.bfloat16):
    values = scale * jax.random.normal(key, shape, jnp.float32)
    if cuts:
        values = values * steps_of(key, shape, cuts, -0.22, 0.18)
    return jnp.clip(values, -bound, bound).astype(held_as)


def setup_inputs(seed: int = 0) -> dict:
    keys = jax.random.split(jax.random.key(seed), 10)
    return {
        "les_state": scatter_about(keys[0], (SECTIONS, 3, GX, LY), 0.5, 3.0, ((0, 4), (2, 32)), jnp.float32),
        "les_density": jnp.clip(jnp.exp(math.log(2.0) - 1.3862944 * jax.random.uniform(keys[1], (SECTIONS, GX, LY), jnp.float32) ** steps_of(keys[1], (SECTIONS, GX, LY), ((0, 4), (1, 32)), -0.2, 0.2)), 0.5, 2.0),
        "far_state": scatter_about(keys[2], (SECTIONS, 3, GF, LY), 0.5, 3.0, ((0, 4), (2, 32)), jnp.float32),
        "far_density": jnp.clip(jnp.exp(math.log(2.0) - 1.3862944 * jax.random.uniform(keys[3], (SECTIONS, GF, LY), jnp.float32) ** steps_of(keys[3], (SECTIONS, GF, LY), ((0, 4), (1, 32)), -0.2, 0.2)), 0.5, 2.0),
        "face_cell": with_ends(jax.random.randint(keys[4], (FACES,), 0, LX * LY), jax.random.fold_in(keys[4], 1), 0, (LX * LY) - 1).astype(jnp.int32),
        "face_area": jnp.clip(jnp.exp(math.log(4.0) - 2.7725887 * jax.random.uniform(keys[5], (FACES,), jnp.float32) ** steps_of(keys[5], (FACES,), ((0, 128),), -0.2, 0.2)), 0.25, 4.0),
        "face_owner": draw_face_owner(jax.random.fold_in(keys[9], 71), 0),
        "face_counts": draw_face_counts(jax.random.fold_in(keys[9], 71), 0),
        "face_target": with_ends(jax.random.randint(keys[8], (FACES,), 0, FX * LY), jax.random.fold_in(keys[8], 1), 0, (FX * LY) - 1).astype(jnp.int32),
    }


TIME_STEP = 0.1
LES_STIFF = 1.0
FAR_STIFF = 1.0
FILTER_WEIGHT = 0.5
MEAN_FLOW = 0.3


def pad_rows(field, margin):
    return jnp.pad(field, [(0, 0)] * (field.ndim - 2) + [(margin, margin), (0, 0)])


def along_x(padded):
    return (8.0 * (padded[..., 3:-1, :] - padded[..., 1:-3, :]) - (padded[..., 4:, :] - padded[..., :-4, :])) / 12.0


def along_y(field):
    return (8.0 * (jnp.roll(field, -1, -1) - jnp.roll(field, 1, -1)) - (jnp.roll(field, -2, -1) - jnp.roll(field, 2, -1))) / 12.0


def les_update(padded, inv_density):
    centre = padded[..., 2:-2, :]
    dx_all = along_x(padded)
    dy_all = along_y(centre)
    speed_u = centre[..., 0, :, :]
    speed_v = centre[..., 1, :, :]
    rate_u = speed_u * dx_all[..., 0, :, :] + speed_v * dy_all[..., 0, :, :] + dx_all[..., 2, :, :] * inv_density
    rate_v = speed_u * dx_all[..., 1, :, :] + speed_v * dy_all[..., 1, :, :] + dy_all[..., 2, :, :] * inv_density
    rate_p = speed_u * dx_all[..., 2, :, :] + speed_v * dy_all[..., 2, :, :] + LES_STIFF * (dx_all[..., 0, :, :] + dy_all[..., 1, :, :])
    return centre - TIME_STEP * jnp.stack([rate_u, rate_v, rate_p], axis=-3)


def smooth(padded):
    centre = padded[..., 1:-1, :]
    lateral = padded[..., :-2, :] + padded[..., 2:, :] - 2.0 * centre
    across = jnp.roll(centre, 1, -1) + jnp.roll(centre, -1, -1) - 2.0 * centre
    return centre + (FILTER_WEIGHT / 4.0) * (lateral + across)


def far_update(padded, inv_density):
    centre = padded[..., 2:-2, :]
    dx_all = along_x(padded)
    dy_all = along_y(centre)
    rate_u = MEAN_FLOW * dx_all[..., 0, :, :] + dx_all[..., 2, :, :] * inv_density
    rate_v = MEAN_FLOW * dx_all[..., 1, :, :] + dy_all[..., 2, :, :] * inv_density
    rate_p = MEAN_FLOW * dx_all[..., 2, :, :] + FAR_STIFF * (dx_all[..., 0, :, :] + dy_all[..., 1, :, :])
    return centre - TIME_STEP * jnp.stack([rate_u, rate_v, rate_p], axis=-3)


def reference(les_state, les_density, far_state, far_density, face_cell, face_area, face_owner, face_counts, face_target):
    inv_les = 1.0 / les_density
    inv_far = 1.0 / far_density
    face_index = jnp.arange(FACES, dtype=jnp.int32)
    source = face_index // F_DEV
    les_sec = source // N_DOM
    les_row = (source % N_DOM) * LX + face_cell // LY
    les_col = face_cell % LY
    current = les_state
    summed = jnp.zeros((FACES, 3), jnp.float32)
    for substep in range(SUBSTEPS):
        advanced = les_update(pad_rows(current, 2), inv_les)
        current = smooth(pad_rows(advanced, 1))
        summed = summed + current[les_sec, :, les_row, les_col]
    surface = summed / SUBSTEPS * face_area[:, None]
    is_live = (face_index % F_DEV) < face_counts[source]
    stepped = far_update(pad_rows(far_state, 2), inv_far)
    owner_sec = face_owner // N_DOM
    owner_row = (face_owner % N_DOM) * FX + face_target // LY
    owner_col = face_target % LY
    far_final = stepped.at[owner_sec, :, owner_row, owner_col].add(jnp.where(is_live[:, None], surface, 0.0))
    return current, far_final
```

```python
import jax
import jax.numpy as jnp
from jax import lax
from jax.experimental import pallas as pl
from jax.experimental.pallas import tpu as pltpu
from jax.sharding import PartitionSpec as P

SUBSTEPS = 5
TIME_STEP = 0.1
LES_STIFF = 1.0
FAR_STIFF = 1.0
FILTER_WEIGHT = 0.5
MEAN_FLOW = 0.3

LANES = 128
TILE = 8
ROWS = 16
COLS = 8192
TILES = COLS // LANES
REGS = TILES // TILE
FACES = 8192
FACE_ROWS = FACES // LANES
DEVICES = 128
RANKS = 128
CELL_ROWS = ROWS * COLS // LANES

MESH = pl.DeviceIdType.MESH
VMEM = pl.BlockSpec(memory_space=pltpu.VMEM)
SMEM = pl.BlockSpec(memory_space=pltpu.SMEM)
F32 = jnp.float32
BF16 = jnp.bfloat16
I32 = jnp.int32


def params(**more):
    return pltpu.CompilerParams(vmem_limit_bytes=56 * 1024 * 1024, **more)


def rows_from_tiles(load, flat, store, rows8):
    for block in range(TILES):
        flat[block * TILE : (block + 1) * TILE, :] = load(block)
    for row in range(TILE):
        for reg in range(REGS):
            store(rows8 * TILE + row, reg, flat[pl.ds(TILE * reg + row, TILE, stride=TILES), :])


def tiles_from_rows(load, flat, store, rows8):
    for row in range(TILE):
        for reg in range(REGS):
            flat[pl.ds(TILE * reg + row, TILE, stride=TILES), :] = load(rows8 * TILE + row, reg)
    for block in range(TILES):
        store(block, flat[block * TILE : (block + 1) * TILE, :])


def shifted(row, by, lane):
    if by > 0:
        turned = pltpu.roll(row, LANES - by, 1)
        crossed = jnp.concatenate([turned[TILE:], pltpu.roll(turned[:TILE], TILE - 1, 0)], axis=0)
        return jnp.where(lane >= LANES - by, crossed, turned)
    turned = pltpu.roll(row, -by, 1)
    crossed = jnp.concatenate(
        [pltpu.roll(turned[TILES - TILE :], 1, 0), turned[: TILES - TILE]], axis=0
    )
    return jnp.where(lane < -by, crossed, turned)


def difference(far_left, left, right, far_right):
    return 8.0 * (right - left) - (far_right - far_left)


def across(row, lane):
    return difference(
        shifted(row, -2, lane), shifted(row, -1, lane), shifted(row, 1, lane), shifted(row, 2, lane)
    )


def fields_kernel(
    les_ref,
    les_density_ref,
    far_ref,
    far_density_ref,
    les_out,
    total_out,
    stepped_out,
    state,
    advanced,
    inverse,
    far,
    far_inverse,
    flat,
    send_sem,
    recv_sem,
    inverse_send,
    inverse_recv,
    far_send,
    far_recv,
):
    dom = lax.axis_index("dom")
    doms = lax.axis_size("dom")
    has_up = dom > 0
    has_down = dom < doms - 1
    up = lax.rem(dom + doms - 1, doms)
    down = lax.rem(dom + 1, doms)
    lane = lax.broadcasted_iota(I32, (TILES, LANES), 1)
    step = TIME_STEP / 12.0

    barrier = pltpu.get_barrier_semaphore()

    @pl.when(has_up)
    def _():
        pl.semaphore_signal(barrier, inc=1, device_id={"dom": up}, device_id_type=MESH)

    @pl.when(has_down)
    def _():
        pl.semaphore_signal(barrier, inc=1, device_id={"dom": down}, device_id_type=MESH)

    def remote(ref, first, count, landing, sems, where):
        return pltpu.make_async_remote_copy(
            src_ref=ref.at[pl.ds(first, count)],
            dst_ref=ref.at[pl.ds(landing, count)],
            send_sem=sems[0],
            recv_sem=sems[1],
            device_id={"dom": where},
            device_id_type=MESH,
        )

    def up_copy(sub):
        sems = (send_sem.at[sub, 0], recv_sem.at[sub, 0])
        return remote(state.at[sub], 3, 3, ROWS + 3, sems, up)

    def down_copy(sub):
        sems = (send_sem.at[sub, 1], recv_sem.at[sub, 1])
        return remote(state.at[sub], ROWS, 3, 0, sems, down)

    def inverse_up():
        return remote(inverse, 1, 1, ROWS + 1, (inverse_send.at[0], inverse_recv.at[0]), up)

    def inverse_down():
        return remote(inverse, ROWS, 1, 0, (inverse_send.at[1], inverse_recv.at[1]), down)

    def far_up():
        return remote(far, 2, 2, ROWS + 2, (far_send.at[0], far_recv.at[0]), up)

    def far_down():
        return remote(far, ROWS, 2, 0, (far_send.at[1], far_recv.at[1]), down)

    @pl.when(jnp.logical_not(has_up))
    def _():
        for sub in range(SUBSTEPS):
            state[sub, 0:3] = jnp.zeros((3, 3, TILES, LANES), F32)
        inverse[0] = jnp.zeros((TILES, LANES), F32)
        far[0:2] = jnp.zeros((2, 3, TILES, LANES), F32)

    @pl.when(jnp.logical_not(has_down))
    def _():
        for sub in range(SUBSTEPS):
            state[sub, ROWS + 3 :] = jnp.zeros((3, 3, TILES, LANES), F32)
        inverse[ROWS + 1] = jnp.zeros((TILES, LANES), F32)
        far[ROWS + 2 : ROWS + 4] = jnp.zeros((2, 3, TILES, LANES), F32)

    def convert_state(source, target, offset):
        @pl.loop(0, 6)
        def _(index):
            part, rows8 = index // 2, index % 2

            def load(block):
                return source[part, pl.ds(rows8 * TILE, TILE), block * LANES : (block + 1) * LANES]

            def store(row, reg, value):
                target[offset + row, part, reg * TILE : (reg + 1) * TILE, :] = value

            rows_from_tiles(load, flat, store, rows8)

    def convert_density(source, target, offset):
        @pl.loop(0, 2)
        def _(rows8):
            def load(block):
                return 1.0 / source[pl.ds(rows8 * TILE, TILE), block * LANES : (block + 1) * LANES]

            def store(row, reg, value):
                target[offset + row, reg * TILE : (reg + 1) * TILE, :] = value

            rows_from_tiles(load, flat, store, rows8)

    def advance(sub, row):
        base = row + 3
        u, v, p = (state[sub, base, part] for part in range(3))
        dx = [
            difference(*(state[sub, base + by, part] for by in (-2, -1, 1, 2)))
            for part in range(3)
        ]
        dy = [across(field, lane) for field in (u, v, p)]
        inv = inverse[row + 1]
        rate_u = u * dx[0] + v * dy[0] + inv * dx[2]
        rate_v = u * dx[1] + v * dy[1] + inv * dy[2]
        rate_p = u * dx[2] + v * dy[2] + LES_STIFF * (dx[0] + dy[1])
        return u - step * rate_u, v - step * rate_v, p - step * rate_p

    def put_advanced(row, fields):
        for part in range(3):
            advanced[row + 1, part] = fields[part]

    def smooth(sub, row):
        for part in range(3):
            centre = advanced[row + 1, part]
            lateral = advanced[row, part] + advanced[row + 2, part]
            sides = shifted(centre, 1, lane) + shifted(centre, -1, lane)
            value = (1.0 - FILTER_WEIGHT) * centre + FILTER_WEIGHT / 4.0 * (lateral + sides)
            state[sub + 1, row + 3, part] = value
            if sub == 0:
                total_out[part, row] = value
            else:
                total_out[part, row] += value

    def far_row(row):
        base = row + 2
        u, v, p = (far[base, part] for part in range(3))
        dx = [
            difference(*(far[base + by, part] for by in (-2, -1, 1, 2))) for part in range(3)
        ]
        inv = far_inverse[row]
        dy_v, dy_p = across(v, lane), across(p, lane)
        far[base + ROWS + 4, 0] = u - step * (MEAN_FLOW * dx[0] + inv * dx[2])
        far[base + ROWS + 4, 1] = v - step * (MEAN_FLOW * dx[1] + inv * dy_p)
        far[base + ROWS + 4, 2] = p - step * (MEAN_FLOW * dx[2] + FAR_STIFF * (dx[0] + dy_v))

    def loop(low, high, body):
        @pl.loop(low, high)
        def _(row):
            body(row)

    def write_tiles(source, target):
        @pl.loop(0, 6)
        def _(index):
            part, rows8 = index // 2, index % 2

            def load(row, reg):
                return source(row, part, reg)

            def store(block, value):
                target[part, pl.ds(rows8 * TILE, TILE), block * LANES : (block + 1) * LANES] = value

            tiles_from_rows(load, flat, store, rows8)

    convert_state(les_ref, state.at[0], 3)
    convert_density(les_density_ref, inverse, 1)

    pl.semaphore_wait(barrier, jnp.where(has_up, 1, 0) + jnp.where(has_down, 1, 0))

    @pl.when(has_up)
    def _():
        up_copy(0).start()
        inverse_up().start()

    @pl.when(has_down)
    def _():
        down_copy(0).start()
        inverse_down().start()

    for sub in range(SUBSTEPS):
        loop(2, ROWS - 2, lambda row: put_advanced(row, advance(sub, row)))
        loop(3, ROWS - 3, lambda row: smooth(sub, row))
        if sub == 0:
            convert_state(far_ref, far, 2)
            convert_density(far_density_ref, far_inverse, 0)
        if sub == 1:
            loop(2, ROWS - 2, far_row)

        @pl.when(has_up)
        def _():
            down_copy(sub).wait_recv()
            if sub == 0:
                inverse_down().wait_recv()

        loop(0, 2, lambda row: put_advanced(row, advance(sub, row)))
        put_advanced(-1, [jnp.where(has_up, field, 0.0) for field in advance(sub, -1)])
        loop(0, 3, lambda row: smooth(sub, row))

        if sub < SUBSTEPS - 1:

            @pl.when(has_up)
            def _():
                up_copy(sub + 1).start()

        @pl.when(has_down)
        def _():
            up_copy(sub).wait_recv()
            if sub == 0:
                inverse_up().wait_recv()

        loop(ROWS - 2, ROWS, lambda row: put_advanced(row, advance(sub, row)))
        put_advanced(ROWS, [jnp.where(has_down, field, 0.0) for field in advance(sub, ROWS)])
        loop(ROWS - 3, ROWS, lambda row: smooth(sub, row))

        if sub < SUBSTEPS - 1:

            @pl.when(has_down)
            def _():
                down_copy(sub + 1).start()

        if sub == SUBSTEPS - 2:

            @pl.when(has_up)
            def _():
                far_up().start()

            @pl.when(has_down)
            def _():
                far_down().start()

    write_tiles(
        lambda row, part, reg: state[SUBSTEPS, row + 3, part, reg * TILE : (reg + 1) * TILE, :],
        les_out,
    )

    @pl.when(has_up)
    def _():
        far_down().wait_recv()

    @pl.when(has_down)
    def _():
        far_up().wait_recv()

    loop(0, 2, far_row)
    loop(ROWS - 2, ROWS, far_row)
    write_tiles(
        lambda row, part, reg: far[row + ROWS + 6, part, reg * TILE : (reg + 1) * TILE, :],
        stepped_out,
    )

    @pl.when(has_up)
    def _():
        for sub in range(SUBSTEPS):
            up_copy(sub).wait_send()
        inverse_up().wait_send()
        far_up().wait_send()

    @pl.when(has_down)
    def _():
        for sub in range(SUBSTEPS):
            down_copy(sub).wait_send()
        inverse_down().wait_send()
        far_down().wait_send()


def fields(les_state, les_density, far_state, far_density):
    block = jax.ShapeDtypeStruct((3, ROWS, COLS), F32)
    return pl.pallas_call(
        fields_kernel,
        out_shape=(block, jax.ShapeDtypeStruct((3, ROWS, TILES, LANES), F32), block),
        in_specs=[VMEM] * 4,
        out_specs=(VMEM,) * 3,
        scratch_shapes=[
            pltpu.VMEM((SUBSTEPS + 1, ROWS + 6, 3, TILES, LANES), F32),
            pltpu.VMEM((ROWS + 2, 3, TILES, LANES), F32),
            pltpu.VMEM((ROWS + 2, TILES, LANES), F32),
            pltpu.VMEM((2 * ROWS + 6, 3, TILES, LANES), F32),
            pltpu.VMEM((ROWS, TILES, LANES), F32),
            pltpu.VMEM((TILES * TILE, LANES), F32),
            pltpu.SemaphoreType.DMA((SUBSTEPS, 2)),
            pltpu.SemaphoreType.DMA((SUBSTEPS, 2)),
            pltpu.SemaphoreType.DMA((2,)),
            pltpu.SemaphoreType.DMA((2,)),
            pltpu.SemaphoreType.DMA((2,)),
            pltpu.SemaphoreType.DMA((2,)),
        ],
        compiler_params=params(collective_id=0, has_side_effects=True),
        name="fields",
    )(les_state, les_density, far_state, far_density)


RANK_BLOCK = 256


def rank_kernel(count_ref, owner_ref, rank_out):
    live = count_ref[0]
    owners = lax.broadcasted_iota(I32, (DEVICES, RANK_BLOCK), 0)
    before = lax.broadcasted_iota(I32, (RANK_BLOCK, RANK_BLOCK), 0)
    after = lax.broadcasted_iota(I32, (RANK_BLOCK, RANK_BLOCK), 1)
    weights = jnp.concatenate(
        [
            jnp.where(before < after, 1.0, 0.0).astype(BF16),
            jnp.ones((RANK_BLOCK, RANK_BLOCK), BF16),
        ],
        axis=1,
    )
    place = lax.broadcasted_iota(I32, (1, RANK_BLOCK), 1)
    base = jnp.zeros((DEVICES, RANK_BLOCK), F32)
    wide = RANK_BLOCK // LANES
    for block in range(FACES // RANK_BLOCK):
        rows = [owner_ref[block * wide + i : block * wide + i + 1, :] for i in range(wide)]
        named = jnp.concatenate(rows, axis=1)
        is_live = place + block * RANK_BLOCK < live
        named = jnp.where(is_live, named, -1)
        hits = jnp.where(owners == named, 1.0, 0.0)
        counted = jnp.dot(hits.astype(BF16), weights, preferred_element_type=F32)
        rank = jnp.sum(hits * (counted[:, :RANK_BLOCK] + base), axis=0, keepdims=True)
        base = base + counted[:, RANK_BLOCK:]
        rank = jnp.where(is_live, rank.astype(I32), -1)
        for i in range(wide):
            rank_out[block * wide + i : block * wide + i + 1, :] = rank[
                :, i * LANES : (i + 1) * LANES
            ]


def ranks(counts, owner):
    return pl.pallas_call(
        rank_kernel,
        out_shape=jax.ShapeDtypeStruct((FACE_ROWS, LANES), I32),
        in_specs=[SMEM, VMEM],
        out_specs=VMEM,
        compiler_params=params(),
        name="ranks",
    )(counts, owner)


def halves(values):
    high = values.astype(BF16).astype(F32)
    return high, values - high


PICK = 512


def pick_kernel(total_ref, cell_ref, area_ref, owner_ref, target_ref, rank_ref, out, turned, slots):
    for part in range(3):
        for block in range(CELL_ROWS // LANES):
            columns = slice(block * LANES, (block + 1) * LANES)
            high, low = halves(total_ref[part, columns, :].T)
            turned[2 * part * LANES : (2 * part + 1) * LANES, columns] = high.astype(BF16)
            turned[(2 * part + 1) * LANES : (2 * part + 2) * LANES, columns] = low.astype(BF16)
    slots[...] = jnp.zeros_like(slots)
    wide = PICK // LANES
    cell_rows = lax.broadcasted_iota(I32, (CELL_ROWS, PICK), 0)
    index = lax.broadcasted_iota(I32, (LANES, PICK), 0)

    @pl.loop(0, FACES // PICK)
    def _(block):
        def line(ref):
            return jnp.concatenate([ref[pl.ds(block * wide + i, 1), :] for i in range(wide)], axis=1)

        cell, area, owner, target, rank = (
            line(ref) for ref in (cell_ref, area_ref, owner_ref, target_ref, rank_ref)
        )
        row, column = cell >> 13, cell & (COLS - 1)
        cell_row = row * TILES + ((column >> 7) & 7) * TILE + (column >> 10)
        picked = jnp.where(cell_rows == cell_row, 1.0, 0.0).astype(BF16)
        found = jnp.dot(turned[...], picked, preferred_element_type=F32)
        is_lane = index == (column & (LANES - 1))
        is_rank = index == rank
        parts = []
        for part in range(3):
            both = (
                found[2 * part * LANES : (2 * part + 1) * LANES]
                + found[(2 * part + 1) * LANES : (2 * part + 2) * LANES]
            )
            value = jnp.sum(jnp.where(is_lane, both, 0.0), axis=0, keepdims=True)
            parts.extend(halves(value * (area * (1.0 / SUBSTEPS))))
        for shift in (0, 7, 14):
            parts.append(((target >> shift) & (LANES - 1)).astype(F32))
        spread = jnp.concatenate(
            [jnp.where(is_rank, part, 0.0).astype(BF16) for part in parts], axis=0
        )
        named = jnp.where(index == owner, 1.0, 0.0).astype(BF16)
        slots[...] += lax.dot_general(
            named, spread, (((1,), (1,)), ((), ())), preferred_element_type=F32
        )

    pieces = [slots[:, i * LANES : (i + 1) * LANES] for i in range(9)]
    for part in range(3):
        out[pl.ds(part, DEVICES, stride=4), :] = pieces[2 * part] + pieces[2 * part + 1]
    out[pl.ds(3, DEVICES, stride=4), :] = (
        pieces[6] + pieces[7] * float(LANES) + pieces[8] * float(LANES * LANES)
    )


def pick(total, cell, area, owner, target, rank):
    return pl.pallas_call(
        pick_kernel,
        out_shape=jax.ShapeDtypeStruct((4 * DEVICES, LANES), F32),
        in_specs=[VMEM] * 6,
        out_specs=VMEM,
        scratch_shapes=[
            pltpu.VMEM((6 * LANES, CELL_ROWS), BF16),
            pltpu.VMEM((DEVICES, 9 * LANES), F32),
        ],
        compiler_params=params(),
        name="pick",
    )(total, cell, area, owner, target, rank)


def exchange_kernel(ready, arrived, local_sem, send_sem, recv_sem):
    secs, doms = lax.axis_size("sec"), lax.axis_size("dom")
    devices = secs * doms
    me = lax.axis_index("sec") * doms + lax.axis_index("dom")
    barrier = pltpu.get_barrier_semaphore()

    def place(offset):
        other = lax.rem(me + offset, devices)
        return other, {"sec": other // doms, "dom": lax.rem(other, doms)}

    @pl.loop(1, devices)
    def _(offset):
        pl.semaphore_signal(barrier, inc=1, device_id=place(offset)[1], device_id_type=MESH)

    own = pltpu.make_async_copy(ready.at[me], arrived.at[me], local_sem)
    own.start()
    pl.semaphore_wait(barrier, devices - 1)

    @pl.loop(1, devices)
    def _(offset):
        other, where = place(offset)
        pltpu.make_async_remote_copy(
            src_ref=ready.at[other],
            dst_ref=arrived.at[me],
            send_sem=send_sem,
            recv_sem=recv_sem,
            device_id=where,
            device_id_type=MESH,
        ).start()

    own.wait()
    all_but_one = pl.ds(0, devices - 1)
    pltpu.make_async_copy(arrived.at[all_but_one], arrived.at[all_but_one], recv_sem).wait()
    pltpu.make_async_copy(ready.at[all_but_one], ready.at[all_but_one], send_sem).wait()


def exchange(ready):
    return pl.pallas_call(
        exchange_kernel,
        out_shape=jax.ShapeDtypeStruct(ready.shape, F32),
        in_specs=[VMEM],
        out_specs=VMEM,
        scratch_shapes=[pltpu.SemaphoreType.DMA] * 3,
        compiler_params=params(collective_id=1, has_side_effects=True),
        name="exchange",
    )(ready)


ADD = 512


def add_kernel(arrived_ref, stepped_ref, out, held, sums):
    for part in range(4):
        held[part] = arrived_ref[pl.ds(part, DEVICES, stride=4), :]
    sums[...] = jnp.zeros_like(sums)
    wide = ADD // LANES
    cell_rows = lax.broadcasted_iota(I32, (CELL_ROWS, ADD), 0)
    index = lax.broadcasted_iota(I32, (LANES, ADD), 0)

    @pl.loop(0, DEVICES * RANKS // ADD)
    def _(block):
        def line(part):
            return jnp.concatenate(
                [held[part, pl.ds(block * wide + i, 1), :] for i in range(wide)], axis=1
            )

        target = line(3).astype(I32)
        row, column = target >> 13, target & (COLS - 1)
        cell_row = ((row >> 3) * TILES + (column >> 7)) * TILE + (row & 7)
        hits = jnp.where(cell_rows == cell_row, 1.0, 0.0).astype(BF16)
        is_lane = index == (column & (LANES - 1))
        parts = [half for part in range(3) for half in halves(line(part))]
        spread = jnp.concatenate(
            [jnp.where(is_lane, part, 0.0).astype(BF16) for part in parts], axis=0
        )
        sums[...] += lax.dot_general(
            hits, spread, (((1,), (1,)), ((), ())), preferred_element_type=F32
        )

    for part in range(3):
        high = slice(2 * part * LANES, (2 * part + 1) * LANES)
        low = slice((2 * part + 1) * LANES, (2 * part + 2) * LANES)
        for band in range(ROWS // TILE):
            rows = slice(band * TILE, (band + 1) * TILE)
            for block in range(TILES):
                first = (band * TILES + block) * TILE
                columns = slice(block * LANES, (block + 1) * LANES)
                out[part, rows, columns] = stepped_ref[part, rows, columns] + (
                    sums[first : first + TILE, high] + sums[first : first + TILE, low]
                )


def add(arrived, stepped):
    return pl.pallas_call(
        add_kernel,
        out_shape=jax.ShapeDtypeStruct((3, ROWS, COLS), F32),
        in_specs=[VMEM] * 2,
        out_specs=VMEM,
        scratch_shapes=[
            pltpu.VMEM((4, DEVICES, RANKS), F32),
            pltpu.VMEM((CELL_ROWS, 6 * LANES), F32),
        ],
        compiler_params=params(),
        name="add",
    )(arrived, stepped)


def local(
    les_state,
    les_density,
    far_state,
    far_density,
    face_cell,
    face_area,
    face_owner,
    face_counts,
    face_target,
):
    cell, area, owner, target = (
        array.reshape(FACE_ROWS, LANES) for array in (face_cell, face_area, face_owner, face_target)
    )
    rank = ranks(face_counts, owner)
    les_final, total, stepped = fields(les_state[0], les_density[0], far_state[0], far_density[0])
    ready = pick(total.reshape(3, CELL_ROWS, LANES), cell, area, owner, target, rank)
    arrived = exchange(ready.reshape(DEVICES, 4, LANES))
    far_final = add(arrived.reshape(4 * DEVICES, LANES), stepped)
    return les_final[None], far_final[None]


def solution(mesh):
    field = P("sec", None, "dom", None)
    density = P("sec", "dom", None)
    faces = P(("sec", "dom"))
    return jax.shard_map(
        local,
        mesh=mesh,
        in_specs=(field, density, field, density) + (faces,) * 5,
        out_specs=(field, field),
        check_vma=False,
    )
```

```python
import jax
import jax.numpy as jnp
from jax import lax
from jax.experimental import pallas as pl
from jax.experimental.pallas import tpu as pltpu
from jax.sharding import PartitionSpec as P

SUBSTEPS = 5
UNROLL = {12: 4, 10: 5}
TIME_STEP = 0.1
LES_STIFF = 1.0
FAR_STIFF = 1.0
FILTER_WEIGHT = 0.5
MEAN_FLOW = 0.3

LANES = 128
TILE = 8
ROWS = 16
COLS = 8192
TILES = COLS // LANES
REGS = TILES // TILE
FACES = 8192
FACE_ROWS = FACES // LANES
DEVICES = 128
RANKS = 128
CELL_ROWS = ROWS * COLS // LANES

MESH = pl.DeviceIdType.MESH
VMEM = pl.BlockSpec(memory_space=pltpu.VMEM)
SMEM = pl.BlockSpec(memory_space=pltpu.SMEM)
F32 = jnp.float32
BF16 = jnp.bfloat16
I32 = jnp.int32


def params(**more):
    return pltpu.CompilerParams(vmem_limit_bytes=56 * 1024 * 1024, **more)


def rows_from_tiles(load, flat, store, rows8):
    for block in range(TILES):
        flat[block * TILE : (block + 1) * TILE, :] = load(block)
    for row in range(TILE):
        for reg in range(REGS):
            store(rows8 * TILE + row, reg, flat[pl.ds(TILE * reg + row, TILE, stride=TILES), :])


def tiles_from_rows(load, flat, store, rows8):
    for row in range(TILE):
        for reg in range(REGS):
            flat[pl.ds(TILE * reg + row, TILE, stride=TILES), :] = load(rows8 * TILE + row, reg)
    for block in range(TILES):
        store(block, flat[block * TILE : (block + 1) * TILE, :])


def shifted(row, by, lane):
    if by > 0:
        turned = pltpu.roll(row, LANES - by, 1)
        crossed = jnp.concatenate([turned[TILE:], pltpu.roll(turned[:TILE], TILE - 1, 0)], axis=0)
        return jnp.where(lane >= LANES - by, crossed, turned)
    turned = pltpu.roll(row, -by, 1)
    crossed = jnp.concatenate(
        [pltpu.roll(turned[TILES - TILE :], 1, 0), turned[: TILES - TILE]], axis=0
    )
    return jnp.where(lane < -by, crossed, turned)


def difference(far_left, left, right, far_right):
    return 8.0 * (right - left) - (far_right - far_left)


def across(row, lane):
    return difference(
        shifted(row, -2, lane), shifted(row, -1, lane), shifted(row, 1, lane), shifted(row, 2, lane)
    )


def fields_kernel(
    les_ref,
    les_density_ref,
    far_ref,
    far_density_ref,
    les_out,
    total_out,
    stepped_out,
    state,
    advanced,
    inverse,
    far,
    far_inverse,
    flat,
    send_sem,
    recv_sem,
    inverse_send,
    inverse_recv,
    far_send,
    far_recv,
):
    dom = lax.axis_index("dom")
    doms = lax.axis_size("dom")
    has_up = dom > 0
    has_down = dom < doms - 1
    up = lax.rem(dom + doms - 1, doms)
    down = lax.rem(dom + 1, doms)
    lane = lax.broadcasted_iota(I32, (TILES, LANES), 1)
    step = TIME_STEP / 12.0

    barrier = pltpu.get_barrier_semaphore()

    @pl.when(has_up)
    def _():
        pl.semaphore_signal(barrier, inc=1, device_id={"dom": up}, device_id_type=MESH)

    @pl.when(has_down)
    def _():
        pl.semaphore_signal(barrier, inc=1, device_id={"dom": down}, device_id_type=MESH)

    def remote(ref, first, count, landing, sems, where):
        return pltpu.make_async_remote_copy(
            src_ref=ref.at[pl.ds(first, count)],
            dst_ref=ref.at[pl.ds(landing, count)],
            send_sem=sems[0],
            recv_sem=sems[1],
            device_id={"dom": where},
            device_id_type=MESH,
        )

    def up_copy(sub):
        sems = (send_sem.at[sub, 0], recv_sem.at[sub, 0])
        return remote(state.at[sub], 3, 3, ROWS + 3, sems, up)

    def down_copy(sub):
        sems = (send_sem.at[sub, 1], recv_sem.at[sub, 1])
        return remote(state.at[sub], ROWS, 3, 0, sems, down)

    def inverse_up():
        return remote(inverse, 1, 1, ROWS + 1, (inverse_send.at[0], inverse_recv.at[0]), up)

    def inverse_down():
        return remote(inverse, ROWS, 1, 0, (inverse_send.at[1], inverse_recv.at[1]), down)

    def far_up():
        return remote(far, 2, 2, ROWS + 2, (far_send.at[0], far_recv.at[0]), up)

    def far_down():
        return remote(far, ROWS, 2, 0, (far_send.at[1], far_recv.at[1]), down)

    @pl.when(jnp.logical_not(has_up))
    def _():
        for sub in range(SUBSTEPS):
            state[sub, 0:3] = jnp.zeros((3, 3, TILES, LANES), F32)
        inverse[0] = jnp.zeros((TILES, LANES), F32)
        far[0:2] = jnp.zeros((2, 3, TILES, LANES), F32)

    @pl.when(jnp.logical_not(has_down))
    def _():
        for sub in range(SUBSTEPS):
            state[sub, ROWS + 3 :] = jnp.zeros((3, 3, TILES, LANES), F32)
        inverse[ROWS + 1] = jnp.zeros((TILES, LANES), F32)
        far[ROWS + 2 : ROWS + 4] = jnp.zeros((2, 3, TILES, LANES), F32)

    def convert_state(source, target, offset):
        @pl.loop(0, 6)
        def _(index):
            part, rows8 = index // 2, index % 2

            def load(block):
                return source[part, pl.ds(rows8 * TILE, TILE), block * LANES : (block + 1) * LANES]

            def store(row, reg, value):
                target[offset + row, part, reg * TILE : (reg + 1) * TILE, :] = value

            rows_from_tiles(load, flat, store, rows8)

    def convert_density(source, target, offset):
        @pl.loop(0, 2)
        def _(rows8):
            def load(block):
                return 1.0 / source[pl.ds(rows8 * TILE, TILE), block * LANES : (block + 1) * LANES]

            def store(row, reg, value):
                target[offset + row, reg * TILE : (reg + 1) * TILE, :] = value

            rows_from_tiles(load, flat, store, rows8)

    def advance(sub, row):
        base = row + 3
        u, v, p = (state[sub, base, part] for part in range(3))
        dx = [
            difference(*(state[sub, base + by, part] for by in (-2, -1, 1, 2)))
            for part in range(3)
        ]
        dy = [across(field, lane) for field in (u, v, p)]
        inv = inverse[row + 1]
        rate_u = u * dx[0] + v * dy[0] + inv * dx[2]
        rate_v = u * dx[1] + v * dy[1] + inv * dy[2]
        rate_p = u * dx[2] + v * dy[2] + LES_STIFF * (dx[0] + dy[1])
        return u - step * rate_u, v - step * rate_v, p - step * rate_p

    def put_advanced(row, fields):
        for part in range(3):
            advanced[row + 1, part] = fields[part]

    def smooth(sub, row):
        for part in range(3):
            centre = advanced[row + 1, part]
            lateral = advanced[row, part] + advanced[row + 2, part]
            sides = shifted(centre, 1, lane) + shifted(centre, -1, lane)
            value = (1.0 - FILTER_WEIGHT) * centre + FILTER_WEIGHT / 4.0 * (lateral + sides)
            state[sub + 1, row + 3, part] = value
            if sub == 0:
                total_out[part, row] = value
            else:
                total_out[part, row] += value

    def far_row(row):
        base = row + 2
        u, v, p = (far[base, part] for part in range(3))
        dx = [
            difference(*(far[base + by, part] for by in (-2, -1, 1, 2))) for part in range(3)
        ]
        inv = far_inverse[row]
        dy_v, dy_p = across(v, lane), across(p, lane)
        far[base + ROWS + 4, 0] = u - step * (MEAN_FLOW * dx[0] + inv * dx[2])
        far[base + ROWS + 4, 1] = v - step * (MEAN_FLOW * dx[1] + inv * dy_p)
        far[base + ROWS + 4, 2] = p - step * (MEAN_FLOW * dx[2] + FAR_STIFF * (dx[0] + dy_v))

    def loop(low, high, body):
        @pl.loop(low, high, unroll=UNROLL.get(high - low, high - low))
        def _(row):
            body(row)

    def write_tiles(source, target):
        @pl.loop(0, 6)
        def _(index):
            part, rows8 = index // 2, index % 2

            def load(row, reg):
                return source(row, part, reg)

            def store(block, value):
                target[part, pl.ds(rows8 * TILE, TILE), block * LANES : (block + 1) * LANES] = value

            tiles_from_rows(load, flat, store, rows8)

    convert_state(les_ref, state.at[0], 3)
    convert_density(les_density_ref, inverse, 1)

    pl.semaphore_wait(barrier, jnp.where(has_up, 1, 0) + jnp.where(has_down, 1, 0))

    @pl.when(has_up)
    def _():
        up_copy(0).start()
        inverse_up().start()

    @pl.when(has_down)
    def _():
        down_copy(0).start()
        inverse_down().start()

    for sub in range(SUBSTEPS):
        loop(2, ROWS - 2, lambda row: put_advanced(row, advance(sub, row)))
        loop(3, ROWS - 3, lambda row: smooth(sub, row))
        if sub == 0:
            convert_state(far_ref, far, 2)
            convert_density(far_density_ref, far_inverse, 0)
        if sub == 1:
            loop(2, ROWS - 2, far_row)

        @pl.when(has_up)
        def _():
            down_copy(sub).wait_recv()
            if sub == 0:
                inverse_down().wait_recv()

        loop(0, 2, lambda row: put_advanced(row, advance(sub, row)))
        put_advanced(-1, [jnp.where(has_up, field, 0.0) for field in advance(sub, -1)])
        loop(0, 3, lambda row: smooth(sub, row))

        if sub < SUBSTEPS - 1:

            @pl.when(has_up)
            def _():
                up_copy(sub + 1).start()

        @pl.when(has_down)
        def _():
            up_copy(sub).wait_recv()
            if sub == 0:
                inverse_up().wait_recv()

        loop(ROWS - 2, ROWS, lambda row: put_advanced(row, advance(sub, row)))
        put_advanced(ROWS, [jnp.where(has_down, field, 0.0) for field in advance(sub, ROWS)])
        loop(ROWS - 3, ROWS, lambda row: smooth(sub, row))

        if sub < SUBSTEPS - 1:

            @pl.when(has_down)
            def _():
                down_copy(sub + 1).start()

        if sub == SUBSTEPS - 2:

            @pl.when(has_up)
            def _():
                far_up().start()

            @pl.when(has_down)
            def _():
                far_down().start()

    write_tiles(
        lambda row, part, reg: state[SUBSTEPS, row + 3, part, reg * TILE : (reg + 1) * TILE, :],
        les_out,
    )

    @pl.when(has_up)
    def _():
        far_down().wait_recv()

    @pl.when(has_down)
    def _():
        far_up().wait_recv()

    loop(0, 2, far_row)
    loop(ROWS - 2, ROWS, far_row)
    write_tiles(
        lambda row, part, reg: far[row + ROWS + 6, part, reg * TILE : (reg + 1) * TILE, :],
        stepped_out,
    )

    @pl.when(has_up)
    def _():
        for sub in range(SUBSTEPS):
            up_copy(sub).wait_send()
        inverse_up().wait_send()
        far_up().wait_send()

    @pl.when(has_down)
    def _():
        for sub in range(SUBSTEPS):
            down_copy(sub).wait_send()
        inverse_down().wait_send()
        far_down().wait_send()


def fields(les_state, les_density, far_state, far_density):
    block = jax.ShapeDtypeStruct((3, ROWS, COLS), F32)
    return pl.pallas_call(
        fields_kernel,
        out_shape=(block, jax.ShapeDtypeStruct((3, ROWS, TILES, LANES), F32), block),
        in_specs=[VMEM] * 4,
        out_specs=(VMEM,) * 3,
        scratch_shapes=[
            pltpu.VMEM((SUBSTEPS + 1, ROWS + 6, 3, TILES, LANES), F32),
            pltpu.VMEM((ROWS + 2, 3, TILES, LANES), F32),
            pltpu.VMEM((ROWS + 2, TILES, LANES), F32),
            pltpu.VMEM((2 * ROWS + 6, 3, TILES, LANES), F32),
            pltpu.VMEM((ROWS, TILES, LANES), F32),
            pltpu.VMEM((TILES * TILE, LANES), F32),
            pltpu.SemaphoreType.DMA((SUBSTEPS, 2)),
            pltpu.SemaphoreType.DMA((SUBSTEPS, 2)),
            pltpu.SemaphoreType.DMA((2,)),
            pltpu.SemaphoreType.DMA((2,)),
            pltpu.SemaphoreType.DMA((2,)),
            pltpu.SemaphoreType.DMA((2,)),
        ],
        compiler_params=params(collective_id=0, has_side_effects=True),
        name="fields",
    )(les_state, les_density, far_state, far_density)


RANK_BLOCK = 256
BUCKETS = 4
BUCKET = CELL_ROWS // BUCKETS
BLOCK = 256
LINE = 512
TOGETHER = 4
PLANNED = 48
SORTED = 80


def halves(values):
    high = values.astype(BF16).astype(F32)
    return high, values - high


def indices(rows, columns):
    return lax.broadcasted_iota(I32, (rows, columns), 0).astype(F32).astype(BF16)


def one_hot(index, line):
    return jnp.where(index == line.astype(BF16), jnp.ones((), BF16), jnp.zeros((), BF16))


def spread(index, line, parts):
    here = index == line.astype(BF16)
    return jnp.concatenate(
        [jnp.where(here, part.astype(BF16), jnp.zeros((), BF16)) for part in parts], axis=0
    )


def product(left, right):
    return lax.dot_general(left, right, (((1,), (1,)), ((), ())), preferred_element_type=F32)


def lines(ref, first, count):
    return jnp.concatenate([ref[pl.ds(first + i, 1), :] for i in range(count)], axis=1)


def bucket_places(bucket, rows, starts_ref):
    before = lax.broadcasted_iota(I32, (LANES, 2 * LANES), 0)
    after = lax.broadcasted_iota(I32, (LANES, 2 * LANES), 1)
    weights = jnp.where((before < after) | (after >= LANES), 1.0, 0.0).astype(BF16)
    below = lax.broadcasted_iota(I32, (rows, rows), 0) > lax.broadcasted_iota(I32, (rows, rows), 1)
    below = jnp.where(below, 1.0, 0.0).astype(BF16)
    place = jnp.full((rows, LANES), -1.0, F32)
    base = jnp.zeros((1, LANES), F32)
    for b in range(BUCKETS):
        starts_ref[b] = jnp.max(base).astype(I32)
        here = bucket == b
        counted = jnp.dot(
            jnp.where(here, 1.0, 0.0).astype(BF16), weights, preferred_element_type=F32
        )
        totals = counted[:, LANES:]
        offset = jnp.dot(below, totals.astype(BF16), preferred_element_type=F32)
        place = jnp.where(here, counted[:, :LANES] + offset + base * float(BLOCK), place)
        total = offset[rows - 1 :] + totals[rows - 1 :]
        base = base + jnp.floor((total + (BLOCK - 1.0)) * (1.0 / BLOCK))
    starts_ref[BUCKETS] = jnp.max(base).astype(I32)
    return place


def block_and_lane(place):
    block = jnp.floor(place * (1.0 / BLOCK))
    return block, place - block * float(BLOCK)


def plan_kernel(
    count_ref, owner_ref, cell_ref, area_ref, target_ref, order, starts, targets, facts, grid
):
    live = count_ref[0]
    owners = lax.broadcasted_iota(I32, (DEVICES, RANK_BLOCK), 0)
    before = lax.broadcasted_iota(I32, (RANK_BLOCK, RANK_BLOCK), 0)
    after = lax.broadcasted_iota(I32, (RANK_BLOCK, RANK_BLOCK), 1)
    weights = jnp.concatenate(
        [
            jnp.where(before < after, 1.0, 0.0).astype(BF16),
            jnp.ones((RANK_BLOCK, RANK_BLOCK), BF16),
        ],
        axis=1,
    )
    face = lax.broadcasted_iota(I32, (1, RANK_BLOCK), 1)
    base = jnp.zeros((DEVICES, RANK_BLOCK), F32)
    wide = RANK_BLOCK // LANES
    for block in range(FACES // RANK_BLOCK):
        named = lines(owner_ref, block * wide, wide)
        named = jnp.where(face + block * RANK_BLOCK < live, named, -1)
        hits = jnp.where(owners == named, 1.0, 0.0)
        counted = jnp.dot(hits.astype(BF16), weights, preferred_element_type=F32)
        rank = jnp.sum(hits * (counted[:, :RANK_BLOCK] + base), axis=0, keepdims=True)
        base = base + counted[:, RANK_BLOCK:]
        for i in range(wide):
            facts[3, block * wide + i : block * wide + i + 1, :] = rank[
                :, i * LANES : (i + 1) * LANES
            ]

    cell = cell_ref[...]
    target = target_ref[...] + 1
    row, column = cell >> 13, cell & (COLS - 1)
    cell_row = row * TILES + ((column >> 7) & 7) * TILE + (column >> 10)
    number = (
        lax.broadcasted_iota(I32, (FACE_ROWS, LANES), 0) * LANES
        + lax.broadcasted_iota(I32, (FACE_ROWS, LANES), 1)
    )
    bucket = jnp.where(number < live, cell_row >> 8, -1)
    facts[0] = (cell_row & (BUCKET - 1)).astype(F32)
    facts[1] = (column & (LANES - 1)).astype(F32)
    facts[2] = jnp.where(number < live, owner_ref[...], -1).astype(F32)
    facts[4], facts[5] = halves(area_ref[...] * (1.0 / SUBSTEPS))
    for i in range(3):
        facts[6 + i] = ((target >> (7 * i)) & (LANES - 1)).astype(F32)
    facts[9], facts[10] = block_and_lane(bucket_places(bucket, FACE_ROWS, starts))

    order[...] = jnp.zeros_like(order)
    grid[...] = jnp.zeros_like(grid)
    by_lane = indices(BLOCK, LINE)
    by_block = indices(PLANNED, LINE)
    by_device = indices(DEVICES, LINE)
    wide = LINE // LANES

    @pl.loop(0, FACES // LINE, unroll=2)
    def _(step):
        fact = [lines(facts.at[i], step * wide, wide) for i in range(11)]
        order[...] += product(spread(by_block, fact[9], fact[:6]), one_hot(by_lane, fact[10]))
        grid[...] += product(spread(by_device, fact[2], fact[6:9]), one_hot(by_device, fact[3]))

    targets[...] = (
        grid[:DEVICES]
        + grid[DEVICES : 2 * DEVICES] * float(LANES)
        + grid[2 * DEVICES :] * float(LANES * LANES)
    )


def plan(counts, owner, cell, area, target):
    return pl.pallas_call(
        plan_kernel,
        out_shape=(
            jax.ShapeDtypeStruct((6 * PLANNED, BLOCK), F32),
            jax.ShapeDtypeStruct((BUCKETS + 1,), I32),
            jax.ShapeDtypeStruct((DEVICES, RANKS), F32),
        ),
        in_specs=[SMEM] + [VMEM] * 4,
        out_specs=(VMEM, SMEM, VMEM),
        scratch_shapes=[
            pltpu.VMEM((11, FACE_ROWS, LANES), F32),
            pltpu.VMEM((3 * DEVICES, RANKS), F32),
        ],
        compiler_params=params(),
        name="plan",
    )(counts, owner, cell, area, target)


def bucket_of(block, starts_ref):
    bucket = 0
    for b in range(1, BUCKETS):
        bucket = bucket + jnp.where(block >= starts_ref[b], 1, 0)
    return bucket


def steps_of(starts_ref):
    return (starts_ref[BUCKETS] + TOGETHER - 1) // TOGETHER


def pick_kernel(total_ref, order_ref, starts_ref, targets_ref, out, turned, slots):
    for part in range(3):
        for block in range(CELL_ROWS // LANES):
            high, low = halves(total_ref[part, block * LANES : (block + 1) * LANES, :].T)
            bucket = block * LANES // BUCKET
            columns = slice(block * LANES % BUCKET, block * LANES % BUCKET + LANES)
            turned[bucket, 2 * part * LANES : (2 * part + 1) * LANES, columns] = high.astype(BF16)
            turned[bucket, (2 * part + 1) * LANES : (2 * part + 2) * LANES, columns] = low.astype(
                BF16
            )
    slots[...] = jnp.zeros_like(slots)
    by_row = indices(BUCKET, BLOCK)
    lane = lax.broadcasted_iota(I32, (LANES, BLOCK), 0).astype(F32)
    by_device = indices(DEVICES, BLOCK * TOGETHER)

    @pl.loop(0, steps_of(starts_ref))
    def _(step):
        surface = []
        placed = []
        for i in range(TOGETHER):
            block = step * TOGETHER + i
            row, where, owner, rank, high, low = (
                order_ref[pl.ds(part * PLANNED + block, 1), :] for part in range(6)
            )
            found = jnp.dot(
                turned[bucket_of(block, starts_ref)],
                one_hot(by_row, row),
                preferred_element_type=F32,
            )
            is_lane = lane == where
            parts = []
            for part in range(3):
                both = (
                    found[2 * part * LANES : (2 * part + 1) * LANES]
                    + found[(2 * part + 1) * LANES : (2 * part + 2) * LANES]
                )
                value = jnp.sum(jnp.where(is_lane, both, 0.0), axis=0, keepdims=True)
                parts.extend(halves(value * (high + low)))
            surface.append(parts)
            placed.append((owner, rank))
        joined = [jnp.concatenate(part, axis=1) for part in zip(*surface)]
        owner, rank = (jnp.concatenate(part, axis=1) for part in zip(*placed))
        slots[...] += product(spread(by_device, owner, joined), one_hot(by_device, rank))

    pieces = [slots[i * DEVICES : (i + 1) * DEVICES] for i in range(6)]
    for part in range(3):
        out[pl.ds(part, DEVICES, stride=4), :] = pieces[2 * part] + pieces[2 * part + 1]
    out[pl.ds(3, DEVICES, stride=4), :] = targets_ref[...]


def pick(total, order, starts, targets):
    return pl.pallas_call(
        pick_kernel,
        out_shape=jax.ShapeDtypeStruct((4 * DEVICES, LANES), F32),
        in_specs=[VMEM, VMEM, SMEM, VMEM],
        out_specs=VMEM,
        scratch_shapes=[
            pltpu.VMEM((BUCKETS, 6 * LANES, BUCKET), BF16),
            pltpu.VMEM((6 * DEVICES, RANKS), F32),
        ],
        compiler_params=params(),
        name="pick",
    )(total, order, starts, targets)


def exchange_kernel(ready, arrived, local_sem, send_sem, recv_sem):
    secs, doms = lax.axis_size("sec"), lax.axis_size("dom")
    devices = secs * doms
    me = lax.axis_index("sec") * doms + lax.axis_index("dom")
    barrier = pltpu.get_barrier_semaphore()

    def place(offset):
        other = lax.rem(me + offset, devices)
        return other, {"sec": other // doms, "dom": lax.rem(other, doms)}

    @pl.loop(1, devices)
    def _(offset):
        pl.semaphore_signal(barrier, inc=1, device_id=place(offset)[1], device_id_type=MESH)

    own = pltpu.make_async_copy(ready.at[me], arrived.at[me], local_sem)
    own.start()
    pl.semaphore_wait(barrier, devices - 1)

    @pl.loop(1, devices)
    def _(offset):
        other, where = place(offset)
        pltpu.make_async_remote_copy(
            src_ref=ready.at[other],
            dst_ref=arrived.at[me],
            send_sem=send_sem,
            recv_sem=recv_sem,
            device_id=where,
            device_id_type=MESH,
        ).start()

    own.wait()
    all_but_one = pl.ds(0, devices - 1)
    pltpu.make_async_copy(arrived.at[all_but_one], arrived.at[all_but_one], recv_sem).wait()
    pltpu.make_async_copy(ready.at[all_but_one], ready.at[all_but_one], send_sem).wait()


def exchange(ready):
    return pl.pallas_call(
        exchange_kernel,
        out_shape=jax.ShapeDtypeStruct(ready.shape, F32),
        in_specs=[VMEM],
        out_specs=VMEM,
        scratch_shapes=[pltpu.SemaphoreType.DMA] * 3,
        compiler_params=params(collective_id=1, has_side_effects=True),
        name="exchange",
    )(ready)


def add_kernel(arrived_ref, stepped_ref, out, held, order, sums, starts):
    for part in range(3):
        high, low = halves(arrived_ref[pl.ds(part, DEVICES, stride=4), :])
        held[2 * part] = high
        held[2 * part + 1] = low
    target = arrived_ref[pl.ds(3, DEVICES, stride=4), :].astype(I32) - 1
    row, column = target >> 13, target & (COLS - 1)
    cell_row = ((row >> 3) * TILES + (column >> 7)) * TILE + (row & 7)
    bucket = jnp.where(target >= 0, cell_row >> 8, -1)
    held[6] = (cell_row & (BUCKET - 1)).astype(F32)
    held[7] = (column & (LANES - 1)).astype(F32)
    held[8], held[9] = block_and_lane(bucket_places(bucket, DEVICES, starts))
    order[...] = jnp.zeros_like(order)
    sums[...] = jnp.zeros_like(sums)
    by_lane = indices(BLOCK, LINE)
    by_block = indices(SORTED, LINE)
    wide = LINE // LANES

    @pl.loop(0, DEVICES * RANKS // LINE, unroll=2)
    def _(step):
        fact = [lines(held.at[i], step * wide, wide) for i in range(10)]
        order[...] += product(spread(by_block, fact[8], fact[:8]), one_hot(by_lane, fact[9]))

    by_row = indices(BUCKET, BLOCK)
    by_column = indices(LANES, BLOCK)

    @pl.loop(0, steps_of(starts))
    def _(step):
        for i in range(TOGETHER):
            block = step * TOGETHER + i
            fact = [order[pl.ds(part * SORTED + block, 1), :] for part in range(8)]
            bucket = bucket_of(block, starts)
            sums[bucket] += product(one_hot(by_row, fact[6]), spread(by_column, fact[7], fact[:6]))

    for part in range(3):
        high = slice(2 * part * LANES, (2 * part + 1) * LANES)
        low = slice((2 * part + 1) * LANES, (2 * part + 2) * LANES)
        for band in range(ROWS // TILE):
            rows = slice(band * TILE, (band + 1) * TILE)
            for block in range(TILES):
                first = (band * TILES + block) * TILE
                bucket, first = first // BUCKET, first % BUCKET
                columns = slice(block * LANES, (block + 1) * LANES)
                out[part, rows, columns] = stepped_ref[part, rows, columns] + (
                    sums[bucket, first : first + TILE, high]
                    + sums[bucket, first : first + TILE, low]
                )


def add(arrived, stepped):
    return pl.pallas_call(
        add_kernel,
        out_shape=jax.ShapeDtypeStruct((3, ROWS, COLS), F32),
        in_specs=[VMEM] * 2,
        out_specs=VMEM,
        scratch_shapes=[
            pltpu.VMEM((10, DEVICES, RANKS), F32),
            pltpu.VMEM((8 * SORTED, BLOCK), F32),
            pltpu.VMEM((BUCKETS, BUCKET, 6 * LANES), F32),
            pltpu.SMEM((BUCKETS + 1,), I32),
        ],
        compiler_params=params(),
        name="add",
    )(arrived, stepped)


def local(
    les_state,
    les_density,
    far_state,
    far_density,
    face_cell,
    face_area,
    face_owner,
    face_counts,
    face_target,
):
    cell, area, owner, target = (
        array.reshape(FACE_ROWS, LANES) for array in (face_cell, face_area, face_owner, face_target)
    )
    order, starts, targets = plan(face_counts, owner, cell, area, target)
    les_final, total, stepped = fields(les_state[0], les_density[0], far_state[0], far_density[0])
    ready = pick(total.reshape(3, CELL_ROWS, LANES), order, starts, targets)
    arrived = exchange(ready.reshape(DEVICES, 4, LANES))
    far_final = add(arrived.reshape(4 * DEVICES, LANES), stepped)
    return les_final[None], far_final[None]


def solution(mesh):
    field = P("sec", None, "dom", None)
    density = P("sec", "dom", None)
    faces = P(("sec", "dom"))
    return jax.shard_map(
        local,
        mesh=mesh,
        in_specs=(field, density, field, density) + (faces,) * 5,
        out_specs=(field, field),
        check_vma=False,
    )
```

```python
import jax
import jax.numpy as jnp
from jax import lax
from jax.experimental import pallas as pl
from jax.experimental.pallas import tpu as pltpu
from jax.sharding import PartitionSpec as P

SUBSTEPS = 5
UNROLL = {12: 4, 10: 5}
TIME_STEP = 0.1
LES_STIFF = 1.0
FAR_STIFF = 1.0
FILTER_WEIGHT = 0.5
MEAN_FLOW = 0.3

LANES = 128
TILE = 8
ROWS = 16
COLS = 8192
TILES = COLS // LANES
REGS = TILES // TILE
FACES = 8192
FACE_ROWS = FACES // LANES
DEVICES = 128
RANKS = 128
CELL_ROWS = ROWS * COLS // LANES

MESH = pl.DeviceIdType.MESH
VMEM = pl.BlockSpec(memory_space=pltpu.VMEM)
SMEM = pl.BlockSpec(memory_space=pltpu.SMEM)
F32 = jnp.float32
BF16 = jnp.bfloat16
I32 = jnp.int32


def params(**more):
    return pltpu.CompilerParams(vmem_limit_bytes=56 * 1024 * 1024, **more)


def rows_from_tiles(load, flat, store, rows8):
    for block in range(TILES):
        flat[block * TILE : (block + 1) * TILE, :] = load(block)
    for row in range(TILE):
        for reg in range(REGS):
            store(rows8 * TILE + row, reg, flat[pl.ds(TILE * reg + row, TILE, stride=TILES), :])


def tiles_from_rows(load, flat, store, rows8):
    for row in range(TILE):
        for reg in range(REGS):
            flat[pl.ds(TILE * reg + row, TILE, stride=TILES), :] = load(rows8 * TILE + row, reg)
    for block in range(TILES):
        store(block, flat[block * TILE : (block + 1) * TILE, :])


def shifted(row, by, lane):
    if by > 0:
        turned = pltpu.roll(row, LANES - by, 1)
        crossed = jnp.concatenate([turned[TILE:], pltpu.roll(turned[:TILE], TILE - 1, 0)], axis=0)
        return jnp.where(lane >= LANES - by, crossed, turned)
    turned = pltpu.roll(row, -by, 1)
    crossed = jnp.concatenate(
        [pltpu.roll(turned[TILES - TILE :], 1, 0), turned[: TILES - TILE]], axis=0
    )
    return jnp.where(lane < -by, crossed, turned)


def difference(far_left, left, right, far_right):
    return 8.0 * (right - left) - (far_right - far_left)


def across(row, lane):
    return difference(
        shifted(row, -2, lane), shifted(row, -1, lane), shifted(row, 1, lane), shifted(row, 2, lane)
    )


def fields_kernel(
    les_ref,
    les_density_ref,
    far_ref,
    far_density_ref,
    les_out,
    total_out,
    stepped_out,
    state,
    advanced,
    inverse,
    far,
    far_inverse,
    flat,
    send_sem,
    recv_sem,
    inverse_send,
    inverse_recv,
    far_send,
    far_recv,
):
    dom = lax.axis_index("dom")
    doms = lax.axis_size("dom")
    has_up = dom > 0
    has_down = dom < doms - 1
    up = lax.rem(dom + doms - 1, doms)
    down = lax.rem(dom + 1, doms)
    lane = lax.broadcasted_iota(I32, (TILES, LANES), 1)
    step = TIME_STEP / 12.0

    barrier = pltpu.get_barrier_semaphore()

    @pl.when(has_up)
    def _():
        pl.semaphore_signal(barrier, inc=1, device_id={"dom": up}, device_id_type=MESH)

    @pl.when(has_down)
    def _():
        pl.semaphore_signal(barrier, inc=1, device_id={"dom": down}, device_id_type=MESH)

    def remote(ref, first, count, landing, sems, where):
        return pltpu.make_async_remote_copy(
            src_ref=ref.at[pl.ds(first, count)],
            dst_ref=ref.at[pl.ds(landing, count)],
            send_sem=sems[0],
            recv_sem=sems[1],
            device_id={"dom": where},
            device_id_type=MESH,
        )

    def up_copy(number):
        sems = (send_sem.at[number, 0], recv_sem.at[number, 0])
        near = number == 0
        first, landing = (6, ROWS + 6) if near else (9, ROWS + 9)
        return remote(state.at[0 if near else number - 1], first, 3, landing, sems, up)

    def down_copy(number):
        sems = (send_sem.at[number, 1], recv_sem.at[number, 1])
        near = number == 0
        first, landing = (ROWS + 3, 3) if near else (ROWS, 0)
        return remote(state.at[0 if near else number - 1], first, 3, landing, sems, down)

    def inverse_up():
        return remote(inverse, 4, 4, ROWS + 4, (inverse_send.at[0], inverse_recv.at[0]), up)

    def inverse_down():
        return remote(inverse, ROWS, 4, 0, (inverse_send.at[1], inverse_recv.at[1]), down)

    def far_up():
        return remote(far, 2, 2, ROWS + 2, (far_send.at[0], far_recv.at[0]), up)

    def far_down():
        return remote(far, ROWS, 2, 0, (far_send.at[1], far_recv.at[1]), down)

    @pl.when(jnp.logical_not(has_up))
    def _():
        for sub in range(SUBSTEPS):
            state[sub, 0:6] = jnp.zeros((6, 3, TILES, LANES), F32)
        advanced[0:4] = jnp.zeros((4, 3, TILES, LANES), F32)
        far[0:2] = jnp.zeros((2, 3, TILES, LANES), F32)

    @pl.when(jnp.logical_not(has_down))
    def _():
        for sub in range(SUBSTEPS):
            state[sub, ROWS + 6 :] = jnp.zeros((6, 3, TILES, LANES), F32)
        advanced[ROWS + 4 :] = jnp.zeros((4, 3, TILES, LANES), F32)
        far[ROWS + 2 : ROWS + 4] = jnp.zeros((2, 3, TILES, LANES), F32)

    def convert_state(source, target, offset):
        @pl.loop(0, 6)
        def _(index):
            part, rows8 = index // 2, index % 2

            def load(block):
                return source[part, pl.ds(rows8 * TILE, TILE), block * LANES : (block + 1) * LANES]

            def store(row, reg, value):
                target[offset + row, part, reg * TILE : (reg + 1) * TILE, :] = value

            rows_from_tiles(load, flat, store, rows8)

    def convert_density(source, target, offset):
        @pl.loop(0, 2)
        def _(rows8):
            def load(block):
                return 1.0 / source[pl.ds(rows8 * TILE, TILE), block * LANES : (block + 1) * LANES]

            def store(row, reg, value):
                target[offset + row, reg * TILE : (reg + 1) * TILE, :] = value

            rows_from_tiles(load, flat, store, rows8)

    def advance(sub, row):
        base = row + 6
        u, v, p = (state[sub, base, part] for part in range(3))
        dx = [
            difference(*(state[sub, base + by, part] for by in (-2, -1, 1, 2)))
            for part in range(3)
        ]
        dy = [across(field, lane) for field in (u, v, p)]
        inv = inverse[row + 4]
        rate_u = u * dx[0] + v * dy[0] + inv * dx[2]
        rate_v = u * dx[1] + v * dy[1] + inv * dy[2]
        rate_p = u * dx[2] + v * dy[2] + LES_STIFF * (dx[0] + dy[1])
        return u - step * rate_u, v - step * rate_v, p - step * rate_p

    def put_advanced(row, fields):
        for part in range(3):
            advanced[row + 4, part] = fields[part]

    def advance_rows(sub, low, high):
        loop(low, high, lambda row: put_advanced(row, advance(sub, row)))

    def smooth(sub, row, own):
        for part in range(3):
            centre = advanced[row + 4, part]
            lateral = advanced[row + 3, part] + advanced[row + 5, part]
            sides = shifted(centre, 1, lane) + shifted(centre, -1, lane)
            value = (1.0 - FILTER_WEIGHT) * centre + FILTER_WEIGHT / 4.0 * (lateral + sides)
            state[sub + 1, row + 6, part] = value
            if own:
                if sub == 0:
                    total_out[part, row] = value
                else:
                    total_out[part, row] += value

    def smooth_rows(sub, low, high, own=True):
        loop(low, high, lambda row: smooth(sub, row, own))

    def far_row(row):
        base = row + 2
        u, v, p = (far[base, part] for part in range(3))
        dx = [
            difference(*(far[base + by, part] for by in (-2, -1, 1, 2))) for part in range(3)
        ]
        inv = far_inverse[row]
        dy_v, dy_p = across(v, lane), across(p, lane)
        far[base + ROWS + 4, 0] = u - step * (MEAN_FLOW * dx[0] + inv * dx[2])
        far[base + ROWS + 4, 1] = v - step * (MEAN_FLOW * dx[1] + inv * dy_p)
        far[base + ROWS + 4, 2] = p - step * (MEAN_FLOW * dx[2] + FAR_STIFF * (dx[0] + dy_v))

    def loop(low, high, body):
        @pl.loop(low, high, unroll=UNROLL.get(high - low, high - low))
        def _(row):
            body(row)

    def write_tiles(source, target):
        @pl.loop(0, 6)
        def _(index):
            part, rows8 = index // 2, index % 2

            def load(row, reg):
                return source(row, part, reg)

            def store(block, value):
                target[part, pl.ds(rows8 * TILE, TILE), block * LANES : (block + 1) * LANES] = value

            tiles_from_rows(load, flat, store, rows8)

    convert_state(les_ref, state.at[0], 6)
    convert_density(les_density_ref, inverse, 4)

    pl.semaphore_wait(barrier, jnp.where(has_up, 1, 0) + jnp.where(has_down, 1, 0))

    @pl.when(has_up)
    def _():
        up_copy(0).start()
        inverse_up().start()
        up_copy(1).start()

    @pl.when(has_down)
    def _():
        down_copy(0).start()
        inverse_down().start()
        down_copy(1).start()

    for sub in range(SUBSTEPS):
        advance_rows(sub, 2, ROWS - 2)
        smooth_rows(sub, 3, ROWS - 3)

        if sub + 2 < SUBSTEPS:

            @pl.when(has_up)
            def _():
                up_copy(sub + 2).start()

            @pl.when(has_down)
            def _():
                down_copy(sub + 2).start()

        if sub + 2 == SUBSTEPS:

            @pl.when(has_up)
            def _():
                far_up().start()

            @pl.when(has_down)
            def _():
                far_down().start()

        if sub == 0:
            convert_state(far_ref, far, 2)
            convert_density(far_density_ref, far_inverse, 0)
        if sub == 1:
            loop(2, ROWS - 2, far_row)

        @pl.when(has_up)
        def _():
            if sub == 0:
                down_copy(0).wait_recv()
                inverse_down().wait_recv()
            put_advanced(-1, advance(sub, -1))

        @pl.when(has_down)
        def _():
            if sub == 0:
                up_copy(0).wait_recv()
                inverse_up().wait_recv()
            put_advanced(ROWS, advance(sub, ROWS))

        advance_rows(sub, 0, 2)
        advance_rows(sub, ROWS - 2, ROWS)
        smooth_rows(sub, 0, 3)
        smooth_rows(sub, ROWS - 3, ROWS)

        if sub + 1 < SUBSTEPS:

            @pl.when(has_up)
            def _():
                down_copy(sub + 1).wait_recv()
                advance_rows(sub, -4, -1)
                smooth_rows(sub, -3, 0, own=False)

            @pl.when(has_down)
            def _():
                up_copy(sub + 1).wait_recv()
                advance_rows(sub, ROWS + 1, ROWS + 4)
                smooth_rows(sub, ROWS, ROWS + 3, own=False)

    write_tiles(
        lambda row, part, reg: state[SUBSTEPS, row + 6, part, reg * TILE : (reg + 1) * TILE, :],
        les_out,
    )

    @pl.when(has_up)
    def _():
        far_down().wait_recv()

    @pl.when(has_down)
    def _():
        far_up().wait_recv()

    loop(0, 2, far_row)
    loop(ROWS - 2, ROWS, far_row)
    write_tiles(
        lambda row, part, reg: far[row + ROWS + 6, part, reg * TILE : (reg + 1) * TILE, :],
        stepped_out,
    )

    @pl.when(has_up)
    def _():
        for sub in range(SUBSTEPS):
            up_copy(sub).wait_send()
        inverse_up().wait_send()
        far_up().wait_send()

    @pl.when(has_down)
    def _():
        for sub in range(SUBSTEPS):
            down_copy(sub).wait_send()
        inverse_down().wait_send()
        far_down().wait_send()


def fields(les_state, les_density, far_state, far_density):
    block = jax.ShapeDtypeStruct((3, ROWS, COLS), F32)
    return pl.pallas_call(
        fields_kernel,
        out_shape=(block, jax.ShapeDtypeStruct((3, ROWS, TILES, LANES), F32), block),
        in_specs=[VMEM] * 4,
        out_specs=(VMEM,) * 3,
        scratch_shapes=[
            pltpu.VMEM((SUBSTEPS + 1, ROWS + 12, 3, TILES, LANES), F32),
            pltpu.VMEM((ROWS + 8, 3, TILES, LANES), F32),
            pltpu.VMEM((ROWS + 8, TILES, LANES), F32),
            pltpu.VMEM((2 * ROWS + 6, 3, TILES, LANES), F32),
            pltpu.VMEM((ROWS, TILES, LANES), F32),
            pltpu.VMEM((TILES * TILE, LANES), F32),
            pltpu.SemaphoreType.DMA((SUBSTEPS, 2)),
            pltpu.SemaphoreType.DMA((SUBSTEPS, 2)),
            pltpu.SemaphoreType.DMA((2,)),
            pltpu.SemaphoreType.DMA((2,)),
            pltpu.SemaphoreType.DMA((2,)),
            pltpu.SemaphoreType.DMA((2,)),
        ],
        compiler_params=params(collective_id=0, has_side_effects=True),
        name="fields",
    )(les_state, les_density, far_state, far_density)


RANK_BLOCK = 256
BUCKETS = 4
BUCKET = CELL_ROWS // BUCKETS
BLOCK = 256
LINE = 512
TOGETHER = 4
PLANNED = 48
SORTED = 80


def halves(values):
    high = values.astype(BF16).astype(F32)
    return high, values - high


def indices(rows, columns):
    return lax.broadcasted_iota(I32, (rows, columns), 0).astype(F32).astype(BF16)


def one_hot(index, line):
    return jnp.where(index == line.astype(BF16), jnp.ones((), BF16), jnp.zeros((), BF16))


def spread(index, line, parts):
    here = index == line.astype(BF16)
    return jnp.concatenate(
        [jnp.where(here, part.astype(BF16), jnp.zeros((), BF16)) for part in parts], axis=0
    )


def product(left, right):
    return lax.dot_general(left, right, (((1,), (1,)), ((), ())), preferred_element_type=F32)


def lines(ref, first, count):
    return jnp.concatenate([ref[pl.ds(first + i, 1), :] for i in range(count)], axis=1)


def bucket_places(bucket, rows, starts_ref):
    before = lax.broadcasted_iota(I32, (LANES, 2 * LANES), 0)
    after = lax.broadcasted_iota(I32, (LANES, 2 * LANES), 1)
    weights = jnp.where((before < after) | (after >= LANES), 1.0, 0.0).astype(BF16)
    below = lax.broadcasted_iota(I32, (rows, rows), 0) > lax.broadcasted_iota(I32, (rows, rows), 1)
    below = jnp.where(below, 1.0, 0.0).astype(BF16)
    place = jnp.full((rows, LANES), -1.0, F32)
    base = jnp.zeros((1, LANES), F32)
    for b in range(BUCKETS):
        starts_ref[b] = jnp.max(base).astype(I32)
        here = bucket == b
        counted = jnp.dot(
            jnp.where(here, 1.0, 0.0).astype(BF16), weights, preferred_element_type=F32
        )
        totals = counted[:, LANES:]
        offset = jnp.dot(below, totals.astype(BF16), preferred_element_type=F32)
        place = jnp.where(here, counted[:, :LANES] + offset + base * float(BLOCK), place)
        total = offset[rows - 1 :] + totals[rows - 1 :]
        base = base + jnp.floor((total + (BLOCK - 1.0)) * (1.0 / BLOCK))
    starts_ref[BUCKETS] = jnp.max(base).astype(I32)
    return place


def block_and_lane(place):
    block = jnp.floor(place * (1.0 / BLOCK))
    return block, place - block * float(BLOCK)


def plan_kernel(
    count_ref, owner_ref, cell_ref, area_ref, target_ref, order, starts, targets, facts, grid
):
    live = count_ref[0]
    owners = lax.broadcasted_iota(I32, (DEVICES, RANK_BLOCK), 0)
    before = lax.broadcasted_iota(I32, (RANK_BLOCK, RANK_BLOCK), 0)
    after = lax.broadcasted_iota(I32, (RANK_BLOCK, RANK_BLOCK), 1)
    weights = jnp.concatenate(
        [
            jnp.where(before < after, 1.0, 0.0).astype(BF16),
            jnp.ones((RANK_BLOCK, RANK_BLOCK), BF16),
        ],
        axis=1,
    )
    face = lax.broadcasted_iota(I32, (1, RANK_BLOCK), 1)
    base = jnp.zeros((DEVICES, RANK_BLOCK), F32)
    wide = RANK_BLOCK // LANES
    for block in range(FACES // RANK_BLOCK):
        named = lines(owner_ref, block * wide, wide)
        named = jnp.where(face + block * RANK_BLOCK < live, named, -1)
        hits = jnp.where(owners == named, 1.0, 0.0)
        counted = jnp.dot(hits.astype(BF16), weights, preferred_element_type=F32)
        rank = jnp.sum(hits * (counted[:, :RANK_BLOCK] + base), axis=0, keepdims=True)
        base = base + counted[:, RANK_BLOCK:]
        for i in range(wide):
            facts[3, block * wide + i : block * wide + i + 1, :] = rank[
                :, i * LANES : (i + 1) * LANES
            ]

    cell = cell_ref[...]
    target = target_ref[...] + 1
    row, column = cell >> 13, cell & (COLS - 1)
    cell_row = row * TILES + ((column >> 7) & 7) * TILE + (column >> 10)
    number = (
        lax.broadcasted_iota(I32, (FACE_ROWS, LANES), 0) * LANES
        + lax.broadcasted_iota(I32, (FACE_ROWS, LANES), 1)
    )
    bucket = jnp.where(number < live, cell_row >> 8, -1)
    facts[0] = (cell_row & (BUCKET - 1)).astype(F32)
    facts[1] = (column & (LANES - 1)).astype(F32)
    facts[2] = jnp.where(number < live, owner_ref[...], -1).astype(F32)
    facts[4], facts[5] = halves(area_ref[...] * (1.0 / SUBSTEPS))
    for i in range(3):
        facts[6 + i] = ((target >> (7 * i)) & (LANES - 1)).astype(F32)
    facts[9], facts[10] = block_and_lane(bucket_places(bucket, FACE_ROWS, starts))

    order[...] = jnp.zeros_like(order)
    grid[...] = jnp.zeros_like(grid)
    by_lane = indices(BLOCK, LINE)
    by_block = indices(PLANNED, LINE)
    by_device = indices(DEVICES, LINE)
    wide = LINE // LANES

    @pl.loop(0, FACES // LINE, unroll=2)
    def _(step):
        fact = [lines(facts.at[i], step * wide, wide) for i in range(11)]
        order[...] += product(spread(by_block, fact[9], fact[:6]), one_hot(by_lane, fact[10]))
        grid[...] += product(spread(by_device, fact[2], fact[6:9]), one_hot(by_device, fact[3]))

    targets[...] = (
        grid[:DEVICES]
        + grid[DEVICES : 2 * DEVICES] * float(LANES)
        + grid[2 * DEVICES :] * float(LANES * LANES)
    )


def plan(counts, owner, cell, area, target):
    return pl.pallas_call(
        plan_kernel,
        out_shape=(
            jax.ShapeDtypeStruct((6 * PLANNED, BLOCK), F32),
            jax.ShapeDtypeStruct((BUCKETS + 1,), I32),
            jax.ShapeDtypeStruct((DEVICES, RANKS), F32),
        ),
        in_specs=[SMEM] + [VMEM] * 4,
        out_specs=(VMEM, SMEM, VMEM),
        scratch_shapes=[
            pltpu.VMEM((11, FACE_ROWS, LANES), F32),
            pltpu.VMEM((3 * DEVICES, RANKS), F32),
        ],
        compiler_params=params(),
        name="plan",
    )(counts, owner, cell, area, target)


def bucket_of(block, starts_ref):
    bucket = 0
    for b in range(1, BUCKETS):
        bucket = bucket + jnp.where(block >= starts_ref[b], 1, 0)
    return bucket


def steps_of(starts_ref):
    return (starts_ref[BUCKETS] + TOGETHER - 1) // TOGETHER


def pick_kernel(total_ref, order_ref, starts_ref, targets_ref, out, turned, slots):
    for part in range(3):
        for block in range(CELL_ROWS // LANES):
            high, low = halves(total_ref[part, block * LANES : (block + 1) * LANES, :].T)
            bucket = block * LANES // BUCKET
            columns = slice(block * LANES % BUCKET, block * LANES % BUCKET + LANES)
            turned[bucket, 2 * part * LANES : (2 * part + 1) * LANES, columns] = high.astype(BF16)
            turned[bucket, (2 * part + 1) * LANES : (2 * part + 2) * LANES, columns] = low.astype(
                BF16
            )
    slots[...] = jnp.zeros_like(slots)
    by_row = indices(BUCKET, BLOCK)
    lane = lax.broadcasted_iota(I32, (LANES, BLOCK), 0).astype(F32)
    by_device = indices(DEVICES, BLOCK * TOGETHER)

    @pl.loop(0, steps_of(starts_ref))
    def _(step):
        surface = []
        placed = []
        for i in range(TOGETHER):
            block = step * TOGETHER + i
            row, where, owner, rank, high, low = (
                order_ref[pl.ds(part * PLANNED + block, 1), :] for part in range(6)
            )
            found = jnp.dot(
                turned[bucket_of(block, starts_ref)],
                one_hot(by_row, row),
                preferred_element_type=F32,
            )
            is_lane = lane == where
            parts = []
            for part in range(3):
                both = (
                    found[2 * part * LANES : (2 * part + 1) * LANES]
                    + found[(2 * part + 1) * LANES : (2 * part + 2) * LANES]
                )
                value = jnp.sum(jnp.where(is_lane, both, 0.0), axis=0, keepdims=True)
                parts.extend(halves(value * (high + low)))
            surface.append(parts)
            placed.append((owner, rank))
        joined = [jnp.concatenate(part, axis=1) for part in zip(*surface)]
        owner, rank = (jnp.concatenate(part, axis=1) for part in zip(*placed))
        slots[...] += product(spread(by_device, owner, joined), one_hot(by_device, rank))

    pieces = [slots[i * DEVICES : (i + 1) * DEVICES] for i in range(6)]
    for part in range(3):
        out[pl.ds(part, DEVICES, stride=4), :] = pieces[2 * part] + pieces[2 * part + 1]
    out[pl.ds(3, DEVICES, stride=4), :] = targets_ref[...]


def pick(total, order, starts, targets):
    return pl.pallas_call(
        pick_kernel,
        out_shape=jax.ShapeDtypeStruct((4 * DEVICES, LANES), F32),
        in_specs=[VMEM, VMEM, SMEM, VMEM],
        out_specs=VMEM,
        scratch_shapes=[
            pltpu.VMEM((BUCKETS, 6 * LANES, BUCKET), BF16),
            pltpu.VMEM((6 * DEVICES, RANKS), F32),
        ],
        compiler_params=params(),
        name="pick",
    )(total, order, starts, targets)


def exchange_kernel(ready, arrived, local_sem, send_sem, recv_sem):
    secs, doms = lax.axis_size("sec"), lax.axis_size("dom")
    devices = secs * doms
    me = lax.axis_index("sec") * doms + lax.axis_index("dom")
    barrier = pltpu.get_barrier_semaphore()

    def place(offset):
        other = lax.rem(me + offset, devices)
        return other, {"sec": other // doms, "dom": lax.rem(other, doms)}

    @pl.loop(1, devices)
    def _(offset):
        pl.semaphore_signal(barrier, inc=1, device_id=place(offset)[1], device_id_type=MESH)

    own = pltpu.make_async_copy(ready.at[me], arrived.at[me], local_sem)
    own.start()
    pl.semaphore_wait(barrier, devices - 1)

    @pl.loop(1, devices)
    def _(offset):
        other, where = place(offset)
        pltpu.make_async_remote_copy(
            src_ref=ready.at[other],
            dst_ref=arrived.at[me],
            send_sem=send_sem,
            recv_sem=recv_sem,
            device_id=where,
            device_id_type=MESH,
        ).start()

    own.wait()
    all_but_one = pl.ds(0, devices - 1)
    pltpu.make_async_copy(arrived.at[all_but_one], arrived.at[all_but_one], recv_sem).wait()
    pltpu.make_async_copy(ready.at[all_but_one], ready.at[all_but_one], send_sem).wait()


def exchange(ready):
    return pl.pallas_call(
        exchange_kernel,
        out_shape=jax.ShapeDtypeStruct(ready.shape, F32),
        in_specs=[VMEM],
        out_specs=VMEM,
        scratch_shapes=[pltpu.SemaphoreType.DMA] * 3,
        compiler_params=params(collective_id=1, has_side_effects=True),
        name="exchange",
    )(ready)


def add_kernel(arrived_ref, stepped_ref, out, held, order, sums, starts):
    for part in range(3):
        high, low = halves(arrived_ref[pl.ds(part, DEVICES, stride=4), :])
        held[2 * part] = high
        held[2 * part + 1] = low
    target = arrived_ref[pl.ds(3, DEVICES, stride=4), :].astype(I32) - 1
    row, column = target >> 13, target & (COLS - 1)
    cell_row = ((row >> 3) * TILES + (column >> 7)) * TILE + (row & 7)
    bucket = jnp.where(target >= 0, cell_row >> 8, -1)
    held[6] = (cell_row & (BUCKET - 1)).astype(F32)
    held[7] = (column & (LANES - 1)).astype(F32)
    held[8], held[9] = block_and_lane(bucket_places(bucket, DEVICES, starts))
    order[...] = jnp.zeros_like(order)
    sums[...] = jnp.zeros_like(sums)
    by_lane = indices(BLOCK, LINE)
    by_block = indices(SORTED, LINE)
    wide = LINE // LANES

    @pl.loop(0, DEVICES * RANKS // LINE, unroll=2)
    def _(step):
        fact = [lines(held.at[i], step * wide, wide) for i in range(10)]
        order[...] += product(spread(by_block, fact[8], fact[:8]), one_hot(by_lane, fact[9]))

    by_row = indices(BUCKET, BLOCK)
    by_column = indices(LANES, BLOCK)

    @pl.loop(0, steps_of(starts))
    def _(step):
        for i in range(TOGETHER):
            block = step * TOGETHER + i
            fact = [order[pl.ds(part * SORTED + block, 1), :] for part in range(8)]
            bucket = bucket_of(block, starts)
            sums[bucket] += product(one_hot(by_row, fact[6]), spread(by_column, fact[7], fact[:6]))

    for part in range(3):
        high = slice(2 * part * LANES, (2 * part + 1) * LANES)
        low = slice((2 * part + 1) * LANES, (2 * part + 2) * LANES)
        for band in range(ROWS // TILE):
            rows = slice(band * TILE, (band + 1) * TILE)
            for block in range(TILES):
                first = (band * TILES + block) * TILE
                bucket, first = first // BUCKET, first % BUCKET
                columns = slice(block * LANES, (block + 1) * LANES)
                out[part, rows, columns] = stepped_ref[part, rows, columns] + (
                    sums[bucket, first : first + TILE, high]
                    + sums[bucket, first : first + TILE, low]
                )


def add(arrived, stepped):
    return pl.pallas_call(
        add_kernel,
        out_shape=jax.ShapeDtypeStruct((3, ROWS, COLS), F32),
        in_specs=[VMEM] * 2,
        out_specs=VMEM,
        scratch_shapes=[
            pltpu.VMEM((10, DEVICES, RANKS), F32),
            pltpu.VMEM((8 * SORTED, BLOCK), F32),
            pltpu.VMEM((BUCKETS, BUCKET, 6 * LANES), F32),
            pltpu.SMEM((BUCKETS + 1,), I32),
        ],
        compiler_params=params(),
        name="add",
    )(arrived, stepped)


def local(
    les_state,
    les_density,
    far_state,
    far_density,
    face_cell,
    face_area,
    face_owner,
    face_counts,
    face_target,
):
    cell, area, owner, target = (
        array.reshape(FACE_ROWS, LANES) for array in (face_cell, face_area, face_owner, face_target)
    )
    order, starts, targets = plan(face_counts, owner, cell, area, target)
    les_final, total, stepped = fields(les_state[0], les_density[0], far_state[0], far_density[0])
    ready = pick(total.reshape(3, CELL_ROWS, LANES), order, starts, targets)
    arrived = exchange(ready.reshape(DEVICES, 4, LANES))
    far_final = add(arrived.reshape(4 * DEVICES, LANES), stepped)
    return les_final[None], far_final[None]


def solution(mesh):
    field = P("sec", None, "dom", None)
    density = P("sec", "dom", None)
    faces = P(("sec", "dom"))
    return jax.shard_map(
        local,
        mesh=mesh,
        in_specs=(field, density, field, density) + (faces,) * 5,
        out_specs=(field, field),
        check_vma=False,
    )
```

```python
import jax
import jax.numpy as jnp
from jax import lax
from jax.experimental import pallas as pl
from jax.experimental.pallas import tpu as pltpu
from jax.sharding import PartitionSpec as P

SUBSTEPS = 5
UNROLL = {12: 4, 10: 5}
TIME_STEP = 0.1
LES_STIFF = 1.0
FAR_STIFF = 1.0
FILTER_WEIGHT = 0.5
MEAN_FLOW = 0.3

LANES = 128
TILE = 8
ROWS = 16
COLS = 8192
TILES = COLS // LANES
REGS = TILES // TILE
FACES = 8192
FACE_ROWS = FACES // LANES
DEVICES = 128
RANKS = 128
CELL_ROWS = ROWS * COLS // LANES

MESH = pl.DeviceIdType.MESH
VMEM = pl.BlockSpec(memory_space=pltpu.VMEM)
SMEM = pl.BlockSpec(memory_space=pltpu.SMEM)
F32 = jnp.float32
BF16 = jnp.bfloat16
I32 = jnp.int32


def params(**more):
    return pltpu.CompilerParams(vmem_limit_bytes=56 * 1024 * 1024, **more)


def rows_from_tiles(load, flat, store, rows8):
    for block in range(TILES):
        flat[block * TILE : (block + 1) * TILE, :] = load(block)
    for row in range(TILE):
        for reg in range(REGS):
            store(rows8 * TILE + row, reg, flat[pl.ds(TILE * reg + row, TILE, stride=TILES), :])


def tiles_from_rows(load, flat, store, rows8):
    for row in range(TILE):
        for reg in range(REGS):
            flat[pl.ds(TILE * reg + row, TILE, stride=TILES), :] = load(rows8 * TILE + row, reg)
    for block in range(TILES):
        store(block, flat[block * TILE : (block + 1) * TILE, :])


def shifted(row, by, lane):
    if by > 0:
        turned = pltpu.roll(row, LANES - by, 1)
        crossed = jnp.concatenate([turned[TILE:], pltpu.roll(turned[:TILE], TILE - 1, 0)], axis=0)
        return jnp.where(lane >= LANES - by, crossed, turned)
    turned = pltpu.roll(row, -by, 1)
    crossed = jnp.concatenate(
        [pltpu.roll(turned[TILES - TILE :], 1, 0), turned[: TILES - TILE]], axis=0
    )
    return jnp.where(lane < -by, crossed, turned)


def difference(far_left, left, right, far_right):
    return 8.0 * (right - left) - (far_right - far_left)


def across(row, lane):
    return difference(
        shifted(row, -2, lane), shifted(row, -1, lane), shifted(row, 1, lane), shifted(row, 2, lane)
    )


RANK_BLOCK = 256
BUCKETS = 4
BUCKET = CELL_ROWS // BUCKETS
BLOCK = 256
LINE = 512
TOGETHER = 4
HALF = DEVICES // 2
PLANNED = 48
SORTED = 80


def halves(values):
    high = values.astype(BF16).astype(F32)
    return high, values - high


def indices(rows, columns):
    return lax.broadcasted_iota(I32, (rows, columns), 0).astype(F32).astype(BF16)


def one_hot(index, line):
    return jnp.where(index == line.astype(BF16), jnp.ones((), BF16), jnp.zeros((), BF16))


def spread(index, line, parts):
    here = index == line.astype(BF16)
    return jnp.concatenate(
        [jnp.where(here, part.astype(BF16), jnp.zeros((), BF16)) for part in parts], axis=0
    )


def product(left, right):
    return lax.dot_general(left, right, (((1,), (1,)), ((), ())), preferred_element_type=F32)


def lines(ref, first, count):
    return jnp.concatenate([ref[pl.ds(first + i, 1), :] for i in range(count)], axis=1)


def bucket_places(bucket, rows, starts_ref):
    before = lax.broadcasted_iota(I32, (LANES, 2 * LANES), 0)
    after = lax.broadcasted_iota(I32, (LANES, 2 * LANES), 1)
    weights = jnp.where((before < after) | (after >= LANES), 1.0, 0.0).astype(BF16)
    below = lax.broadcasted_iota(I32, (rows, rows), 0) > lax.broadcasted_iota(I32, (rows, rows), 1)
    below = jnp.where(below, 1.0, 0.0).astype(BF16)
    place = jnp.full((rows, LANES), -1.0, F32)
    base = jnp.zeros((1, LANES), F32)
    for b in range(BUCKETS):
        starts_ref[b] = jnp.max(base).astype(I32)
        here = bucket == b
        counted = jnp.dot(
            jnp.where(here, 1.0, 0.0).astype(BF16), weights, preferred_element_type=F32
        )
        totals = counted[:, LANES:]
        offset = jnp.dot(below, totals.astype(BF16), preferred_element_type=F32)
        place = jnp.where(here, counted[:, :LANES] + offset + base * float(BLOCK), place)
        total = offset[rows - 1 :] + totals[rows - 1 :]
        base = base + jnp.floor((total + (BLOCK - 1.0)) * (1.0 / BLOCK))
    starts_ref[BUCKETS] = jnp.max(base).astype(I32)
    return place


def block_and_lane(place):
    block = jnp.floor(place * (1.0 / BLOCK))
    return block, place - block * float(BLOCK)


def by_owner(halved):
    return jnp.concatenate([halved[:, :RANKS], halved[:, RANKS:]], axis=0)


def bucket_of(block, starts_ref):
    bucket = 0
    for b in range(1, BUCKETS):
        bucket = bucket + jnp.where(block >= starts_ref[b], 1, 0)
    return bucket


def steps_of(starts_ref):
    return (starts_ref[BUCKETS] + TOGETHER - 1) // TOGETHER


def rank_faces(count_ref, owner_ref, facts):
    live = count_ref[0]
    owners = lax.broadcasted_iota(I32, (DEVICES, RANK_BLOCK), 0)
    before = lax.broadcasted_iota(I32, (RANK_BLOCK, RANK_BLOCK), 0)
    after = lax.broadcasted_iota(I32, (RANK_BLOCK, RANK_BLOCK), 1)
    weights = jnp.concatenate(
        [
            jnp.where(before < after, 1.0, 0.0).astype(BF16),
            jnp.ones((RANK_BLOCK, RANK_BLOCK), BF16),
        ],
        axis=1,
    )
    face = lax.broadcasted_iota(I32, (1, RANK_BLOCK), 1)
    base = jnp.zeros((DEVICES, RANK_BLOCK), F32)
    wide = RANK_BLOCK // LANES
    for block in range(FACES // RANK_BLOCK):
        named = lines(owner_ref, block * wide, wide)
        named = jnp.where(face + block * RANK_BLOCK < live, named, -1)
        hits = jnp.where(owners == named, 1.0, 0.0)
        counted = jnp.dot(hits.astype(BF16), weights, preferred_element_type=F32)
        rank = jnp.sum(hits * (counted[:, :RANK_BLOCK] + base), axis=0, keepdims=True)
        base = base + counted[:, RANK_BLOCK:]
        for i in range(wide):
            facts[3, block * wide + i : block * wide + i + 1, :] = rank[
                :, i * LANES : (i + 1) * LANES
            ]


def sort_faces(
    count_ref, owner_ref, cell_ref, area_ref, target_ref, order, starts, targets, facts, grid
):
    live = count_ref[0]
    cell = cell_ref[...]
    target = target_ref[...] + 1
    row, column = cell >> 13, cell & (COLS - 1)
    cell_row = row * TILES + ((column >> 7) & 7) * TILE + (column >> 10)
    number = (
        lax.broadcasted_iota(I32, (FACE_ROWS, LANES), 0) * LANES
        + lax.broadcasted_iota(I32, (FACE_ROWS, LANES), 1)
    )
    bucket = jnp.where(number < live, cell_row >> 8, -1)
    facts[0] = (cell_row & (BUCKET - 1)).astype(F32)
    facts[1] = (column & (LANES - 1)).astype(F32)
    owner = owner_ref[...]
    facts[2] = jnp.where(number < live, owner & (HALF - 1), -1).astype(F32)
    facts[3] = facts[3] + ((owner >> 6) * RANKS).astype(F32)
    facts[4], facts[5] = halves(area_ref[...] * (1.0 / SUBSTEPS))
    for i in range(3):
        facts[6 + i] = ((target >> (7 * i)) & (LANES - 1)).astype(F32)
    facts[9], facts[10] = block_and_lane(bucket_places(bucket, FACE_ROWS, starts))

    order[...] = jnp.zeros_like(order)
    grid[...] = jnp.zeros_like(grid)
    by_lane = indices(BLOCK, LINE)
    by_block = indices(PLANNED, LINE)
    by_half = indices(HALF, LINE)
    wide = LINE // LANES

    @pl.loop(0, FACES // LINE, unroll=2)
    def _(step):
        fact = [lines(facts.at[i], step * wide, wide) for i in range(11)]
        order[...] += product(spread(by_block, fact[9], fact[:6]), one_hot(by_lane, fact[10]))
        grid[...] += product(spread(by_half, fact[2], fact[6:9]), one_hot(by_lane, fact[3]))

    targets[...] = by_owner(
        grid[:HALF]
        + grid[HALF : 2 * HALF] * float(LANES)
        + grid[2 * HALF :] * float(LANES * LANES)
    )


def pick_faces(total_ref, order_ref, starts_ref, targets_ref, ready, turned, slots):
    for part in range(3):
        for block in range(CELL_ROWS // LANES):
            high, low = halves(total_ref[part, 2 * block : 2 * block + 2].reshape(LANES, LANES).T)
            bucket = block * LANES // BUCKET
            columns = slice(block * LANES % BUCKET, block * LANES % BUCKET + LANES)
            turned[bucket, 2 * part * LANES : (2 * part + 1) * LANES, columns] = high.astype(BF16)
            turned[bucket, (2 * part + 1) * LANES : (2 * part + 2) * LANES, columns] = low.astype(
                BF16
            )
    slots[...] = jnp.zeros_like(slots)
    by_row = indices(BUCKET, BLOCK)
    lane = lax.broadcasted_iota(I32, (LANES, BLOCK), 0).astype(F32)
    by_half = indices(HALF, BLOCK * TOGETHER)
    by_rank = indices(2 * RANKS, BLOCK * TOGETHER)

    @pl.loop(0, (FACES // BLOCK + BUCKETS) // TOGETHER)
    def _(step):
        surface = []
        placed = []
        for i in range(TOGETHER):
            block = step * TOGETHER + i
            row, where, owner, rank, high, low = (
                order_ref[pl.ds(part * PLANNED + block, 1), :] for part in range(6)
            )
            found = jnp.dot(
                turned[bucket_of(block, starts_ref)],
                one_hot(by_row, row),
                preferred_element_type=F32,
            )
            is_lane = lane == where
            parts = []
            for part in range(3):
                both = (
                    found[2 * part * LANES : (2 * part + 1) * LANES]
                    + found[(2 * part + 1) * LANES : (2 * part + 2) * LANES]
                )
                value = jnp.sum(jnp.where(is_lane, both, 0.0), axis=0, keepdims=True)
                parts.extend(halves(value * (high + low)))
            surface.append(parts)
            placed.append((owner, rank))
        joined = [jnp.concatenate(part, axis=1) for part in zip(*surface)]
        owner, rank = (jnp.concatenate(part, axis=1) for part in zip(*placed))
        slots[...] += product(spread(by_half, owner, joined), one_hot(by_rank, rank))

    for part in range(3):
        first = 2 * part * HALF
        ready[:, part, :] = by_owner(
            slots[first : first + HALF] + slots[first + HALF : first + 2 * HALF]
        )
    ready[:, 3, :] = targets_ref[...]


def fields_kernel(
    les_ref,
    les_density_ref,
    far_ref,
    far_density_ref,
    count_ref,
    owner_ref,
    cell_ref,
    area_ref,
    target_ref,
    les_out,
    stepped_out,
    arrived,
    total_out,
    state,
    advanced,
    inverse,
    far,
    far_inverse,
    flat,
    send_sem,
    recv_sem,
    inverse_send,
    inverse_recv,
    far_send,
    far_recv,
    order,
    starts,
    targets,
    facts,
    grid,
    ready,
    turned,
    slots,
    local_sem,
    faces_send,
    faces_recv,
):
    dom = lax.axis_index("dom")
    doms = lax.axis_size("dom")
    has_up = dom > 0
    has_down = dom < doms - 1
    up = lax.rem(dom + doms - 1, doms)
    down = lax.rem(dom + 1, doms)
    lane = lax.broadcasted_iota(I32, (TILES, LANES), 1)
    step = TIME_STEP / 12.0

    devices = lax.axis_size("sec") * doms
    me = lax.axis_index("sec") * doms + dom
    barrier = pltpu.get_barrier_semaphore()

    def place(offset):
        other = lax.rem(me + offset, devices)
        return other, {"sec": other // doms, "dom": lax.rem(other, doms)}

    @pl.loop(1, devices)
    def _(offset):
        pl.semaphore_signal(barrier, inc=1, device_id=place(offset)[1], device_id_type=MESH)

    def remote(ref, first, count, landing, sems, where):
        return pltpu.make_async_remote_copy(
            src_ref=ref.at[pl.ds(first, count)],
            dst_ref=ref.at[pl.ds(landing, count)],
            send_sem=sems[0],
            recv_sem=sems[1],
            device_id={"dom": where},
            device_id_type=MESH,
        )

    def up_copy(number):
        sems = (send_sem.at[number, 0], recv_sem.at[number, 0])
        near = number == 0
        first, landing = (6, ROWS + 6) if near else (9, ROWS + 9)
        return remote(state.at[0 if near else number - 1], first, 3, landing, sems, up)

    def down_copy(number):
        sems = (send_sem.at[number, 1], recv_sem.at[number, 1])
        near = number == 0
        first, landing = (ROWS + 3, 3) if near else (ROWS, 0)
        return remote(state.at[0 if near else number - 1], first, 3, landing, sems, down)

    def inverse_up():
        return remote(inverse, 4, 4, ROWS + 4, (inverse_send.at[0], inverse_recv.at[0]), up)

    def inverse_down():
        return remote(inverse, ROWS, 4, 0, (inverse_send.at[1], inverse_recv.at[1]), down)

    def far_up():
        return remote(far, 2, 2, ROWS + 2, (far_send.at[0], far_recv.at[0]), up)

    def far_down():
        return remote(far, ROWS, 2, 0, (far_send.at[1], far_recv.at[1]), down)

    @pl.when(jnp.logical_not(has_up))
    def _():
        for sub in range(SUBSTEPS):
            state[sub, 0:6] = jnp.zeros((6, 3, TILES, LANES), F32)
        advanced[0:4] = jnp.zeros((4, 3, TILES, LANES), F32)
        far[0:2] = jnp.zeros((2, 3, TILES, LANES), F32)

    @pl.when(jnp.logical_not(has_down))
    def _():
        for sub in range(SUBSTEPS):
            state[sub, ROWS + 6 :] = jnp.zeros((6, 3, TILES, LANES), F32)
        advanced[ROWS + 4 :] = jnp.zeros((4, 3, TILES, LANES), F32)
        far[ROWS + 2 : ROWS + 4] = jnp.zeros((2, 3, TILES, LANES), F32)

    def convert_state(source, target, offset):
        @pl.loop(0, 6)
        def _(index):
            part, rows8 = index // 2, index % 2

            def load(block):
                return source[part, pl.ds(rows8 * TILE, TILE), block * LANES : (block + 1) * LANES]

            def store(row, reg, value):
                target[offset + row, part, reg * TILE : (reg + 1) * TILE, :] = value

            rows_from_tiles(load, flat, store, rows8)

    def convert_density(source, target, offset):
        @pl.loop(0, 2)
        def _(rows8):
            def load(block):
                return 1.0 / source[pl.ds(rows8 * TILE, TILE), block * LANES : (block + 1) * LANES]

            def store(row, reg, value):
                target[offset + row, reg * TILE : (reg + 1) * TILE, :] = value

            rows_from_tiles(load, flat, store, rows8)

    def advance(sub, row):
        base = row + 6
        u, v, p = (state[sub, base, part] for part in range(3))
        dx = [
            difference(*(state[sub, base + by, part] for by in (-2, -1, 1, 2)))
            for part in range(3)
        ]
        dy = [across(field, lane) for field in (u, v, p)]
        inv = inverse[row + 4]
        rate_u = u * dx[0] + v * dy[0] + inv * dx[2]
        rate_v = u * dx[1] + v * dy[1] + inv * dy[2]
        rate_p = u * dx[2] + v * dy[2] + LES_STIFF * (dx[0] + dy[1])
        return u - step * rate_u, v - step * rate_v, p - step * rate_p

    def put_advanced(row, fields):
        for part in range(3):
            advanced[row + 4, part] = fields[part]

    def advance_rows(sub, low, high):
        loop(low, high, lambda row: put_advanced(row, advance(sub, row)))

    def smooth(sub, row, own):
        for part in range(3):
            centre = advanced[row + 4, part]
            lateral = advanced[row + 3, part] + advanced[row + 5, part]
            sides = shifted(centre, 1, lane) + shifted(centre, -1, lane)
            value = (1.0 - FILTER_WEIGHT) * centre + FILTER_WEIGHT / 4.0 * (lateral + sides)
            state[sub + 1, row + 6, part] = value
            if own:
                if sub == 0:
                    total_out[part, row] = value
                else:
                    total_out[part, row] += value

    def smooth_rows(sub, low, high, own=True):
        loop(low, high, lambda row: smooth(sub, row, own))

    def far_row(row):
        base = row + 2
        u, v, p = (far[base, part] for part in range(3))
        dx = [
            difference(*(far[base + by, part] for by in (-2, -1, 1, 2))) for part in range(3)
        ]
        inv = far_inverse[row]
        dy_v, dy_p = across(v, lane), across(p, lane)
        far[base + ROWS + 4, 0] = u - step * (MEAN_FLOW * dx[0] + inv * dx[2])
        far[base + ROWS + 4, 1] = v - step * (MEAN_FLOW * dx[1] + inv * dy_p)
        far[base + ROWS + 4, 2] = p - step * (MEAN_FLOW * dx[2] + FAR_STIFF * (dx[0] + dy_v))

    def loop(low, high, body):
        @pl.loop(low, high, unroll=UNROLL.get(high - low, high - low))
        def _(row):
            body(row)

    def write_tiles(source, target):
        @pl.loop(0, 6)
        def _(index):
            part, rows8 = index // 2, index % 2

            def load(row, reg):
                return source(row, part, reg)

            def store(block, value):
                target[part, pl.ds(rows8 * TILE, TILE), block * LANES : (block + 1) * LANES] = value

            tiles_from_rows(load, flat, store, rows8)

    convert_state(les_ref, state.at[0], 6)
    convert_density(les_density_ref, inverse, 4)

    pl.semaphore_wait(barrier, devices - 1)

    @pl.when(has_up)
    def _():
        up_copy(0).start()
        inverse_up().start()
        up_copy(1).start()

    @pl.when(has_down)
    def _():
        down_copy(0).start()
        inverse_down().start()
        down_copy(1).start()

    for sub in range(SUBSTEPS):
        advance_rows(sub, 2, ROWS - 2)
        smooth_rows(sub, 3, ROWS - 3)

        if sub + 2 < SUBSTEPS:

            @pl.when(has_up)
            def _():
                up_copy(sub + 2).start()

            @pl.when(has_down)
            def _():
                down_copy(sub + 2).start()

        if sub + 2 == SUBSTEPS:

            @pl.when(has_up)
            def _():
                far_up().start()

            @pl.when(has_down)
            def _():
                far_down().start()

        if sub == 0:
            convert_state(far_ref, far, 2)
            convert_density(far_density_ref, far_inverse, 0)
            rank_faces(count_ref, owner_ref, facts)
        if sub == 1:
            sort_faces(
                count_ref,
                owner_ref,
                cell_ref,
                area_ref,
                target_ref,
                order,
                starts,
                targets,
                facts,
                grid,
            )
        if sub == 2:
            loop(2, ROWS - 2, far_row)

        @pl.when(has_up)
        def _():
            if sub == 0:
                down_copy(0).wait_recv()
                inverse_down().wait_recv()
            put_advanced(-1, advance(sub, -1))

        @pl.when(has_down)
        def _():
            if sub == 0:
                up_copy(0).wait_recv()
                inverse_up().wait_recv()
            put_advanced(ROWS, advance(sub, ROWS))

        advance_rows(sub, 0, 2)
        advance_rows(sub, ROWS - 2, ROWS)
        smooth_rows(sub, 0, 3)
        smooth_rows(sub, ROWS - 3, ROWS)

        if sub + 1 < SUBSTEPS:

            @pl.when(has_up)
            def _():
                down_copy(sub + 1).wait_recv()
                advance_rows(sub, -4, -1)
                smooth_rows(sub, -3, 0, own=False)

            @pl.when(has_down)
            def _():
                up_copy(sub + 1).wait_recv()
                advance_rows(sub, ROWS + 1, ROWS + 4)
                smooth_rows(sub, ROWS, ROWS + 3, own=False)

    pick_faces(total_out, order, starts, targets, ready, turned, slots)
    own = pltpu.make_async_copy(ready.at[me], arrived.at[me], local_sem)
    own.start()

    @pl.loop(1, devices)
    def _(offset):
        other, where = place(offset)
        pltpu.make_async_remote_copy(
            src_ref=ready.at[other],
            dst_ref=arrived.at[me],
            send_sem=faces_send,
            recv_sem=faces_recv,
            device_id=where,
            device_id_type=MESH,
        ).start()

    write_tiles(
        lambda row, part, reg: state[SUBSTEPS, row + 6, part, reg * TILE : (reg + 1) * TILE, :],
        les_out,
    )

    @pl.when(has_up)
    def _():
        far_down().wait_recv()

    @pl.when(has_down)
    def _():
        far_up().wait_recv()

    loop(0, 2, far_row)
    loop(ROWS - 2, ROWS, far_row)
    write_tiles(
        lambda row, part, reg: far[row + ROWS + 6, part, reg * TILE : (reg + 1) * TILE, :],
        stepped_out,
    )

    @pl.when(has_up)
    def _():
        for sub in range(SUBSTEPS):
            up_copy(sub).wait_send()
        inverse_up().wait_send()
        far_up().wait_send()

    @pl.when(has_down)
    def _():
        for sub in range(SUBSTEPS):
            down_copy(sub).wait_send()
        inverse_down().wait_send()
        far_down().wait_send()

    own.wait()
    all_but_one = pl.ds(0, devices - 1)
    pltpu.make_async_copy(arrived.at[all_but_one], arrived.at[all_but_one], faces_recv).wait()
    pltpu.make_async_copy(ready.at[all_but_one], ready.at[all_but_one], faces_send).wait()


def fields(les_state, les_density, far_state, far_density, counts, owner, cell, area, target):
    block = jax.ShapeDtypeStruct((3, ROWS, COLS), F32)
    dma = pltpu.SemaphoreType.DMA
    return pl.pallas_call(
        fields_kernel,
        out_shape=(block, block, jax.ShapeDtypeStruct((DEVICES, 4, RANKS), F32)),
        in_specs=[VMEM] * 4 + [SMEM] + [VMEM] * 4,
        out_specs=(VMEM,) * 3,
        scratch_shapes=[
            pltpu.VMEM((3, ROWS, TILES, LANES), F32),
            pltpu.VMEM((SUBSTEPS + 1, ROWS + 12, 3, TILES, LANES), F32),
            pltpu.VMEM((ROWS + 8, 3, TILES, LANES), F32),
            pltpu.VMEM((ROWS + 8, TILES, LANES), F32),
            pltpu.VMEM((2 * ROWS + 6, 3, TILES, LANES), F32),
            pltpu.VMEM((ROWS, TILES, LANES), F32),
            pltpu.VMEM((TILES * TILE, LANES), F32),
            dma((SUBSTEPS, 2)),
            dma((SUBSTEPS, 2)),
            dma((2,)),
            dma((2,)),
            dma((2,)),
            dma((2,)),
            pltpu.VMEM((6 * PLANNED, BLOCK), F32),
            pltpu.SMEM((BUCKETS + 1,), I32),
            pltpu.VMEM((DEVICES, RANKS), F32),
            pltpu.VMEM((11, FACE_ROWS, LANES), F32),
            pltpu.VMEM((3 * HALF, 2 * RANKS), F32),
            pltpu.VMEM((DEVICES, 4, RANKS), F32),
            pltpu.VMEM((BUCKETS, 6 * LANES, BUCKET), BF16),
            pltpu.VMEM((6 * HALF, 2 * RANKS), F32),
            dma,
            dma,
            dma,
        ],
        compiler_params=params(collective_id=0, has_side_effects=True),
        name="fields",
    )(les_state, les_density, far_state, far_density, counts, owner, cell, area, target)


def add_kernel(arrived_ref, stepped_ref, out, held, order, sums, starts):
    for part in range(3):
        high, low = halves(arrived_ref[pl.ds(part, DEVICES, stride=4), :])
        held[2 * part] = high
        held[2 * part + 1] = low
    target = arrived_ref[pl.ds(3, DEVICES, stride=4), :].astype(I32) - 1
    row, column = target >> 13, target & (COLS - 1)
    cell_row = ((row >> 3) * TILES + (column >> 7)) * TILE + (row & 7)
    bucket = jnp.where(target >= 0, cell_row >> 8, -1)
    held[6] = (cell_row & (BUCKET - 1)).astype(F32)
    held[7] = (column & (LANES - 1)).astype(F32)
    held[8], held[9] = block_and_lane(bucket_places(bucket, DEVICES, starts))
    order[...] = jnp.zeros_like(order)
    sums[...] = jnp.zeros_like(sums)
    by_lane = indices(BLOCK, LINE)
    by_block = indices(SORTED, LINE)
    wide = LINE // LANES

    @pl.loop(0, DEVICES * RANKS // LINE, unroll=2)
    def _(step):
        fact = [lines(held.at[i], step * wide, wide) for i in range(10)]
        order[...] += product(spread(by_block, fact[8], fact[:8]), one_hot(by_lane, fact[9]))

    by_row = indices(BUCKET, BLOCK)
    by_column = indices(LANES, BLOCK)

    @pl.loop(0, steps_of(starts))
    def _(step):
        for i in range(TOGETHER):
            block = step * TOGETHER + i
            fact = [order[pl.ds(part * SORTED + block, 1), :] for part in range(8)]
            bucket = bucket_of(block, starts)
            sums[bucket] += product(one_hot(by_row, fact[6]), spread(by_column, fact[7], fact[:6]))

    for part in range(3):
        high = slice(2 * part * LANES, (2 * part + 1) * LANES)
        low = slice((2 * part + 1) * LANES, (2 * part + 2) * LANES)
        for band in range(ROWS // TILE):
            rows = slice(band * TILE, (band + 1) * TILE)
            for block in range(TILES):
                first = (band * TILES + block) * TILE
                bucket, first = first // BUCKET, first % BUCKET
                columns = slice(block * LANES, (block + 1) * LANES)
                out[part, rows, columns] = stepped_ref[part, rows, columns] + (
                    sums[bucket, first : first + TILE, high]
                    + sums[bucket, first : first + TILE, low]
                )


def add(arrived, stepped):
    return pl.pallas_call(
        add_kernel,
        out_shape=jax.ShapeDtypeStruct((3, ROWS, COLS), F32),
        in_specs=[VMEM] * 2,
        out_specs=VMEM,
        scratch_shapes=[
            pltpu.VMEM((10, DEVICES, RANKS), F32),
            pltpu.VMEM((8 * SORTED, BLOCK), F32),
            pltpu.VMEM((BUCKETS, BUCKET, 6 * LANES), F32),
            pltpu.SMEM((BUCKETS + 1,), I32),
        ],
        compiler_params=params(),
        name="add",
    )(arrived, stepped)


def local(
    les_state,
    les_density,
    far_state,
    far_density,
    face_cell,
    face_area,
    face_owner,
    face_counts,
    face_target,
):
    cell, area, owner, target = (
        array.reshape(FACE_ROWS, LANES) for array in (face_cell, face_area, face_owner, face_target)
    )
    les_final, stepped, arrived = fields(
        les_state[0],
        les_density[0],
        far_state[0],
        far_density[0],
        face_counts,
        owner,
        cell,
        area,
        target,
    )
    far_final = add(arrived.reshape(4 * DEVICES, LANES), stepped)
    return les_final[None], far_final[None]


def solution(mesh):
    field = P("sec", None, "dom", None)
    density = P("sec", "dom", None)
    faces = P(("sec", "dom"))
    return jax.shard_map(
        local,
        mesh=mesh,
        in_specs=(field, density, field, density) + (faces,) * 5,
        out_specs=(field, field),
        check_vma=False,
    )
```

```python
import jax
import jax.numpy as jnp
from jax import lax
from jax.experimental import pallas as pl
from jax.experimental.pallas import tpu as pltpu
from jax.sharding import PartitionSpec as P

SUBSTEPS = 5
UNROLL = {12: 4, 10: 5}
TIME_STEP = 0.1
LES_STIFF = 1.0
FAR_STIFF = 1.0
FILTER_WEIGHT = 0.5
MEAN_FLOW = 0.3

LANES = 128
TILE = 8
ROWS = 16
COLS = 8192
TILES = COLS // LANES
REGS = TILES // TILE
FACES = 8192
FACE_ROWS = FACES // LANES
DEVICES = 128
RANKS = 128
CELL_ROWS = ROWS * COLS // LANES

MESH = pl.DeviceIdType.MESH
VMEM = pl.BlockSpec(memory_space=pltpu.VMEM)
SMEM = pl.BlockSpec(memory_space=pltpu.SMEM)
F32 = jnp.float32
BF16 = jnp.bfloat16
I32 = jnp.int32


def params(**more):
    return pltpu.CompilerParams(vmem_limit_bytes=56 * 1024 * 1024, **more)


def rows_from_tiles(load, flat, store, rows8):
    for block in range(TILES):
        flat[block * TILE : (block + 1) * TILE, :] = load(block)
    for row in range(TILE):
        for reg in range(REGS):
            store(rows8 * TILE + row, reg, flat[pl.ds(TILE * reg + row, TILE, stride=TILES), :])


def tiles_from_rows(load, flat, store, rows8):
    for row in range(TILE):
        for reg in range(REGS):
            flat[pl.ds(TILE * reg + row, TILE, stride=TILES), :] = load(rows8 * TILE + row, reg)
    for block in range(TILES):
        store(block, flat[block * TILE : (block + 1) * TILE, :])


def shifted(row, by, lane):
    if by > 0:
        turned = pltpu.roll(row, LANES - by, 1)
        crossed = jnp.concatenate([turned[TILE:], pltpu.roll(turned[:TILE], TILE - 1, 0)], axis=0)
        return jnp.where(lane >= LANES - by, crossed, turned)
    turned = pltpu.roll(row, -by, 1)
    crossed = jnp.concatenate(
        [pltpu.roll(turned[TILES - TILE :], 1, 0), turned[: TILES - TILE]], axis=0
    )
    return jnp.where(lane < -by, crossed, turned)


def difference(far_left, left, right, far_right):
    return 8.0 * (right - left) - (far_right - far_left)


def across(row, lane):
    return difference(
        shifted(row, -2, lane), shifted(row, -1, lane), shifted(row, 1, lane), shifted(row, 2, lane)
    )


RANK_BLOCK = 256
BUCKETS = 4
BUCKET = CELL_ROWS // BUCKETS
BLOCK = 256
LINE = 512
TOGETHER = 4
HALF = DEVICES // 2
PLANNED = 48
SORTED = 80


def halves(values):
    high = values.astype(BF16).astype(F32)
    return high, values - high


def indices(rows, columns):
    return lax.broadcasted_iota(I32, (rows, columns), 0).astype(F32).astype(BF16)


def one_hot(index, line):
    return jnp.where(index == line.astype(BF16), jnp.ones((), BF16), jnp.zeros((), BF16))


def spread(index, line, parts):
    here = index == line.astype(BF16)
    return jnp.concatenate(
        [jnp.where(here, part.astype(BF16), jnp.zeros((), BF16)) for part in parts], axis=0
    )


def product(left, right):
    return lax.dot_general(left, right, (((1,), (1,)), ((), ())), preferred_element_type=F32)


def folded(index, line, parts, right):
    return product(
        jnp.concatenate([spread(index, line, parts[0::2]), spread(index, line, parts[1::2])], axis=1),
        jnp.concatenate([right, right], axis=1),
    )


def lines(ref, first, count):
    return jnp.concatenate([ref[pl.ds(first + i, 1), :] for i in range(count)], axis=1)


def bucket_places(bucket, rows, starts_ref):
    before = lax.broadcasted_iota(I32, (LANES, 2 * LANES), 0)
    after = lax.broadcasted_iota(I32, (LANES, 2 * LANES), 1)
    weights = jnp.where((before < after) | (after >= LANES), 1.0, 0.0).astype(BF16)
    below = lax.broadcasted_iota(I32, (rows, rows), 0) > lax.broadcasted_iota(I32, (rows, rows), 1)
    below = jnp.where(below, 1.0, 0.0).astype(BF16)
    place = jnp.full((rows, LANES), -1.0, F32)
    base = jnp.zeros((1, LANES), F32)
    for b in range(BUCKETS):
        starts_ref[b] = jnp.max(base).astype(I32)
        here = bucket == b
        counted = jnp.dot(
            jnp.where(here, 1.0, 0.0).astype(BF16), weights, preferred_element_type=F32
        )
        totals = counted[:, LANES:]
        offset = jnp.dot(below, totals.astype(BF16), preferred_element_type=F32)
        place = jnp.where(here, counted[:, :LANES] + offset + base * float(BLOCK), place)
        total = offset[rows - 1 :] + totals[rows - 1 :]
        base = base + jnp.floor((total + (BLOCK - 1.0)) * (1.0 / BLOCK))
    starts_ref[BUCKETS] = jnp.max(base).astype(I32)
    return place


def block_and_lane(place):
    block = jnp.floor(place * (1.0 / BLOCK))
    return block, place - block * float(BLOCK)


def by_owner(halved):
    return jnp.concatenate([halved[:, :RANKS], halved[:, RANKS:]], axis=0)


def bucket_of(block, starts_ref):
    bucket = 0
    for b in range(1, BUCKETS):
        bucket = bucket + jnp.where(block >= starts_ref[b], 1, 0)
    return bucket


def steps_of(starts_ref):
    return (starts_ref[BUCKETS] + TOGETHER - 1) // TOGETHER


def rank_faces(count_ref, owner_ref, facts):
    live = count_ref[0]
    owners = lax.broadcasted_iota(I32, (DEVICES, RANK_BLOCK), 0)
    before = lax.broadcasted_iota(I32, (RANK_BLOCK, RANK_BLOCK), 0)
    after = lax.broadcasted_iota(I32, (RANK_BLOCK, RANK_BLOCK), 1)
    weights = jnp.concatenate(
        [
            jnp.where(before < after, 1.0, 0.0).astype(BF16),
            jnp.ones((RANK_BLOCK, RANK_BLOCK), BF16),
        ],
        axis=1,
    )
    face = lax.broadcasted_iota(I32, (1, RANK_BLOCK), 1)
    base = jnp.zeros((DEVICES, RANK_BLOCK), F32)
    wide = RANK_BLOCK // LANES
    for block in range(FACES // RANK_BLOCK):
        named = lines(owner_ref, block * wide, wide)
        named = jnp.where(face + block * RANK_BLOCK < live, named, -1)
        hits = jnp.where(owners == named, 1.0, 0.0)
        counted = jnp.dot(hits.astype(BF16), weights, preferred_element_type=F32)
        rank = jnp.sum(hits * (counted[:, :RANK_BLOCK] + base), axis=0, keepdims=True)
        base = base + counted[:, RANK_BLOCK:]
        for i in range(wide):
            facts[3, block * wide + i : block * wide + i + 1, :] = rank[
                :, i * LANES : (i + 1) * LANES
            ]


def sort_faces(
    count_ref, owner_ref, cell_ref, area_ref, target_ref, order, starts, targets, facts, grid
):
    live = count_ref[0]
    cell = cell_ref[...]
    target = target_ref[...] + 1
    row, column = cell >> 13, cell & (COLS - 1)
    cell_row = row * TILES + ((column >> 7) & 7) * TILE + (column >> 10)
    number = (
        lax.broadcasted_iota(I32, (FACE_ROWS, LANES), 0) * LANES
        + lax.broadcasted_iota(I32, (FACE_ROWS, LANES), 1)
    )
    bucket = jnp.where(number < live, cell_row >> 8, -1)
    facts[0] = (cell_row & (BUCKET - 1)).astype(F32)
    facts[1] = (column & (LANES - 1)).astype(F32)
    owner = owner_ref[...]
    facts[2] = jnp.where(number < live, owner & (HALF - 1), -1).astype(F32)
    facts[3] = facts[3] + ((owner >> 6) * RANKS).astype(F32)
    facts[4], facts[5] = halves(area_ref[...] * (1.0 / SUBSTEPS))
    for i in range(3):
        facts[6 + i] = ((target >> (7 * i)) & (LANES - 1)).astype(F32)
    facts[9], facts[10] = block_and_lane(bucket_places(bucket, FACE_ROWS, starts))

    order[...] = jnp.zeros_like(order)
    grid[...] = jnp.zeros_like(grid)
    by_lane = indices(BLOCK, LINE)
    by_block = indices(PLANNED, LINE)
    by_half = indices(HALF, LINE)
    wide = LINE // LANES

    @pl.loop(0, FACES // LINE, unroll=2)
    def _(step):
        fact = [lines(facts.at[i], step * wide, wide) for i in range(11)]
        order[...] += product(spread(by_block, fact[9], fact[:6]), one_hot(by_lane, fact[10]))
        grid[...] += product(spread(by_half, fact[2], fact[6:9]), one_hot(by_lane, fact[3]))

    targets[...] = by_owner(
        grid[:HALF]
        + grid[HALF : 2 * HALF] * float(LANES)
        + grid[2 * HALF :] * float(LANES * LANES)
    )


def pick_faces(total_ref, order_ref, starts_ref, targets_ref, ready, turned, slots):
    for part in range(3):
        for block in range(CELL_ROWS // LANES):
            high, low = halves(total_ref[part, 2 * block : 2 * block + 2].reshape(LANES, LANES).T)
            bucket = block * LANES // BUCKET
            columns = slice(block * LANES % BUCKET, block * LANES % BUCKET + LANES)
            turned[bucket, 2 * part * LANES : (2 * part + 1) * LANES, columns] = high.astype(BF16)
            turned[bucket, (2 * part + 1) * LANES : (2 * part + 2) * LANES, columns] = low.astype(
                BF16
            )
    slots[...] = jnp.zeros_like(slots)
    by_row = indices(BUCKET, BLOCK)
    lane = lax.broadcasted_iota(I32, (LANES, BLOCK), 0).astype(F32)
    by_half = indices(HALF, BLOCK * TOGETHER)
    by_rank = indices(2 * RANKS, BLOCK * TOGETHER)

    @pl.loop(0, (FACES // BLOCK + BUCKETS) // TOGETHER, unroll=3)
    def _(step):
        surface = []
        placed = []
        for i in range(TOGETHER):
            block = step * TOGETHER + i
            row, where, owner, rank, high, low = (
                order_ref[pl.ds(part * PLANNED + block, 1), :] for part in range(6)
            )
            found = jnp.dot(
                turned[bucket_of(block, starts_ref)],
                one_hot(by_row, row),
                preferred_element_type=F32,
            )
            is_lane = lane == where
            parts = []
            for part in range(3):
                both = (
                    found[2 * part * LANES : (2 * part + 1) * LANES]
                    + found[(2 * part + 1) * LANES : (2 * part + 2) * LANES]
                )
                value = jnp.sum(jnp.where(is_lane, both, 0.0), axis=0, keepdims=True)
                parts.extend(halves(value * (high + low)))
            surface.append(parts)
            placed.append((owner, rank))
        joined = [jnp.concatenate(part, axis=1) for part in zip(*surface)]
        owner, rank = (jnp.concatenate(part, axis=1) for part in zip(*placed))
        slots[...] += product(spread(by_half, owner, joined), one_hot(by_rank, rank))

    for part in range(3):
        first = 2 * part * HALF
        ready[:, part, :] = by_owner(
            slots[first : first + HALF] + slots[first + HALF : first + 2 * HALF]
        )
    ready[:, 3, :] = targets_ref[...]


def fields_kernel(
    les_ref,
    les_density_ref,
    far_ref,
    far_density_ref,
    count_ref,
    owner_ref,
    cell_ref,
    area_ref,
    target_ref,
    les_out,
    stepped_out,
    arrived,
    total_out,
    state,
    advanced,
    inverse,
    far,
    far_inverse,
    flat,
    send_sem,
    recv_sem,
    inverse_send,
    inverse_recv,
    far_send,
    far_recv,
    order,
    starts,
    targets,
    facts,
    grid,
    ready,
    turned,
    slots,
    local_sem,
    faces_send,
    faces_recv,
):
    dom = lax.axis_index("dom")
    doms = lax.axis_size("dom")
    has_up = dom > 0
    has_down = dom < doms - 1
    up = lax.rem(dom + doms - 1, doms)
    down = lax.rem(dom + 1, doms)
    lane = lax.broadcasted_iota(I32, (TILES, LANES), 1)
    step = TIME_STEP / 12.0

    sec = lax.axis_index("sec")
    secs = lax.axis_size("sec")
    devices = secs * doms
    me = sec * doms + dom
    barrier = pltpu.get_barrier_semaphore()

    def for_others(act):
        for ahead in range(secs):
            there = lax.rem(sec + ahead, secs)

            @pl.loop(0 if ahead else 1, doms, unroll=8 if ahead else doms - 1)
            def _(along):
                where = lax.rem(dom + along, doms)
                act(there * doms + where, {"sec": there, "dom": where})

    for_others(
        lambda other, where: pl.semaphore_signal(
            barrier, inc=1, device_id=where, device_id_type=MESH
        )
    )

    def remote(ref, first, count, landing, sems, where):
        return pltpu.make_async_remote_copy(
            src_ref=ref.at[pl.ds(first, count)],
            dst_ref=ref.at[pl.ds(landing, count)],
            send_sem=sems[0],
            recv_sem=sems[1],
            device_id={"dom": where},
            device_id_type=MESH,
        )

    def up_copy(number):
        sems = (send_sem.at[number, 0], recv_sem.at[number, 0])
        near = number == 0
        first, landing = (6, ROWS + 6) if near else (9, ROWS + 9)
        return remote(state.at[0 if near else number - 1], first, 3, landing, sems, up)

    def down_copy(number):
        sems = (send_sem.at[number, 1], recv_sem.at[number, 1])
        near = number == 0
        first, landing = (ROWS + 3, 3) if near else (ROWS, 0)
        return remote(state.at[0 if near else number - 1], first, 3, landing, sems, down)

    def inverse_up():
        return remote(inverse, 4, 4, ROWS + 4, (inverse_send.at[0], inverse_recv.at[0]), up)

    def inverse_down():
        return remote(inverse, ROWS, 4, 0, (inverse_send.at[1], inverse_recv.at[1]), down)

    def far_up():
        return remote(far, 2, 2, ROWS + 2, (far_send.at[0], far_recv.at[0]), up)

    def far_down():
        return remote(far, ROWS, 2, 0, (far_send.at[1], far_recv.at[1]), down)

    @pl.when(jnp.logical_not(has_up))
    def _():
        for sub in range(SUBSTEPS):
            state[sub, 0:6] = jnp.zeros((6, 3, TILES, LANES), F32)
        advanced[0:4] = jnp.zeros((4, 3, TILES, LANES), F32)
        far[0:2] = jnp.zeros((2, 3, TILES, LANES), F32)

    @pl.when(jnp.logical_not(has_down))
    def _():
        for sub in range(SUBSTEPS):
            state[sub, ROWS + 6 :] = jnp.zeros((6, 3, TILES, LANES), F32)
        advanced[ROWS + 4 :] = jnp.zeros((4, 3, TILES, LANES), F32)
        far[ROWS + 2 : ROWS + 4] = jnp.zeros((2, 3, TILES, LANES), F32)

    def convert_state(source, target, offset):
        @pl.loop(0, 6)
        def _(index):
            part, rows8 = index // 2, index % 2

            def load(block):
                return source[part, pl.ds(rows8 * TILE, TILE), block * LANES : (block + 1) * LANES]

            def store(row, reg, value):
                target[offset + row, part, reg * TILE : (reg + 1) * TILE, :] = value

            rows_from_tiles(load, flat, store, rows8)

    def convert_density(source, target, offset):
        @pl.loop(0, 2)
        def _(rows8):
            def load(block):
                return 1.0 / source[pl.ds(rows8 * TILE, TILE), block * LANES : (block + 1) * LANES]

            def store(row, reg, value):
                target[offset + row, reg * TILE : (reg + 1) * TILE, :] = value

            rows_from_tiles(load, flat, store, rows8)

    def advance(sub, row):
        base = row + 6
        u, v, p = (state[sub, base, part] for part in range(3))
        dx = [
            difference(*(state[sub, base + by, part] for by in (-2, -1, 1, 2)))
            for part in range(3)
        ]
        dy = [across(field, lane) for field in (u, v, p)]
        inv = inverse[row + 4]
        rate_u = u * dx[0] + v * dy[0] + inv * dx[2]
        rate_v = u * dx[1] + v * dy[1] + inv * dy[2]
        rate_p = u * dx[2] + v * dy[2] + LES_STIFF * (dx[0] + dy[1])
        return u - step * rate_u, v - step * rate_v, p - step * rate_p

    def put_advanced(row, fields):
        for part in range(3):
            advanced[row + 4, part] = fields[part]

    def advance_rows(sub, low, high):
        loop(low, high, lambda row: put_advanced(row, advance(sub, row)))

    def smooth(sub, row, own):
        for part in range(3):
            centre = advanced[row + 4, part]
            lateral = advanced[row + 3, part] + advanced[row + 5, part]
            sides = shifted(centre, 1, lane) + shifted(centre, -1, lane)
            value = (1.0 - FILTER_WEIGHT) * centre + FILTER_WEIGHT / 4.0 * (lateral + sides)
            state[sub + 1, row + 6, part] = value
            if own:
                if sub == 0:
                    total_out[part, row] = value
                else:
                    total_out[part, row] += value

    def smooth_rows(sub, low, high, own=True):
        loop(low, high, lambda row: smooth(sub, row, own))

    def far_row(row):
        base = row + 2
        u, v, p = (far[base, part] for part in range(3))
        dx = [
            difference(*(far[base + by, part] for by in (-2, -1, 1, 2))) for part in range(3)
        ]
        inv = far_inverse[row]
        dy_v, dy_p = across(v, lane), across(p, lane)
        far[base + ROWS + 4, 0] = u - step * (MEAN_FLOW * dx[0] + inv * dx[2])
        far[base + ROWS + 4, 1] = v - step * (MEAN_FLOW * dx[1] + inv * dy_p)
        far[base + ROWS + 4, 2] = p - step * (MEAN_FLOW * dx[2] + FAR_STIFF * (dx[0] + dy_v))

    def loop(low, high, body):
        @pl.loop(low, high, unroll=UNROLL.get(high - low, high - low))
        def _(row):
            body(row)

    def write_tiles(source, target):
        @pl.loop(0, 6)
        def _(index):
            part, rows8 = index // 2, index % 2

            def load(row, reg):
                return source(row, part, reg)

            def store(block, value):
                target[part, pl.ds(rows8 * TILE, TILE), block * LANES : (block + 1) * LANES] = value

            tiles_from_rows(load, flat, store, rows8)

    convert_state(les_ref, state.at[0], 6)
    convert_density(les_density_ref, inverse, 4)

    pl.semaphore_wait(barrier, devices - 1)

    @pl.when(has_up)
    def _():
        up_copy(0).start()
        inverse_up().start()
        up_copy(1).start()

    @pl.when(has_down)
    def _():
        down_copy(0).start()
        inverse_down().start()
        down_copy(1).start()

    for sub in range(SUBSTEPS):
        advance_rows(sub, 2, ROWS - 2)
        smooth_rows(sub, 3, ROWS - 3)

        if sub + 2 < SUBSTEPS:

            @pl.when(has_up)
            def _():
                up_copy(sub + 2).start()

            @pl.when(has_down)
            def _():
                down_copy(sub + 2).start()

        if sub + 2 == SUBSTEPS:

            @pl.when(has_up)
            def _():
                far_up().start()

            @pl.when(has_down)
            def _():
                far_down().start()

        if sub == 0:
            convert_state(far_ref, far, 2)
            convert_density(far_density_ref, far_inverse, 0)
            rank_faces(count_ref, owner_ref, facts)
        if sub == 1:
            sort_faces(
                count_ref,
                owner_ref,
                cell_ref,
                area_ref,
                target_ref,
                order,
                starts,
                targets,
                facts,
                grid,
            )
        if sub == 2:
            loop(2, ROWS - 2, far_row)

        @pl.when(has_up)
        def _():
            down_copy(sub).wait_recv()
            if sub == 0:
                inverse_down().wait_recv()
            else:
                advance_rows(sub - 1, -4, -1)
                smooth_rows(sub - 1, -3, 0, own=False)
            put_advanced(-1, advance(sub, -1))

        @pl.when(has_down)
        def _():
            up_copy(sub).wait_recv()
            if sub == 0:
                inverse_up().wait_recv()
            else:
                advance_rows(sub - 1, ROWS + 1, ROWS + 4)
                smooth_rows(sub - 1, ROWS, ROWS + 3, own=False)
            put_advanced(ROWS, advance(sub, ROWS))

        advance_rows(sub, 0, 2)
        advance_rows(sub, ROWS - 2, ROWS)
        smooth_rows(sub, 0, 3)
        smooth_rows(sub, ROWS - 3, ROWS)

    pick_faces(total_out, order, starts, targets, ready, turned, slots)
    own = pltpu.make_async_copy(ready.at[me], arrived.at[me], local_sem)
    own.start()

    for_others(
        lambda other, where: pltpu.make_async_remote_copy(
            src_ref=ready.at[other],
            dst_ref=arrived.at[me],
            send_sem=faces_send,
            recv_sem=faces_recv,
            device_id=where,
            device_id_type=MESH,
        ).start()
    )

    write_tiles(
        lambda row, part, reg: state[SUBSTEPS, row + 6, part, reg * TILE : (reg + 1) * TILE, :],
        les_out,
    )

    @pl.when(has_up)
    def _():
        far_down().wait_recv()

    @pl.when(has_down)
    def _():
        far_up().wait_recv()

    loop(0, 2, far_row)
    loop(ROWS - 2, ROWS, far_row)
    write_tiles(
        lambda row, part, reg: far[row + ROWS + 6, part, reg * TILE : (reg + 1) * TILE, :],
        stepped_out,
    )

    @pl.when(has_up)
    def _():
        for sub in range(SUBSTEPS):
            up_copy(sub).wait_send()
        inverse_up().wait_send()
        far_up().wait_send()

    @pl.when(has_down)
    def _():
        for sub in range(SUBSTEPS):
            down_copy(sub).wait_send()
        inverse_down().wait_send()
        far_down().wait_send()

    own.wait()
    all_but_one = pl.ds(0, devices - 1)
    pltpu.make_async_copy(arrived.at[all_but_one], arrived.at[all_but_one], faces_recv).wait()
    pltpu.make_async_copy(ready.at[all_but_one], ready.at[all_but_one], faces_send).wait()


def fields(les_state, les_density, far_state, far_density, counts, owner, cell, area, target):
    block = jax.ShapeDtypeStruct((3, ROWS, COLS), F32)
    dma = pltpu.SemaphoreType.DMA
    return pl.pallas_call(
        fields_kernel,
        out_shape=(block, block, jax.ShapeDtypeStruct((DEVICES, 4, RANKS), F32)),
        in_specs=[VMEM] * 4 + [SMEM] + [VMEM] * 4,
        out_specs=(VMEM,) * 3,
        scratch_shapes=[
            pltpu.VMEM((3, ROWS, TILES, LANES), F32),
            pltpu.VMEM((SUBSTEPS + 1, ROWS + 12, 3, TILES, LANES), F32),
            pltpu.VMEM((ROWS + 8, 3, TILES, LANES), F32),
            pltpu.VMEM((ROWS + 8, TILES, LANES), F32),
            pltpu.VMEM((2 * ROWS + 6, 3, TILES, LANES), F32),
            pltpu.VMEM((ROWS, TILES, LANES), F32),
            pltpu.VMEM((TILES * TILE, LANES), F32),
            dma((SUBSTEPS, 2)),
            dma((SUBSTEPS, 2)),
            dma((2,)),
            dma((2,)),
            dma((2,)),
            dma((2,)),
            pltpu.VMEM((6 * PLANNED, BLOCK), F32),
            pltpu.SMEM((BUCKETS + 1,), I32),
            pltpu.VMEM((DEVICES, RANKS), F32),
            pltpu.VMEM((11, FACE_ROWS, LANES), F32),
            pltpu.VMEM((3 * HALF, 2 * RANKS), F32),
            pltpu.VMEM((DEVICES, 4, RANKS), F32),
            pltpu.VMEM((BUCKETS, 6 * LANES, BUCKET), BF16),
            pltpu.VMEM((6 * HALF, 2 * RANKS), F32),
            dma,
            dma,
            dma,
        ],
        compiler_params=params(collective_id=0, has_side_effects=True),
        name="fields",
    )(les_state, les_density, far_state, far_density, counts, owner, cell, area, target)


def add_kernel(arrived_ref, stepped_ref, out, held, order, sums, starts):
    for part in range(3):
        held[2 * part], held[2 * part + 1] = halves(
            arrived_ref[pl.ds(part, DEVICES, stride=4), :]
        )
    target = arrived_ref[pl.ds(3, DEVICES, stride=4), :].astype(I32) - 1
    row, column = target >> 13, target & (COLS - 1)
    cell_row = ((row >> 3) * TILES + (column >> 7)) * TILE + (row & 7)
    bucket = jnp.where(target >= 0, cell_row >> 8, -1)
    held[6] = (cell_row & (BUCKET - 1)).astype(F32)
    held[7] = (column & (LANES - 1)).astype(F32)
    held[8], held[9] = block_and_lane(bucket_places(bucket, DEVICES, starts))
    order[...] = jnp.zeros_like(order)
    sums[...] = jnp.zeros_like(sums)
    by_lane = indices(BLOCK, LINE)
    by_block = indices(SORTED, LINE)
    wide = LINE // LANES

    @pl.loop(0, DEVICES * RANKS // LINE, unroll=4)
    def _(step):
        fact = [lines(held.at[i], step * wide, wide) for i in range(10)]
        order[...] += product(spread(by_block, fact[8], fact[:8]), one_hot(by_lane, fact[9]))

    by_row = indices(BUCKET, BLOCK)
    by_column = indices(LANES, BLOCK)

    @pl.loop(0, steps_of(starts))
    def _(step):
        for i in range(TOGETHER):
            block = step * TOGETHER + i
            *parts, row, column = (order[pl.ds(part * SORTED + block, 1), :] for part in range(8))
            sums[bucket_of(block, starts)] += folded(by_column, column, parts, one_hot(by_row, row))

    for part in range(3):
        for bucket in range(BUCKETS):
            for half in range(BUCKET // LANES):
                cells = sums[
                    bucket,
                    part * LANES : (part + 1) * LANES,
                    half * LANES : (half + 1) * LANES,
                ].T
                for tile in range(LANES // TILE):
                    number = (bucket * BUCKET + half * LANES) // TILE + tile
                    rows = slice(number // TILES * TILE, (number // TILES + 1) * TILE)
                    columns = slice(number % TILES * LANES, (number % TILES + 1) * LANES)
                    out[part, rows, columns] = (
                        stepped_ref[part, rows, columns] + cells[tile * TILE : (tile + 1) * TILE]
                    )


def add(arrived, stepped):
    return pl.pallas_call(
        add_kernel,
        out_shape=jax.ShapeDtypeStruct((3, ROWS, COLS), F32),
        in_specs=[VMEM] * 2,
        out_specs=VMEM,
        scratch_shapes=[
            pltpu.VMEM((10, DEVICES, RANKS), F32),
            pltpu.VMEM((8 * SORTED, BLOCK), F32),
            pltpu.VMEM((BUCKETS, 3 * LANES, BUCKET), F32),
            pltpu.SMEM((BUCKETS + 1,), I32),
        ],
        compiler_params=params(),
        name="add",
    )(arrived, stepped)


def local(
    les_state,
    les_density,
    far_state,
    far_density,
    face_cell,
    face_area,
    face_owner,
    face_counts,
    face_target,
):
    cell, area, owner, target = (
        array.reshape(FACE_ROWS, LANES) for array in (face_cell, face_area, face_owner, face_target)
    )
    les_final, stepped, arrived = fields(
        les_state[0],
        les_density[0],
        far_state[0],
        far_density[0],
        face_counts,
        owner,
        cell,
        area,
        target,
    )
    far_final = add(arrived.reshape(4 * DEVICES, LANES), stepped)
    return les_final[None], far_final[None]


def solution(mesh):
    field = P("sec", None, "dom", None)
    density = P("sec", "dom", None)
    faces = P(("sec", "dom"))
    return jax.shard_map(
        local,
        mesh=mesh,
        in_specs=(field, density, field, density) + (faces,) * 5,
        out_specs=(field, field),
        check_vma=False,
    )
```

```python
import jax
import jax.numpy as jnp
from jax import lax
from jax.experimental import pallas as pl
from jax.experimental.pallas import tpu as pltpu
from jax.sharding import PartitionSpec as P

SUBSTEPS = 5
UNROLL = {12: 4, 10: 5}
TIME_STEP = 0.1
LES_STIFF = 1.0
FAR_STIFF = 1.0
FILTER_WEIGHT = 0.5
MEAN_FLOW = 0.3

LANES = 128
TILE = 8
ROWS = 16
COLS = 8192
TILES = COLS // LANES
GREETINGS = SUBSTEPS + 1
REGS = TILES // TILE
FACES = 8192
FACE_ROWS = FACES // LANES
DEVICES = 128
RANKS = 128
CELL_ROWS = ROWS * COLS // LANES

MESH = pl.DeviceIdType.MESH
VMEM = pl.BlockSpec(memory_space=pltpu.VMEM)
HBM = pl.BlockSpec(memory_space=pl.ANY)
SMEM = pl.BlockSpec(memory_space=pltpu.SMEM)
F32 = jnp.float32
BF16 = jnp.bfloat16
I32 = jnp.int32


def params(**more):
    return pltpu.CompilerParams(vmem_limit_bytes=56 * 1024 * 1024, **more)


def rows_from_tiles(load, flat, store, rows8):
    for block in range(TILES):
        flat[block * TILE : (block + 1) * TILE, :] = load(block)
    for row in range(TILE):
        for reg in range(REGS):
            store(rows8 * TILE + row, reg, flat[pl.ds(TILE * reg + row, TILE, stride=TILES), :])


def tiles_from_rows(load, flat, store, rows8):
    for row in range(TILE):
        for reg in range(REGS):
            flat[pl.ds(TILE * reg + row, TILE, stride=TILES), :] = load(rows8 * TILE + row, reg)
    for block in range(TILES):
        store(block, flat[block * TILE : (block + 1) * TILE, :])


def shifted(row, by, lane):
    if by > 0:
        turned = pltpu.roll(row, LANES - by, 1)
        crossed = jnp.concatenate([turned[TILE:], pltpu.roll(turned[:TILE], TILE - 1, 0)], axis=0)
        return jnp.where(lane >= LANES - by, crossed, turned)
    turned = pltpu.roll(row, -by, 1)
    crossed = jnp.concatenate(
        [pltpu.roll(turned[TILES - TILE :], 1, 0), turned[: TILES - TILE]], axis=0
    )
    return jnp.where(lane < -by, crossed, turned)


def difference(far_left, left, right, far_right):
    return 8.0 * (right - left) - (far_right - far_left)


def across(row, lane):
    return difference(
        shifted(row, -2, lane), shifted(row, -1, lane), shifted(row, 1, lane), shifted(row, 2, lane)
    )


RANK_BLOCK = 256
BUCKETS = 4
BUCKET = CELL_ROWS // BUCKETS
BLOCK = 256
LINE = 512
TOGETHER = 4
HALF = DEVICES // 2
PLANNED = 48
GROUPS = 2
SORTED = 48


def halves(values):
    high = values.astype(BF16).astype(F32)
    return high, values - high


def indices(rows, columns):
    return lax.broadcasted_iota(I32, (rows, columns), 0).astype(F32).astype(BF16)


def one_hot(index, line):
    return jnp.where(index == line.astype(BF16), jnp.ones((), BF16), jnp.zeros((), BF16))


def spread(index, line, parts):
    here = index == line.astype(BF16)
    return jnp.concatenate(
        [jnp.where(here, part.astype(BF16), jnp.zeros((), BF16)) for part in parts], axis=0
    )


def product(left, right):
    return lax.dot_general(left, right, (((1,), (1,)), ((), ())), preferred_element_type=F32)


def folded(index, line, parts, right):
    return product(
        jnp.concatenate([spread(index, line, parts[0::2]), spread(index, line, parts[1::2])], axis=1),
        jnp.concatenate([right, right], axis=1),
    )


def lines(ref, first, count):
    return jnp.concatenate([ref[pl.ds(first + i, 1), :] for i in range(count)], axis=1)


def bucket_places(bucket, rows, starts_ref):
    before = lax.broadcasted_iota(I32, (LANES, 2 * LANES), 0)
    after = lax.broadcasted_iota(I32, (LANES, 2 * LANES), 1)
    weights = jnp.where((before < after) | (after >= LANES), 1.0, 0.0).astype(BF16)
    below = lax.broadcasted_iota(I32, (rows, rows), 0) > lax.broadcasted_iota(I32, (rows, rows), 1)
    below = jnp.where(below, 1.0, 0.0).astype(BF16)
    place = jnp.full((rows, LANES), -1.0, F32)
    base = jnp.zeros((1, LANES), F32)
    for b in range(BUCKETS):
        starts_ref[b] = jnp.max(base).astype(I32)
        here = bucket == b
        counted = jnp.dot(
            jnp.where(here, 1.0, 0.0).astype(BF16), weights, preferred_element_type=F32
        )
        totals = counted[:, LANES:]
        offset = jnp.dot(below, totals.astype(BF16), preferred_element_type=F32)
        place = jnp.where(here, counted[:, :LANES] + offset + base * float(BLOCK), place)
        total = offset[rows - 1 :] + totals[rows - 1 :]
        base = base + jnp.floor((total + (BLOCK - 1.0)) * (1.0 / BLOCK))
    starts_ref[BUCKETS] = jnp.max(base).astype(I32)
    return place


def block_and_lane(place):
    block = jnp.floor(place * (1.0 / BLOCK))
    return block, place - block * float(BLOCK)


def by_owner(halved):
    return jnp.concatenate([halved[:, :RANKS], halved[:, RANKS:]], axis=0)


def bucket_of(block, starts_ref):
    bucket = 0
    for b in range(1, BUCKETS):
        bucket = bucket + jnp.where(block >= starts_ref[b], 1, 0)
    return bucket


def steps_of(starts_ref):
    return (starts_ref[BUCKETS] + TOGETHER - 1) // TOGETHER


def rank_faces(count_ref, owner_ref, facts):
    live = count_ref[0]
    owners = lax.broadcasted_iota(I32, (DEVICES, RANK_BLOCK), 0)
    before = lax.broadcasted_iota(I32, (RANK_BLOCK, RANK_BLOCK), 0)
    after = lax.broadcasted_iota(I32, (RANK_BLOCK, RANK_BLOCK), 1)
    weights = jnp.concatenate(
        [
            jnp.where(before < after, 1.0, 0.0).astype(BF16),
            jnp.ones((RANK_BLOCK, RANK_BLOCK), BF16),
        ],
        axis=1,
    )
    face = lax.broadcasted_iota(I32, (1, RANK_BLOCK), 1)
    base = jnp.zeros((DEVICES, RANK_BLOCK), F32)
    wide = RANK_BLOCK // LANES
    for block in range(FACES // RANK_BLOCK):
        named = lines(owner_ref, block * wide, wide)
        named = jnp.where(face + block * RANK_BLOCK < live, named, -1)
        hits = jnp.where(owners == named, 1.0, 0.0)
        counted = jnp.dot(hits.astype(BF16), weights, preferred_element_type=F32)
        rank = jnp.sum(hits * (counted[:, :RANK_BLOCK] + base), axis=0, keepdims=True)
        base = base + counted[:, RANK_BLOCK:]
        for i in range(wide):
            facts[3, block * wide + i : block * wide + i + 1, :] = rank[
                :, i * LANES : (i + 1) * LANES
            ]


def sort_faces(
    count_ref, owner_ref, cell_ref, area_ref, target_ref, order, starts, targets, facts, grid
):
    live = count_ref[0]
    cell = cell_ref[...]
    target = target_ref[...] + 1
    row, column = cell >> 13, cell & (COLS - 1)
    cell_row = row * TILES + ((column >> 7) & 7) * TILE + (column >> 10)
    number = (
        lax.broadcasted_iota(I32, (FACE_ROWS, LANES), 0) * LANES
        + lax.broadcasted_iota(I32, (FACE_ROWS, LANES), 1)
    )
    bucket = jnp.where(number < live, cell_row >> 8, -1)
    facts[0] = (cell_row & (BUCKET - 1)).astype(F32)
    facts[1] = (column & (LANES - 1)).astype(F32)
    owner = owner_ref[...]
    facts[2] = jnp.where(number < live, owner & (HALF - 1), -1).astype(F32)
    facts[3] = facts[3] + ((owner >> 6) * RANKS).astype(F32)
    facts[4], facts[5] = halves(area_ref[...] * (1.0 / SUBSTEPS))
    for i in range(3):
        facts[6 + i] = ((target >> (7 * i)) & (LANES - 1)).astype(F32)
    facts[9], facts[10] = block_and_lane(bucket_places(bucket, FACE_ROWS, starts))

    order[...] = jnp.zeros_like(order)
    grid[...] = jnp.zeros_like(grid)
    by_lane = indices(BLOCK, LINE)
    by_block = indices(PLANNED, LINE)
    by_half = indices(HALF, LINE)
    wide = LINE // LANES

    @pl.loop(0, FACES // LINE, unroll=2)
    def _(step):
        fact = [lines(facts.at[i], step * wide, wide) for i in range(11)]
        order[...] += product(spread(by_block, fact[9], fact[:6]), one_hot(by_lane, fact[10]))
        grid[...] += product(spread(by_half, fact[2], fact[6:9]), one_hot(by_lane, fact[3]))

    targets[...] = by_owner(
        grid[:HALF]
        + grid[HALF : 2 * HALF] * float(LANES)
        + grid[2 * HALF :] * float(LANES * LANES)
    )


def pick_faces(total_ref, order_ref, starts_ref, targets_ref, ready, turned, slots):
    for part in range(3):
        for block in range(CELL_ROWS // LANES):
            high, low = halves(total_ref[part, 2 * block : 2 * block + 2].reshape(LANES, LANES).T)
            bucket = block * LANES // BUCKET
            columns = slice(block * LANES % BUCKET, block * LANES % BUCKET + LANES)
            turned[bucket, 2 * part * LANES : (2 * part + 1) * LANES, columns] = high.astype(BF16)
            turned[bucket, (2 * part + 1) * LANES : (2 * part + 2) * LANES, columns] = low.astype(
                BF16
            )
    slots[...] = jnp.zeros_like(slots)
    by_row = indices(BUCKET, BLOCK)
    lane = lax.broadcasted_iota(I32, (LANES, BLOCK), 0).astype(F32)
    by_half = indices(HALF, BLOCK * TOGETHER)
    by_rank = indices(2 * RANKS, BLOCK * TOGETHER)

    @pl.loop(0, (FACES // BLOCK + BUCKETS) // TOGETHER, unroll=9)
    def _(step):
        surface = []
        placed = []
        for i in range(TOGETHER):
            block = step * TOGETHER + i
            row, where, owner, rank, high, low = (
                order_ref[pl.ds(part * PLANNED + block, 1), :] for part in range(6)
            )
            found = jnp.dot(
                turned[bucket_of(block, starts_ref)],
                one_hot(by_row, row),
                preferred_element_type=F32,
            )
            is_lane = lane == where
            parts = []
            for part in range(3):
                both = (
                    found[2 * part * LANES : (2 * part + 1) * LANES]
                    + found[(2 * part + 1) * LANES : (2 * part + 2) * LANES]
                )
                value = jnp.sum(jnp.where(is_lane, both, 0.0), axis=0, keepdims=True)
                parts.extend(halves(value * (high + low)))
            surface.append(parts)
            placed.append((owner, rank))
        joined = [jnp.concatenate(part, axis=1) for part in zip(*surface)]
        owner, rank = (jnp.concatenate(part, axis=1) for part in zip(*placed))
        slots[...] += product(spread(by_half, owner, joined), one_hot(by_rank, rank))

    for part in range(3):
        first = 2 * part * HALF
        ready[:, part, :] = by_owner(
            slots[first : first + HALF] + slots[first + HALF : first + 2 * HALF]
        )
    ready[:, 3, :] = targets_ref[...]


def fields_kernel(
    les_ref,
    les_density_ref,
    far_ref,
    far_density_ref,
    count_ref,
    owner_ref,
    cell_ref,
    area_ref,
    target_ref,
    les_out,
    stepped_out,
    arrived,
    les_tiles,
    stepped_tiles,
    out_sem,
    total_out,
    state,
    advanced,
    inverse,
    far,
    far_inverse,
    flat,
    send_sem,
    recv_sem,
    inverse_send,
    inverse_recv,
    far_send,
    far_recv,
    order,
    starts,
    targets,
    facts,
    grid,
    ready,
    turned,
    slots,
    local_sem,
    faces_send,
    faces_recv,
    greeted,
):
    dom = lax.axis_index("dom")
    doms = lax.axis_size("dom")
    has_up = dom > 0
    has_down = dom < doms - 1
    up = lax.rem(dom + doms - 1, doms)
    down = lax.rem(dom + 1, doms)
    lane = lax.broadcasted_iota(I32, (TILES, LANES), 1)
    step = TIME_STEP / 12.0

    sec = lax.axis_index("sec")
    secs = lax.axis_size("sec")
    devices = secs * doms
    me = sec * doms + dom
    barrier = pltpu.get_barrier_semaphore()

    def for_others(act):
        for ahead in range(secs):
            there = lax.rem(sec + ahead, secs)

            @pl.loop(0 if ahead else 1, doms, unroll=8 if ahead else doms - 1)
            def _(along):
                where = lax.rem(dom + along, doms)
                act(there * doms + where, {"sec": there, "dom": where})

    def greet(distance, semaphore):
        for by in (distance, devices - distance):
            other = lax.rem(me + by, devices)
            pl.semaphore_signal(
                semaphore,
                inc=1,
                device_id={"sec": other // doms, "dom": lax.rem(other, doms)},
                device_id_type=MESH,
            )

    def pass_on(number):
        pl.semaphore_wait(greeted.at[number], 2)
        if number + 1 < GREETINGS:
            greet(2 << number, greeted.at[number + 1])

    greet(1, barrier)

    def remote(ref, first, count, landing, sems, where):
        return pltpu.make_async_remote_copy(
            src_ref=ref.at[pl.ds(first, count)],
            dst_ref=ref.at[pl.ds(landing, count)],
            send_sem=sems[0],
            recv_sem=sems[1],
            device_id={"dom": where},
            device_id_type=MESH,
        )

    def up_copy(number):
        sems = (send_sem.at[number, 0], recv_sem.at[number, 0])
        near = number == 0
        first, landing = (6, ROWS + 6) if near else (9, ROWS + 9)
        return remote(state.at[0 if near else number - 1], first, 3, landing, sems, up)

    def down_copy(number):
        sems = (send_sem.at[number, 1], recv_sem.at[number, 1])
        near = number == 0
        first, landing = (ROWS + 3, 3) if near else (ROWS, 0)
        return remote(state.at[0 if near else number - 1], first, 3, landing, sems, down)

    def inverse_up():
        return remote(inverse, 4, 4, ROWS + 4, (inverse_send.at[0], inverse_recv.at[0]), up)

    def inverse_down():
        return remote(inverse, ROWS, 4, 0, (inverse_send.at[1], inverse_recv.at[1]), down)

    def far_up():
        return remote(far, 2, 2, ROWS + 2, (far_send.at[0], far_recv.at[0]), up)

    def far_down():
        return remote(far, ROWS, 2, 0, (far_send.at[1], far_recv.at[1]), down)

    @pl.when(jnp.logical_not(has_up))
    def _():
        for sub in range(SUBSTEPS):
            state[sub, 0:6] = jnp.zeros((6, 3, TILES, LANES), F32)
        advanced[0:4] = jnp.zeros((4, 3, TILES, LANES), F32)
        far[0:2] = jnp.zeros((2, 3, TILES, LANES), F32)

    @pl.when(jnp.logical_not(has_down))
    def _():
        for sub in range(SUBSTEPS):
            state[sub, ROWS + 6 :] = jnp.zeros((6, 3, TILES, LANES), F32)
        advanced[ROWS + 4 :] = jnp.zeros((4, 3, TILES, LANES), F32)
        far[ROWS + 2 : ROWS + 4] = jnp.zeros((2, 3, TILES, LANES), F32)

    def convert_state(source, target, offset):
        @pl.loop(0, 6)
        def _(index):
            part, rows8 = index // 2, index % 2

            def load(block):
                return source[part, pl.ds(rows8 * TILE, TILE), block * LANES : (block + 1) * LANES]

            def store(row, reg, value):
                target[offset + row, part, reg * TILE : (reg + 1) * TILE, :] = value

            rows_from_tiles(load, flat, store, rows8)

    def convert_density(source, target, offset):
        @pl.loop(0, 2)
        def _(rows8):
            def load(block):
                return 1.0 / source[pl.ds(rows8 * TILE, TILE), block * LANES : (block + 1) * LANES]

            def store(row, reg, value):
                target[offset + row, reg * TILE : (reg + 1) * TILE, :] = value

            rows_from_tiles(load, flat, store, rows8)

    def advance(sub, row):
        base = row + 6
        u, v, p = (state[sub, base, part] for part in range(3))
        dx = [
            difference(*(state[sub, base + by, part] for by in (-2, -1, 1, 2)))
            for part in range(3)
        ]
        dy = [across(field, lane) for field in (u, v, p)]
        inv = inverse[row + 4]
        rate_u = u * dx[0] + v * dy[0] + inv * dx[2]
        rate_v = u * dx[1] + v * dy[1] + inv * dy[2]
        rate_p = u * dx[2] + v * dy[2] + LES_STIFF * (dx[0] + dy[1])
        return u - step * rate_u, v - step * rate_v, p - step * rate_p

    def put_advanced(row, fields):
        for part in range(3):
            advanced[row + 4, part] = fields[part]

    def advance_rows(sub, low, high):
        loop(low, high, lambda row: put_advanced(row, advance(sub, row)))

    def smooth(sub, row, own):
        for part in range(3):
            centre = advanced[row + 4, part]
            lateral = advanced[row + 3, part] + advanced[row + 5, part]
            sides = shifted(centre, 1, lane) + shifted(centre, -1, lane)
            value = (1.0 - FILTER_WEIGHT) * centre + FILTER_WEIGHT / 4.0 * (lateral + sides)
            state[sub + 1, row + 6, part] = value
            if own:
                if sub == 0:
                    total_out[part, row] = value
                else:
                    total_out[part, row] += value

    def smooth_rows(sub, low, high, own=True):
        loop(low, high, lambda row: smooth(sub, row, own))

    def far_row(row):
        base = row + 2
        u, v, p = (far[base, part] for part in range(3))
        dx = [
            difference(*(far[base + by, part] for by in (-2, -1, 1, 2))) for part in range(3)
        ]
        inv = far_inverse[row]
        dy_v, dy_p = across(v, lane), across(p, lane)
        far[base + ROWS + 4, 0] = u - step * (MEAN_FLOW * dx[0] + inv * dx[2])
        far[base + ROWS + 4, 1] = v - step * (MEAN_FLOW * dx[1] + inv * dy_p)
        far[base + ROWS + 4, 2] = p - step * (MEAN_FLOW * dx[2] + FAR_STIFF * (dx[0] + dy_v))

    def loop(low, high, body):
        @pl.loop(low, high, unroll=UNROLL.get(high - low, high - low))
        def _(row):
            body(row)

    def write_tiles(source, target):
        @pl.loop(0, 6)
        def _(index):
            part, rows8 = index // 2, index % 2

            def load(row, reg):
                return source(row, part, reg)

            def store(block, value):
                target[part, pl.ds(rows8 * TILE, TILE), block * LANES : (block + 1) * LANES] = value

            tiles_from_rows(load, flat, store, rows8)

    convert_state(les_ref, state.at[0], 6)
    convert_density(les_density_ref, inverse, 4)

    pl.semaphore_wait(barrier, 2)
    greet(1, greeted.at[0])

    @pl.when(has_up)
    def _():
        up_copy(0).start()
        inverse_up().start()
        up_copy(1).start()

    @pl.when(has_down)
    def _():
        down_copy(0).start()
        inverse_down().start()
        down_copy(1).start()

    for sub in range(SUBSTEPS):
        advance_rows(sub, 2, ROWS - 2)
        smooth_rows(sub, 3, ROWS - 3)

        if sub + 2 < SUBSTEPS:

            @pl.when(has_up)
            def _():
                up_copy(sub + 2).start()

            @pl.when(has_down)
            def _():
                down_copy(sub + 2).start()

        if sub + 2 == SUBSTEPS:

            @pl.when(has_up)
            def _():
                far_up().start()

            @pl.when(has_down)
            def _():
                far_down().start()

        pass_on(sub)

        if sub == 0:
            convert_state(far_ref, far, 2)
            convert_density(far_density_ref, far_inverse, 0)
            rank_faces(count_ref, owner_ref, facts)
        if sub == 1:
            sort_faces(
                count_ref,
                owner_ref,
                cell_ref,
                area_ref,
                target_ref,
                order,
                starts,
                targets,
                facts,
                grid,
            )
        if sub == 2:
            loop(2, ROWS - 2, far_row)

        @pl.when(has_up)
        def _():
            down_copy(sub).wait_recv()
            if sub == 0:
                inverse_down().wait_recv()
            else:
                advance_rows(sub - 1, -4, -1)
                smooth_rows(sub - 1, -3, 0, own=False)
            put_advanced(-1, advance(sub, -1))

        @pl.when(has_down)
        def _():
            up_copy(sub).wait_recv()
            if sub == 0:
                inverse_up().wait_recv()
            else:
                advance_rows(sub - 1, ROWS + 1, ROWS + 4)
                smooth_rows(sub - 1, ROWS, ROWS + 3, own=False)
            put_advanced(ROWS, advance(sub, ROWS))

        advance_rows(sub, 0, 2)
        advance_rows(sub, ROWS - 2, ROWS)
        smooth_rows(sub, 0, 3)
        smooth_rows(sub, ROWS - 3, ROWS)

    pick_faces(total_out, order, starts, targets, ready, turned, slots)
    pass_on(GREETINGS - 1)
    own = pltpu.make_async_copy(ready.at[me], arrived.at[me], local_sem)
    own.start()

    for_others(
        lambda other, where: pltpu.make_async_remote_copy(
            src_ref=ready.at[other],
            dst_ref=arrived.at[me],
            send_sem=faces_send,
            recv_sem=faces_recv,
            device_id=where,
            device_id_type=MESH,
        ).start()
    )

    write_tiles(
        lambda row, part, reg: state[SUBSTEPS, row + 6, part, reg * TILE : (reg + 1) * TILE, :],
        les_tiles,
    )
    les_copy = pltpu.make_async_copy(les_tiles, les_out, out_sem.at[0])
    les_copy.start()

    @pl.when(has_up)
    def _():
        far_down().wait_recv()

    @pl.when(has_down)
    def _():
        far_up().wait_recv()

    loop(0, 2, far_row)
    loop(ROWS - 2, ROWS, far_row)
    write_tiles(
        lambda row, part, reg: far[row + ROWS + 6, part, reg * TILE : (reg + 1) * TILE, :],
        stepped_tiles,
    )
    stepped_copy = pltpu.make_async_copy(stepped_tiles, stepped_out, out_sem.at[1])
    stepped_copy.start()

    @pl.when(has_up)
    def _():
        for sub in range(SUBSTEPS):
            up_copy(sub).wait_send()
        inverse_up().wait_send()
        far_up().wait_send()

    @pl.when(has_down)
    def _():
        for sub in range(SUBSTEPS):
            down_copy(sub).wait_send()
        inverse_down().wait_send()
        far_down().wait_send()

    own.wait()
    les_copy.wait()
    stepped_copy.wait()
    all_but_one = pl.ds(0, devices - 1)
    pltpu.make_async_copy(arrived.at[all_but_one], arrived.at[all_but_one], faces_recv).wait()
    pltpu.make_async_copy(ready.at[all_but_one], ready.at[all_but_one], faces_send).wait()


def fields(les_state, les_density, far_state, far_density, counts, owner, cell, area, target):
    block = jax.ShapeDtypeStruct((3, ROWS, COLS), F32)
    dma = pltpu.SemaphoreType.DMA
    return pl.pallas_call(
        fields_kernel,
        out_shape=(block, block, jax.ShapeDtypeStruct((DEVICES, 4, RANKS), F32)),
        in_specs=[VMEM] * 4 + [SMEM] + [VMEM] * 4,
        out_specs=(HBM, HBM, VMEM),
        scratch_shapes=[
            pltpu.VMEM((3, ROWS, COLS), F32),
            pltpu.VMEM((3, ROWS, COLS), F32),
            dma((2,)),
            pltpu.VMEM((3, ROWS, TILES, LANES), F32),
            pltpu.VMEM((SUBSTEPS + 1, ROWS + 12, 3, TILES, LANES), F32),
            pltpu.VMEM((ROWS + 8, 3, TILES, LANES), F32),
            pltpu.VMEM((ROWS + 8, TILES, LANES), F32),
            pltpu.VMEM((2 * ROWS + 6, 3, TILES, LANES), F32),
            pltpu.VMEM((ROWS, TILES, LANES), F32),
            pltpu.VMEM((TILES * TILE, LANES), F32),
            dma((SUBSTEPS, 2)),
            dma((SUBSTEPS, 2)),
            dma((2,)),
            dma((2,)),
            dma((2,)),
            dma((2,)),
            pltpu.VMEM((6 * PLANNED, BLOCK), F32),
            pltpu.SMEM((BUCKETS + 1,), I32),
            pltpu.VMEM((DEVICES, RANKS), F32),
            pltpu.VMEM((11, FACE_ROWS, LANES), F32),
            pltpu.VMEM((3 * HALF, 2 * RANKS), F32),
            pltpu.VMEM((DEVICES, 4, RANKS), F32),
            pltpu.VMEM((BUCKETS, 6 * LANES, BUCKET), BF16),
            pltpu.VMEM((6 * HALF, 2 * RANKS), F32),
            dma,
            dma,
            dma,
            pltpu.SemaphoreType.REGULAR((GREETINGS,)),
        ],
        compiler_params=params(collective_id=0, has_side_effects=True),
        name="fields",
    )(les_state, les_density, far_state, far_density, counts, owner, cell, area, target)


def add_kernel(arrived_ref, stepped_ref, out, held, order, sums, starts):
    for part in range(3):
        held[2 * part], held[2 * part + 1] = halves(
            arrived_ref[pl.ds(part, DEVICES, stride=4), :]
        )
    target = arrived_ref[pl.ds(3, DEVICES, stride=4), :].astype(I32) - 1
    row, column = target >> 13, target & (COLS - 1)
    cell_row = ((row >> 3) * TILES + (column >> 7)) * TILE + (row & 7)
    bucket = jnp.where(target >= 0, cell_row >> 8, -1)
    held[6] = (cell_row & (BUCKET - 1)).astype(F32)
    held[7] = (column & (LANES - 1)).astype(F32)
    share = DEVICES // GROUPS
    for group in range(GROUPS):
        rows = slice(group * share, (group + 1) * share)
        held[8, rows], held[9, rows] = block_and_lane(
            bucket_places(bucket[rows], share, starts.at[group])
        )
    order[...] = jnp.zeros_like(order)
    sums[...] = jnp.zeros_like(sums)
    by_lane = indices(BLOCK, LINE)
    by_block = indices(SORTED, LINE)
    wide = LINE // LANES

    for group in range(GROUPS):

        @pl.loop(0, share // wide, unroll=4)
        def _(step):
            fact = [lines(held.at[i], group * share + step * wide, wide) for i in range(10)]
            order[group] += product(spread(by_block, fact[8], fact[:8]), one_hot(by_lane, fact[9]))

    by_row = indices(BUCKET, BLOCK)
    by_column = indices(LANES, BLOCK)

    for group in range(GROUPS):

        @pl.loop(0, steps_of(starts.at[group]))
        def _(step):
            for i in range(TOGETHER):
                block = step * TOGETHER + i
                *parts, row, column = (
                    order[group, pl.ds(part * SORTED + block, 1), :] for part in range(8)
                )
                here = folded(by_column, column, parts, one_hot(by_row, row))
                sums[bucket_of(block, starts.at[group])] += here

    for part in range(3):
        for bucket in range(BUCKETS):
            for half in range(BUCKET // LANES):
                cells = sums[
                    bucket,
                    part * LANES : (part + 1) * LANES,
                    half * LANES : (half + 1) * LANES,
                ].T
                for tile in range(LANES // TILE):
                    number = (bucket * BUCKET + half * LANES) // TILE + tile
                    rows = slice(number // TILES * TILE, (number // TILES + 1) * TILE)
                    columns = slice(number % TILES * LANES, (number % TILES + 1) * LANES)
                    out[part, rows, columns] = (
                        stepped_ref[part, rows, columns] + cells[tile * TILE : (tile + 1) * TILE]
                    )


def add(arrived, stepped):
    return pl.pallas_call(
        add_kernel,
        out_shape=jax.ShapeDtypeStruct((3, ROWS, COLS), F32),
        in_specs=[VMEM] * 2,
        out_specs=VMEM,
        scratch_shapes=[
            pltpu.VMEM((10, DEVICES, RANKS), F32),
            pltpu.VMEM((GROUPS, 8 * SORTED, BLOCK), F32),
            pltpu.VMEM((BUCKETS, 3 * LANES, BUCKET), F32),
            pltpu.SMEM((GROUPS, BUCKETS + 1), I32),
        ],
        compiler_params=params(),
        name="add",
    )(arrived, stepped)


def local(
    les_state,
    les_density,
    far_state,
    far_density,
    face_cell,
    face_area,
    face_owner,
    face_counts,
    face_target,
):
    cell, area, owner, target = (
        array.reshape(FACE_ROWS, LANES) for array in (face_cell, face_area, face_owner, face_target)
    )
    les_final, stepped, arrived = fields(
        les_state[0],
        les_density[0],
        far_state[0],
        far_density[0],
        face_counts,
        owner,
        cell,
        area,
        target,
    )
    far_final = add(arrived.reshape(4 * DEVICES, LANES), stepped)
    return les_final[None], far_final[None]


def solution(mesh):
    field = P("sec", None, "dom", None)
    density = P("sec", "dom", None)
    faces = P(("sec", "dom"))
    return jax.shard_map(
        local,
        mesh=mesh,
        in_specs=(field, density, field, density) + (faces,) * 5,
        out_specs=(field, field),
        check_vma=False,
    )
```

```python
import jax
import jax.numpy as jnp
from jax import lax
from jax.experimental import pallas as pl
from jax.experimental.pallas import tpu as pltpu
from jax.sharding import PartitionSpec as P

SUBSTEPS = 5
UNROLL = {12: 4, 10: 5}
TIME_STEP = 0.1
LES_STIFF = 1.0
FAR_STIFF = 1.0
FILTER_WEIGHT = 0.5
MEAN_FLOW = 0.3

LANES = 128
TILE = 8
ROWS = 16
COLS = 8192
TILES = COLS // LANES
GREETINGS = SUBSTEPS + 1
REGS = TILES // TILE
FACES = 8192
FACE_ROWS = FACES // LANES
DEVICES = 128
RANKS = 128
CELL_ROWS = ROWS * COLS // LANES

MESH = pl.DeviceIdType.MESH
VMEM = pl.BlockSpec(memory_space=pltpu.VMEM)
HBM = pl.BlockSpec(memory_space=pl.ANY)
SMEM = pl.BlockSpec(memory_space=pltpu.SMEM)
F32 = jnp.float32
BF16 = jnp.bfloat16
I32 = jnp.int32


def params(**more):
    return pltpu.CompilerParams(vmem_limit_bytes=56 * 1024 * 1024, **more)


def rows_from_tiles(load, flat, store, rows8):
    for block in range(TILES):
        flat[block * TILE : (block + 1) * TILE, :] = load(block)
    for row in range(TILE):
        for reg in range(REGS):
            store(rows8 * TILE + row, reg, flat[pl.ds(TILE * reg + row, TILE, stride=TILES), :])


def tiles_from_rows(load, flat, store, rows8):
    for row in range(TILE):
        for reg in range(REGS):
            flat[pl.ds(TILE * reg + row, TILE, stride=TILES), :] = load(rows8 * TILE + row, reg)
    for block in range(TILES):
        store(block, flat[block * TILE : (block + 1) * TILE, :])


def shifted(row, by, lane):
    if by > 0:
        turned = pltpu.roll(row, LANES - by, 1)
        crossed = jnp.concatenate([turned[TILE:], pltpu.roll(turned[:TILE], TILE - 1, 0)], axis=0)
        return jnp.where(lane >= LANES - by, crossed, turned)
    turned = pltpu.roll(row, -by, 1)
    crossed = jnp.concatenate(
        [pltpu.roll(turned[TILES - TILE :], 1, 0), turned[: TILES - TILE]], axis=0
    )
    return jnp.where(lane < -by, crossed, turned)


def difference(far_left, left, right, far_right):
    return 8.0 * (right - left) - (far_right - far_left)


def across(row, lane):
    return difference(
        shifted(row, -2, lane), shifted(row, -1, lane), shifted(row, 1, lane), shifted(row, 2, lane)
    )


RANK_BLOCK = 256
BUCKETS = 4
BUCKET = CELL_ROWS // BUCKETS
BLOCK = 256
LINE = 512
TOGETHER = 4
HALF = DEVICES // 2
PLANNED = 48
GROUPS = 2
SORTED = 48


def halves(values):
    high = values.astype(BF16).astype(F32)
    return high, values - high


def indices(rows, columns):
    return lax.broadcasted_iota(I32, (rows, columns), 0).astype(F32).astype(BF16)


def one_hot(index, line):
    return jnp.where(index == line.astype(BF16), jnp.ones((), BF16), jnp.zeros((), BF16))


def spread(index, line, parts):
    here = index == line.astype(BF16)
    return jnp.concatenate(
        [jnp.where(here, part.astype(BF16), jnp.zeros((), BF16)) for part in parts], axis=0
    )


def product(left, right):
    return lax.dot_general(left, right, (((1,), (1,)), ((), ())), preferred_element_type=F32)


def folded(index, line, parts, right):
    return product(
        jnp.concatenate([spread(index, line, parts[0::2]), spread(index, line, parts[1::2])], axis=1),
        jnp.concatenate([right, right], axis=1),
    )


def lines(ref, first, count):
    return jnp.concatenate([ref[pl.ds(first + i, 1), :] for i in range(count)], axis=1)


def bucket_places(bucket, rows, starts_ref):
    before = lax.broadcasted_iota(I32, (LANES, 2 * LANES), 0)
    after = lax.broadcasted_iota(I32, (LANES, 2 * LANES), 1)
    weights = jnp.where((before < after) | (after >= LANES), 1.0, 0.0).astype(BF16)
    below = lax.broadcasted_iota(I32, (rows, rows), 0) > lax.broadcasted_iota(I32, (rows, rows), 1)
    below = jnp.where(below, 1.0, 0.0).astype(BF16)
    place = jnp.full((rows, LANES), -1.0, F32)
    base = jnp.zeros((1, LANES), F32)
    for b in range(BUCKETS):
        starts_ref[b] = jnp.max(base).astype(I32)
        here = bucket == b
        counted = jnp.dot(
            jnp.where(here, 1.0, 0.0).astype(BF16), weights, preferred_element_type=F32
        )
        totals = counted[:, LANES:]
        offset = jnp.dot(below, totals.astype(BF16), preferred_element_type=F32)
        place = jnp.where(here, counted[:, :LANES] + offset + base * float(BLOCK), place)
        total = offset[rows - 1 :] + totals[rows - 1 :]
        base = base + jnp.floor((total + (BLOCK - 1.0)) * (1.0 / BLOCK))
    starts_ref[BUCKETS] = jnp.max(base).astype(I32)
    return place


def block_and_lane(place):
    block = jnp.floor(place * (1.0 / BLOCK))
    return block, place - block * float(BLOCK)


def by_owner(halved):
    return jnp.concatenate([halved[:, :RANKS], halved[:, RANKS:]], axis=0)


def bucket_of(block, starts_ref):
    bucket = 0
    for b in range(1, BUCKETS):
        bucket = bucket + jnp.where(block >= starts_ref[b], 1, 0)
    return bucket


def steps_of(starts_ref):
    return (starts_ref[BUCKETS] + TOGETHER - 1) // TOGETHER


def rank_faces(count_ref, owner_ref, facts):
    live = count_ref[0]
    owners = lax.broadcasted_iota(I32, (DEVICES, RANK_BLOCK), 0)
    before = lax.broadcasted_iota(I32, (RANK_BLOCK, RANK_BLOCK), 0)
    after = lax.broadcasted_iota(I32, (RANK_BLOCK, RANK_BLOCK), 1)
    weights = jnp.concatenate(
        [
            jnp.where(before < after, 1.0, 0.0).astype(BF16),
            jnp.ones((RANK_BLOCK, RANK_BLOCK), BF16),
        ],
        axis=1,
    )
    face = lax.broadcasted_iota(I32, (1, RANK_BLOCK), 1)
    base = jnp.zeros((DEVICES, RANK_BLOCK), F32)
    wide = RANK_BLOCK // LANES
    for block in range(FACES // RANK_BLOCK):
        named = lines(owner_ref, block * wide, wide)
        named = jnp.where(face + block * RANK_BLOCK < live, named, -1)
        hits = jnp.where(owners == named, 1.0, 0.0)
        counted = jnp.dot(hits.astype(BF16), weights, preferred_element_type=F32)
        rank = jnp.sum(hits * (counted[:, :RANK_BLOCK] + base), axis=0, keepdims=True)
        base = base + counted[:, RANK_BLOCK:]
        for i in range(wide):
            facts[3, block * wide + i : block * wide + i + 1, :] = rank[
                :, i * LANES : (i + 1) * LANES
            ]


def sort_faces(
    count_ref, owner_ref, cell_ref, area_ref, target_ref, order, starts, targets, facts, grid
):
    live = count_ref[0]
    cell = cell_ref[...]
    target = target_ref[...] + 1
    row, column = cell >> 13, cell & (COLS - 1)
    cell_row = row * TILES + ((column >> 7) & 7) * TILE + (column >> 10)
    number = (
        lax.broadcasted_iota(I32, (FACE_ROWS, LANES), 0) * LANES
        + lax.broadcasted_iota(I32, (FACE_ROWS, LANES), 1)
    )
    bucket = jnp.where(number < live, cell_row >> 8, -1)
    facts[0] = (cell_row & (BUCKET - 1)).astype(F32)
    facts[1] = (column & (LANES - 1)).astype(F32)
    owner = owner_ref[...]
    facts[2] = jnp.where(number < live, owner & (HALF - 1), -1).astype(F32)
    facts[3] = facts[3] + ((owner >> 6) * RANKS).astype(F32)
    facts[4], facts[5] = halves(area_ref[...] * (1.0 / SUBSTEPS))
    for i in range(3):
        facts[6 + i] = ((target >> (7 * i)) & (LANES - 1)).astype(F32)
    facts[9], facts[10] = block_and_lane(bucket_places(bucket, FACE_ROWS, starts))

    order[...] = jnp.zeros_like(order)
    grid[...] = jnp.zeros_like(grid)
    by_lane = indices(BLOCK, LINE)
    by_block = indices(PLANNED, LINE)
    by_half = indices(HALF, LINE)
    wide = LINE // LANES

    @pl.loop(0, FACES // LINE, unroll=2)
    def _(step):
        fact = [lines(facts.at[i], step * wide, wide) for i in range(11)]
        order[...] += product(spread(by_block, fact[9], fact[:6]), one_hot(by_lane, fact[10]))
        grid[...] += product(spread(by_half, fact[2], fact[6:9]), one_hot(by_lane, fact[3]))

    targets[...] = by_owner(
        grid[:HALF]
        + grid[HALF : 2 * HALF] * float(LANES)
        + grid[2 * HALF :] * float(LANES * LANES)
    )


def pick_faces(total_ref, order_ref, starts_ref, targets_ref, ready, turned, slots):
    for part in range(3):
        for block in range(CELL_ROWS // LANES):
            high, low = halves(total_ref[part, 2 * block : 2 * block + 2].reshape(LANES, LANES).T)
            bucket = block * LANES // BUCKET
            columns = slice(block * LANES % BUCKET, block * LANES % BUCKET + LANES)
            turned[bucket, 2 * part * LANES : (2 * part + 1) * LANES, columns] = high.astype(BF16)
            turned[bucket, (2 * part + 1) * LANES : (2 * part + 2) * LANES, columns] = low.astype(
                BF16
            )
    slots[...] = jnp.zeros_like(slots)
    by_row = indices(BUCKET, BLOCK)
    lane = lax.broadcasted_iota(I32, (LANES, BLOCK), 0).astype(F32)
    by_half = indices(HALF, BLOCK * TOGETHER)
    by_rank = indices(2 * RANKS, BLOCK * TOGETHER)

    @pl.loop(0, (FACES // BLOCK + BUCKETS) // TOGETHER, unroll=9)
    def _(step):
        surface = []
        placed = []
        for i in range(TOGETHER):
            block = step * TOGETHER + i
            row, where, owner, rank, high, low = (
                order_ref[pl.ds(part * PLANNED + block, 1), :] for part in range(6)
            )
            found = jnp.dot(
                turned[bucket_of(block, starts_ref)],
                one_hot(by_row, row),
                preferred_element_type=F32,
            )
            is_lane = lane == where
            parts = []
            for part in range(3):
                both = (
                    found[2 * part * LANES : (2 * part + 1) * LANES]
                    + found[(2 * part + 1) * LANES : (2 * part + 2) * LANES]
                )
                value = jnp.sum(jnp.where(is_lane, both, 0.0), axis=0, keepdims=True)
                parts.extend(halves(value * (high + low)))
            surface.append(parts)
            placed.append((owner, rank))
        joined = [jnp.concatenate(part, axis=1) for part in zip(*surface)]
        owner, rank = (jnp.concatenate(part, axis=1) for part in zip(*placed))
        slots[...] += product(spread(by_half, owner, joined), one_hot(by_rank, rank))

    for part in range(3):
        first = 2 * part * HALF
        ready[:, part, :] = by_owner(
            slots[first : first + HALF] + slots[first + HALF : first + 2 * HALF]
        )
    ready[:, 3, :] = targets_ref[...]


def fields_kernel(
    les_ref,
    les_density_ref,
    far_ref,
    far_density_ref,
    count_ref,
    owner_ref,
    cell_ref,
    area_ref,
    target_ref,
    les_out,
    stepped_out,
    arrived,
    les_tiles,
    stepped_tiles,
    out_sem,
    total_out,
    state,
    advanced,
    inverse,
    far,
    far_inverse,
    flat,
    send_sem,
    recv_sem,
    inverse_send,
    inverse_recv,
    far_send,
    far_recv,
    order,
    starts,
    targets,
    facts,
    grid,
    ready,
    turned,
    slots,
    local_sem,
    faces_send,
    faces_recv,
    greeted,
):
    dom = lax.axis_index("dom")
    doms = lax.axis_size("dom")
    has_up = dom > 0
    has_down = dom < doms - 1
    up = lax.rem(dom + doms - 1, doms)
    down = lax.rem(dom + 1, doms)
    lane = lax.broadcasted_iota(I32, (TILES, LANES), 1)
    step = TIME_STEP / 12.0

    sec = lax.axis_index("sec")
    secs = lax.axis_size("sec")
    devices = secs * doms
    me = sec * doms + dom
    barrier = pltpu.get_barrier_semaphore()

    def for_others(act):
        for ahead in range(secs):
            there = lax.rem(sec + ahead, secs)

            @pl.loop(0 if ahead else 1, doms, unroll=8 if ahead else doms - 1)
            def _(along):
                where = lax.rem(dom + along, doms)
                act(there * doms + where, {"sec": there, "dom": where})

    def greet(distance, semaphore):
        for by in (distance, devices - distance):
            other = lax.rem(me + by, devices)
            pl.semaphore_signal(
                semaphore,
                inc=1,
                device_id={"sec": other // doms, "dom": lax.rem(other, doms)},
                device_id_type=MESH,
            )

    def pass_on(number):
        pl.semaphore_wait(greeted.at[number], 2)
        if number + 1 < GREETINGS:
            greet(2 << number, greeted.at[number + 1])

    greet(1, barrier)

    def remote(ref, first, count, landing, sems, where):
        return pltpu.make_async_remote_copy(
            src_ref=ref.at[pl.ds(first, count)],
            dst_ref=ref.at[pl.ds(landing, count)],
            send_sem=sems[0],
            recv_sem=sems[1],
            device_id={"dom": where},
            device_id_type=MESH,
        )

    def up_copy(number):
        sems = (send_sem.at[number, 0], recv_sem.at[number, 0])
        near = number == 0
        first, landing = (6, ROWS + 6) if near else (9, ROWS + 9)
        return remote(state.at[0 if near else number - 1], first, 3, landing, sems, up)

    def down_copy(number):
        sems = (send_sem.at[number, 1], recv_sem.at[number, 1])
        near = number == 0
        first, landing = (ROWS + 3, 3) if near else (ROWS, 0)
        return remote(state.at[0 if near else number - 1], first, 3, landing, sems, down)

    def inverse_up():
        return remote(inverse, 4, 4, ROWS + 4, (inverse_send.at[0], inverse_recv.at[0]), up)

    def inverse_down():
        return remote(inverse, ROWS, 4, 0, (inverse_send.at[1], inverse_recv.at[1]), down)

    def far_up():
        return remote(far, 2, 2, ROWS + 2, (far_send.at[0], far_recv.at[0]), up)

    def far_down():
        return remote(far, ROWS, 2, 0, (far_send.at[1], far_recv.at[1]), down)

    @pl.when(jnp.logical_not(has_up))
    def _():
        for sub in range(SUBSTEPS):
            state[sub, 0:6] = jnp.zeros((6, 3, TILES, LANES), F32)
        advanced[0:4] = jnp.zeros((4, 3, TILES, LANES), F32)
        far[0:2] = jnp.zeros((2, 3, TILES, LANES), F32)

    @pl.when(jnp.logical_not(has_down))
    def _():
        for sub in range(SUBSTEPS):
            state[sub, ROWS + 6 :] = jnp.zeros((6, 3, TILES, LANES), F32)
        advanced[ROWS + 4 :] = jnp.zeros((4, 3, TILES, LANES), F32)
        far[ROWS + 2 : ROWS + 4] = jnp.zeros((2, 3, TILES, LANES), F32)

    def convert_state(source, target, offset):
        @pl.loop(0, 6)
        def _(index):
            part, rows8 = index // 2, index % 2

            def load(block):
                return source[part, pl.ds(rows8 * TILE, TILE), block * LANES : (block + 1) * LANES]

            def store(row, reg, value):
                target[offset + row, part, reg * TILE : (reg + 1) * TILE, :] = value

            rows_from_tiles(load, flat, store, rows8)

    def convert_density(source, target, offset):
        @pl.loop(0, 2)
        def _(rows8):
            def load(block):
                return 1.0 / source[pl.ds(rows8 * TILE, TILE), block * LANES : (block + 1) * LANES]

            def store(row, reg, value):
                target[offset + row, reg * TILE : (reg + 1) * TILE, :] = value

            rows_from_tiles(load, flat, store, rows8)

    def advance(sub, row):
        base = row + 6
        u, v, p = (state[sub, base, part] for part in range(3))
        dx = [
            difference(*(state[sub, base + by, part] for by in (-2, -1, 1, 2)))
            for part in range(3)
        ]
        dy = [across(field, lane) for field in (u, v, p)]
        inv = inverse[row + 4]
        rate_u = u * dx[0] + v * dy[0] + inv * dx[2]
        rate_v = u * dx[1] + v * dy[1] + inv * dy[2]
        rate_p = u * dx[2] + v * dy[2] + LES_STIFF * (dx[0] + dy[1])
        return u - step * rate_u, v - step * rate_v, p - step * rate_p

    def put_advanced(row, fields):
        for part in range(3):
            advanced[row + 4, part] = fields[part]

    def advance_rows(sub, low, high):
        loop(low, high, lambda row: put_advanced(row, advance(sub, row)))

    def smooth(sub, row, own):
        for part in range(3):
            centre = advanced[row + 4, part]
            lateral = advanced[row + 3, part] + advanced[row + 5, part]
            sides = shifted(centre, 1, lane) + shifted(centre, -1, lane)
            value = (1.0 - FILTER_WEIGHT) * centre + FILTER_WEIGHT / 4.0 * (lateral + sides)
            state[sub + 1, row + 6, part] = value
            if own:
                if sub == 0:
                    total_out[part, row] = value
                else:
                    total_out[part, row] += value

    def smooth_rows(sub, low, high, own=True):
        loop(low, high, lambda row: smooth(sub, row, own))

    def far_row(row):
        base = row + 2
        u, v, p = (far[base, part] for part in range(3))
        dx = [
            difference(*(far[base + by, part] for by in (-2, -1, 1, 2))) for part in range(3)
        ]
        inv = far_inverse[row]
        dy_v, dy_p = across(v, lane), across(p, lane)
        far[base + ROWS + 4, 0] = u - step * (MEAN_FLOW * dx[0] + inv * dx[2])
        far[base + ROWS + 4, 1] = v - step * (MEAN_FLOW * dx[1] + inv * dy_p)
        far[base + ROWS + 4, 2] = p - step * (MEAN_FLOW * dx[2] + FAR_STIFF * (dx[0] + dy_v))

    def loop(low, high, body):
        @pl.loop(low, high, unroll=UNROLL.get(high - low, high - low))
        def _(row):
            body(row)

    def write_tiles(source, target):
        @pl.loop(0, 6)
        def _(index):
            part, rows8 = index // 2, index % 2

            def load(row, reg):
                return source(row, part, reg)

            def store(block, value):
                target[part, pl.ds(rows8 * TILE, TILE), block * LANES : (block + 1) * LANES] = value

            tiles_from_rows(load, flat, store, rows8)

    convert_state(les_ref, state.at[0], 6)
    convert_density(les_density_ref, inverse, 4)

    pl.semaphore_wait(barrier, 2)
    greet(1, greeted.at[0])

    @pl.when(has_up)
    def _():
        up_copy(0).start()
        inverse_up().start()
        up_copy(1).start()

    @pl.when(has_down)
    def _():
        down_copy(0).start()
        inverse_down().start()
        down_copy(1).start()

    for sub in range(SUBSTEPS):
        advance_rows(sub, 2, ROWS - 2)
        smooth_rows(sub, 3, ROWS - 3)

        if sub + 2 < SUBSTEPS:

            @pl.when(has_up)
            def _():
                up_copy(sub + 2).start()

            @pl.when(has_down)
            def _():
                down_copy(sub + 2).start()

        if sub + 2 == SUBSTEPS:

            @pl.when(has_up)
            def _():
                far_up().start()

            @pl.when(has_down)
            def _():
                far_down().start()

        pass_on(sub)

        if sub == 0:
            convert_state(far_ref, far, 2)
            convert_density(far_density_ref, far_inverse, 0)
            rank_faces(count_ref, owner_ref, facts)
        if sub == 1:
            sort_faces(
                count_ref,
                owner_ref,
                cell_ref,
                area_ref,
                target_ref,
                order,
                starts,
                targets,
                facts,
                grid,
            )
        if sub == 2:
            loop(2, ROWS - 2, far_row)

        @pl.when(has_up)
        def _():
            down_copy(sub).wait_recv()
            if sub == 0:
                inverse_down().wait_recv()
            else:
                advance_rows(sub - 1, -4, -1)
                smooth_rows(sub - 1, -3, 0, own=False)
            put_advanced(-1, advance(sub, -1))

        @pl.when(has_down)
        def _():
            up_copy(sub).wait_recv()
            if sub == 0:
                inverse_up().wait_recv()
            else:
                advance_rows(sub - 1, ROWS + 1, ROWS + 4)
                smooth_rows(sub - 1, ROWS, ROWS + 3, own=False)
            put_advanced(ROWS, advance(sub, ROWS))

        advance_rows(sub, 0, 2)
        advance_rows(sub, ROWS - 2, ROWS)
        smooth_rows(sub, 0, 3)
        smooth_rows(sub, ROWS - 3, ROWS)

    pick_faces(total_out, order, starts, targets, ready, turned, slots)
    pass_on(GREETINGS - 1)
    own = pltpu.make_async_copy(ready.at[me], arrived.at[me], local_sem)
    own.start()

    for_others(
        lambda other, where: pltpu.make_async_remote_copy(
            src_ref=ready.at[other],
            dst_ref=arrived.at[me],
            send_sem=faces_send,
            recv_sem=faces_recv,
            device_id=where,
            device_id_type=MESH,
        ).start()
    )

    write_tiles(
        lambda row, part, reg: state[SUBSTEPS, row + 6, part, reg * TILE : (reg + 1) * TILE, :],
        les_tiles,
    )
    les_copy = pltpu.make_async_copy(les_tiles, les_out, out_sem.at[0])
    les_copy.start()

    @pl.when(has_up)
    def _():
        far_down().wait_recv()

    @pl.when(has_down)
    def _():
        far_up().wait_recv()

    loop(0, 2, far_row)
    loop(ROWS - 2, ROWS, far_row)
    write_tiles(
        lambda row, part, reg: far[row + ROWS + 6, part, reg * TILE : (reg + 1) * TILE, :],
        stepped_tiles,
    )
    stepped_copy = pltpu.make_async_copy(stepped_tiles, stepped_out, out_sem.at[1])
    stepped_copy.start()

    @pl.when(has_up)
    def _():
        for sub in range(SUBSTEPS):
            up_copy(sub).wait_send()
        inverse_up().wait_send()
        far_up().wait_send()

    @pl.when(has_down)
    def _():
        for sub in range(SUBSTEPS):
            down_copy(sub).wait_send()
        inverse_down().wait_send()
        far_down().wait_send()

    own.wait()
    les_copy.wait()
    stepped_copy.wait()
    all_but_one = pl.ds(0, devices - 1)
    pltpu.make_async_copy(arrived.at[all_but_one], arrived.at[all_but_one], faces_recv).wait()
    pltpu.make_async_copy(ready.at[all_but_one], ready.at[all_but_one], faces_send).wait()


def fields(les_state, les_density, far_state, far_density, counts, owner, cell, area, target):
    block = jax.ShapeDtypeStruct((3, ROWS, COLS), F32)
    dma = pltpu.SemaphoreType.DMA
    return pl.pallas_call(
        fields_kernel,
        out_shape=(block, block, jax.ShapeDtypeStruct((DEVICES, 4, RANKS), F32)),
        in_specs=[VMEM] * 4 + [SMEM] + [VMEM] * 4,
        out_specs=(HBM, HBM, VMEM),
        scratch_shapes=[
            pltpu.VMEM((3, ROWS, COLS), F32),
            pltpu.VMEM((3, ROWS, COLS), F32),
            dma((2,)),
            pltpu.VMEM((3, ROWS, TILES, LANES), F32),
            pltpu.VMEM((SUBSTEPS + 1, ROWS + 12, 3, TILES, LANES), F32),
            pltpu.VMEM((ROWS + 8, 3, TILES, LANES), F32),
            pltpu.VMEM((ROWS + 8, TILES, LANES), F32),
            pltpu.VMEM((2 * ROWS + 6, 3, TILES, LANES), F32),
            pltpu.VMEM((ROWS, TILES, LANES), F32),
            pltpu.VMEM((TILES * TILE, LANES), F32),
            dma((SUBSTEPS, 2)),
            dma((SUBSTEPS, 2)),
            dma((2,)),
            dma((2,)),
            dma((2,)),
            dma((2,)),
            pltpu.VMEM((6 * PLANNED, BLOCK), F32),
            pltpu.SMEM((BUCKETS + 1,), I32),
            pltpu.VMEM((DEVICES, RANKS), F32),
            pltpu.VMEM((11, FACE_ROWS, LANES), F32),
            pltpu.VMEM((3 * HALF, 2 * RANKS), F32),
            pltpu.VMEM((DEVICES, 4, RANKS), F32),
            pltpu.VMEM((BUCKETS, 6 * LANES, BUCKET), BF16),
            pltpu.VMEM((6 * HALF, 2 * RANKS), F32),
            dma,
            dma,
            dma,
            pltpu.SemaphoreType.REGULAR((GREETINGS,)),
        ],
        compiler_params=params(collective_id=0, has_side_effects=True),
        name="fields",
    )(les_state, les_density, far_state, far_density, counts, owner, cell, area, target)


def add_kernel(
    arrived_ref,
    les_hbm,
    stepped_hbm,
    les_out,
    out,
    stepped_ref,
    les_held,
    held,
    order,
    sums,
    starts,
    copy_sem,
):
    les_copy = pltpu.make_async_copy(les_hbm, les_held, copy_sem.at[0])
    les_store = pltpu.make_async_copy(les_held, les_out, copy_sem.at[2])
    stepped_copy = pltpu.make_async_copy(stepped_hbm, stepped_ref, copy_sem.at[1])
    stepped_copy.start()
    les_copy.start()
    for part in range(3):
        held[2 * part], held[2 * part + 1] = halves(
            arrived_ref[pl.ds(part, DEVICES, stride=4), :]
        )
    target = arrived_ref[pl.ds(3, DEVICES, stride=4), :].astype(I32) - 1
    row, column = target >> 13, target & (COLS - 1)
    cell_row = ((row >> 3) * TILES + (column >> 7)) * TILE + (row & 7)
    bucket = jnp.where(target >= 0, cell_row >> 8, -1)
    held[6] = (cell_row & (BUCKET - 1)).astype(F32)
    held[7] = (column & (LANES - 1)).astype(F32)
    share = DEVICES // GROUPS
    for group in range(GROUPS):
        rows = slice(group * share, (group + 1) * share)
        held[8, rows], held[9, rows] = block_and_lane(
            bucket_places(bucket[rows], share, starts.at[group])
        )
    order[...] = jnp.zeros_like(order)
    sums[...] = jnp.zeros_like(sums)
    by_lane = indices(BLOCK, LINE)
    by_block = indices(SORTED, LINE)
    wide = LINE // LANES

    for group in range(GROUPS):

        @pl.loop(0, share // wide, unroll=8)
        def _(step):
            fact = [lines(held.at[i], group * share + step * wide, wide) for i in range(10)]
            order[group] += product(spread(by_block, fact[8], fact[:8]), one_hot(by_lane, fact[9]))

    les_copy.wait()
    les_store.start()
    by_row = indices(BUCKET, BLOCK)
    by_column = indices(LANES, BLOCK)

    for group in range(GROUPS):

        @pl.loop(0, steps_of(starts.at[group]))
        def _(step):
            for i in range(TOGETHER):
                block = step * TOGETHER + i
                *parts, row, column = (
                    order[group, pl.ds(part * SORTED + block, 1), :] for part in range(8)
                )
                here = folded(by_column, column, parts, one_hot(by_row, row))
                sums[bucket_of(block, starts.at[group])] += here

    stepped_copy.wait()
    for part in range(3):
        for bucket in range(BUCKETS):
            for half in range(BUCKET // LANES):
                cells = sums[
                    bucket,
                    part * LANES : (part + 1) * LANES,
                    half * LANES : (half + 1) * LANES,
                ].T
                for tile in range(LANES // TILE):
                    number = (bucket * BUCKET + half * LANES) // TILE + tile
                    rows = slice(number // TILES * TILE, (number // TILES + 1) * TILE)
                    columns = slice(number % TILES * LANES, (number % TILES + 1) * LANES)
                    out[part, rows, columns] = (
                        stepped_ref[part, rows, columns] + cells[tile * TILE : (tile + 1) * TILE]
                    )
    les_store.wait()


def add(arrived, les_final, stepped):
    return pl.pallas_call(
        add_kernel,
        out_shape=(jax.ShapeDtypeStruct((3, ROWS, COLS), F32),) * 2,
        in_specs=[VMEM, HBM, HBM],
        out_specs=(HBM, VMEM),
        scratch_shapes=[
            pltpu.VMEM((3, ROWS, COLS), F32),
            pltpu.VMEM((3, ROWS, COLS), F32),
            pltpu.VMEM((10, DEVICES, RANKS), F32),
            pltpu.VMEM((GROUPS, 8 * SORTED, BLOCK), F32),
            pltpu.VMEM((BUCKETS, 3 * LANES, BUCKET), F32),
            pltpu.SMEM((GROUPS, BUCKETS + 1), I32),
            pltpu.SemaphoreType.DMA((3,)),
        ],
        compiler_params=params(),
        name="add",
    )(arrived, les_final, stepped)


def local(
    les_state,
    les_density,
    far_state,
    far_density,
    face_cell,
    face_area,
    face_owner,
    face_counts,
    face_target,
):
    cell, area, owner, target = (
        array.reshape(FACE_ROWS, LANES) for array in (face_cell, face_area, face_owner, face_target)
    )
    les_final, stepped, arrived = fields(
        les_state[0],
        les_density[0],
        far_state[0],
        far_density[0],
        face_counts,
        owner,
        cell,
        area,
        target,
    )
    les_final, far_final = add(arrived.reshape(4 * DEVICES, LANES), les_final, stepped)
    return les_final[None], far_final[None]


def solution(mesh):
    field = P("sec", None, "dom", None)
    density = P("sec", "dom", None)
    faces = P(("sec", "dom"))
    return jax.shard_map(
        local,
        mesh=mesh,
        in_specs=(field, density, field, density) + (faces,) * 5,
        out_specs=(field, field),
        check_vma=False,
    )
```
